128 devices in a mesh: req: 8 (over z, core), pos: 16 (over y, x).
Axes of the slice: x: 4, y: 4, z: 4, core: 2. Of those that a mesh axis runs over, the one named last changes fastest.
Arguments:
- res_latent: bfloat16 [48, 16, 1024, 576], P('req', 'pos'), may hold values from -8 to 8
- res_index: bfloat16 [48, 16, 1024, 128], P('req', 'pos'), may hold values from -6 to 6
- res_len: int32 [48], P('req'), may hold values from 8193 to 16384
- arrive_latent: bfloat16 [32, 16384, 576], P('req', 'pos'), may hold values from -8 to 8
- arrive_index: bfloat16 [32, 16384, 128], P('req', 'pos'), may hold values from -6 to 6
- arrive_len: int32 [32], replicated, may hold values from 8193 to 16384
- destination: int32 [32], replicated, may hold values from 0 to 7, as said below
- q_nope: bfloat16 [4, 80, 128, 128], P(None, 'req', 'pos'), may hold values from -6 to 6
- q_rope: bfloat16 [4, 80, 128, 64], P(None, 'req', 'pos'), may hold values from -18 to 18
- w_uk: bfloat16 [128, 128, 512], P('pos'), may hold values from -0.5 to 0.5
- w_uv: bfloat16 [128, 512, 128], P('pos'), may hold values from -3 to 3
- idx_query: bfloat16 [4, 80, 64, 128], P(None, 'req', 'pos'), may hold values from -6 to 6
- idx_weight: bfloat16 [4, 80, 64], P(None, 'req', 'pos'), may hold values from -0.75 to 0.75
- selected: int32 [4, 80, 32], P(None, 'req'), may hold values from 0 to 127, as said below
Outputs:
- arrived_latent: bfloat16 [32, 16, 1024, 576], P('req', 'pos')
- arrived_index: bfloat16 [32, 16, 1024, 128], P('req', 'pos')
- index_scores: float32 [4, 80, 16, 1024], P(None, 'req', 'pos')
- head_out: bfloat16 [4, 80, 128, 128], P(None, 'req', 'pos')
The draws below stay inside these ranges and needn't reach their ends.
Inputs may be any that keep to these rules, and one draw needn't show every extreme that they name: `destination`: for each k < 4, the finished prefills s * 4 + k over all s go to different groups, and the 4 prefills of one group s go to different groups. `selected`: each row names 32 different pages. At most 8 pages of a row are equal modulo 16, and every row has exactly 8 pages equal modulo 16.
All inputs are finite; a program needn't handle non-finite values.
Results may differ from the reference program's by a relative error of at most 0.025.
Values may be sent and summed in bfloat16 or wider, within the bound.
A program may use at most 192 MiB of HBM per device.

```python
import jax
import jax.numpy as jnp
from jax import lax

KV = 512
ROPE = 64
NOPE = 128
VDIM = 128
HEADS = 128
IHEADS = 64
IDIM = 128
PAGE = 64
NSEL = 32
STEPS = 4
CTX_DEV = 1024
RES = 6
NEW = 4
BATCH = 10
CTX = 16384
PG_LOC = 16
SEL_MOST = 8
N_REQ = 8
N_POS = 16


def latent_values(key, leading):
    first = jax.random.fold_in(key, 0)
    values = jnp.clip(jax.random.normal(first, leading + (KV + ROPE,), jnp.float32), -6.0, 6.0)
    rope_part = values[..., KV:]
    return jnp.concatenate([values[..., :KV], rope_part], axis=-1).astype(jnp.bfloat16)


def draw_res_latent(key, part):
    key = jax.random.fold_in(key, 11)
    return latent_values(key, (N_REQ * RES, N_POS, CTX_DEV))


def draw_arrive_latent(key, part):
    key = jax.random.fold_in(key, 12)
    return latent_values(key, (N_REQ * NEW, CTX))


def draw_q_rope(key, part):
    key = jax.random.fold_in(key, 13)
    first = jax.random.fold_in(key, 0)
    values = jnp.clip(jax.random.normal(first, (STEPS, N_REQ * BATCH, HEADS, ROPE), jnp.float32), -6.0, 6.0)
    return values.astype(jnp.bfloat16)


def draw_destination(key, part):
    key = jax.random.fold_in(key, 17)
    first, second = jax.random.split(key)
    ordering = jax.random.permutation(first, N_REQ)
    offsets = jax.random.permutation(second, N_REQ)[:NEW]
    sources = jnp.arange(N_REQ, dtype=jnp.int32)[:, None]
    targets = ordering[(sources + offsets[None, :]) % N_REQ]
    return targets.reshape(N_REQ * NEW).astype(jnp.int32)


def draw_selected(key, part):
    key = jax.random.fold_in(key, 19)
    first, second = jax.random.split(key)
    pair_count = STEPS * N_REQ * BATCH
    shift = jax.random.randint(first, (), 0, N_POS)

    def one_pair(number):
        pair_key = jax.random.fold_in(second, number)
        key_other, key_order = jax.random.split(pair_key)
        busiest = (shift + number) % N_POS
        others = jax.random.permutation(key_other, (N_POS - 1) * SEL_MOST)[:NSEL - SEL_MOST]
        owners = (busiest + 1 + others // SEL_MOST) % N_POS
        pages_other = others % SEL_MOST * N_POS + owners
        pages_busy = jnp.arange(SEL_MOST, dtype=jnp.int32) * N_POS + busiest
        every_page = jnp.concatenate([pages_busy, pages_other.astype(jnp.int32)])
        ordering = jax.random.permutation(key_order, NSEL)
        return every_page[ordering]
    chosen = jax.vmap(one_pair)(jnp.arange(pair_count, dtype=jnp.int32))
    return chosen.reshape(STEPS, N_REQ * BATCH, NSEL).astype(jnp.int32)


def with_ends(array, own_key, smallest, top_value):
    longest = array.shape.index(max(array.shape))
    spots = []
    for shift in (0, 1):
        where = [jax.random.randint(jax.random.fold_in(own_key, axis), (), 0, length) for axis, length in enumerate(array.shape)]
        where[longest] = (where[longest] + shift) % array.shape[longest]
        spots.append(tuple(where))
    return array.at[spots[0]].set(smallest).at[spots[1]].set(top_value)


def shard_levels(key, shape, cuts, smallest, high):
    gain = 1.0
    for axis_at, parts in cuts:
        heights = jax.random.uniform(jax.random.fold_in(jax.random.fold_in(key, 6), axis_at), (parts,), jnp.float32, smallest / len(cuts), high / len(cuts))
        gain = gain * jnp.repeat(jnp.exp(heights), shape[axis_at] // parts).reshape((-1,) + (1,) * (len(shape) - 1 - axis_at))
    return gain


def normal_values(key, dims, width, bound, shards=(), kind=jnp.bfloat16):
    array = jax.random.normal(key, dims, jnp.float32) * width
    if len(shards) > 0:
        array = shard_levels(key, dims, shards, -0.22, 0.18) * array
    return jnp.clip(array, min=-bound, max=bound).astype(kind)


def setup_inputs(seed: int = 0) -> dict:
    seeds = jax.random.split(jax.random.key(seed), 15)
    return {
        "res_latent": draw_res_latent(jax.random.fold_in(seeds[14], 71), 0),
        "res_index": normal_values(seeds[1], (N_REQ * RES, N_POS, CTX_DEV, IDIM), 1.0, 6.0, ((0, 8), (1, 16))),
        "res_len": with_ends(jax.random.randint(seeds[2], (N_REQ * RES,), CTX // 2 + 1, CTX + 1), jax.random.fold_in(seeds[2], 1), CTX // 2 + 1, CTX).astype(jnp.int32),
        "arrive_latent": draw_arrive_latent(jax.random.fold_in(seeds[14], 71), 0),
        "arrive_index": normal_values(seeds[4], (N_REQ * NEW, CTX, IDIM), 1.0, 6.0, ((0, 8), (1, 16))),
        "arrive_len": with_ends(jax.random.randint(seeds[5], (N_REQ * NEW,), CTX // 2 + 1, CTX + 1), jax.random.fold_in(seeds[5], 1), CTX // 2 + 1, CTX).astype(jnp.int32),
        "destination": draw_destination(jax.random.fold_in(seeds[14], 71), 0),
        "q_nope": normal_values(seeds[7], (STEPS, N_REQ * BATCH, HEADS, NOPE), 1.0, 6.0, ((1, 8), (2, 16))),
        "q_rope": draw_q_rope(jax.random.fold_in(seeds[14], 71), 0),
        "w_uk": normal_values(seeds[9], (HEADS, NOPE, KV), NOPE ** -0.5, 0.5, ((0, 16),)),
        "w_uv": normal_values(seeds[10], (HEADS, KV, VDIM), 0.5, 3.0, ((0, 16),)),
        "idx_query": normal_values(seeds[11], (STEPS, N_REQ * BATCH, IHEADS, IDIM), 1.0, 6.0, ((1, 8), (2, 16))),
        "idx_weight": normal_values(seeds[12], (STEPS, N_REQ * BATCH, IHEADS), 0.125, 0.75, ((1, 8), (2, 16))),
        "selected": draw_selected(jax.random.fold_in(seeds[14], 71), 0),
    }


def decode_layout(prefill_rows, lengths):
    row_count = prefill_rows.shape[0]
    lane_width = prefill_rows.shape[-1]
    positions = jnp.arange(CTX, dtype=jnp.int32)
    within = positions[None, :] < lengths[:, None]
    masked = jnp.where(within[:, :, None], prefill_rows, jnp.zeros((), prefill_rows.dtype))
    paged = masked.reshape(row_count, PG_LOC, N_POS, PAGE, lane_width).transpose(0, 2, 1, 3, 4)
    return paged.reshape(row_count, N_POS, CTX_DEV, lane_width)


def arrival_sources(destination):
    routing = destination.reshape(N_REQ, NEW)
    group_ids = jnp.arange(N_REQ, dtype=jnp.int32)
    matches = (routing[None, :, :] == group_ids[:, None, None]).astype(jnp.int32)
    sources = jnp.sum(matches * group_ids[None, :, None], axis=1)
    row_ids = sources * NEW + jnp.arange(NEW, dtype=jnp.int32)[None, :]
    return row_ids.reshape(N_REQ * NEW).astype(jnp.int32)


def logical_positions():
    owners = jnp.arange(N_POS, dtype=jnp.int32)[:, None]
    offsets = jnp.arange(CTX_DEV, dtype=jnp.int32)[None, :]
    return ((offsets // PAGE) * N_POS + owners) * PAGE + offsets % PAGE


def index_slot(operands):
    queries, weights, index_keys, length = operands
    logits = jnp.einsum("shd,old->shol", queries.astype(jnp.float32), index_keys.astype(jnp.float32),
                        precision=lax.Precision.HIGHEST)
    scored = jnp.einsum("shol,sh->sol", jnp.maximum(logits, 0.0), weights.astype(jnp.float32),
                        precision=lax.Precision.HIGHEST) * IDIM ** -0.5
    return jnp.where(logical_positions()[None] < length, scored, jnp.zeros((), scored.dtype))


def attend_slot(operands):
    queries, latents, chosen = operands
    pages = latents.reshape(N_POS, PG_LOC, PAGE, KV + ROPE)
    picked = pages[chosen % N_POS, chosen // N_POS].reshape(STEPS, NSEL * PAGE, KV + ROPE).astype(jnp.float32)
    scores = jnp.einsum("shc,stc->sht", queries.astype(jnp.float32), picked,
                        precision=lax.Precision.HIGHEST) * (NOPE + ROPE) ** -0.5
    largest = jnp.max(scores, axis=-1, keepdims=True)
    exponent = jnp.exp(scores - largest)
    denominator = jnp.sum(exponent, axis=-1)
    rounded = lax.optimization_barrier(exponent.astype(jnp.bfloat16)).astype(jnp.float32)
    numerator = jnp.einsum("sht,stc->shc", rounded, picked[..., :KV], precision=lax.Precision.HIGHEST)
    return (numerator / denominator[..., None]).astype(jnp.bfloat16)


def split_slots(stacked):
    steps_dim = stacked.shape[0]
    trailing = stacked.shape[2:]
    grouped = stacked.reshape((steps_dim, N_REQ, BATCH) + trailing)
    resident = grouped[:, :, :RES].reshape((steps_dim, N_REQ * RES) + trailing)
    arrived = grouped[:, :, RES:].reshape((steps_dim, N_REQ * NEW) + trailing)
    return jnp.moveaxis(resident, 1, 0), jnp.moveaxis(arrived, 1, 0)


def join_slots(resident, arrived):
    trailing = resident.shape[1:]
    combined = jnp.concatenate([resident.reshape((N_REQ, RES) + trailing),
                                arrived.reshape((N_REQ, NEW) + trailing)], axis=1)
    combined = combined.reshape((N_REQ * BATCH,) + trailing)
    return jnp.moveaxis(combined, 0, 1)


def reference(res_latent, res_index, res_len, arrive_latent, arrive_index, arrive_len, destination,
              q_nope, q_rope, w_uk, w_uv, idx_query, idx_weight, selected):
    row_ids = arrival_sources(destination)
    arrived_latent = decode_layout(arrive_latent, arrive_len)[row_ids]
    arrived_index = decode_layout(arrive_index, arrive_len)[row_ids]
    new_lengths = arrive_len[row_ids]
    query_res, query_new = split_slots(idx_query)
    weight_res, weight_new = split_slots(idx_weight)
    index_res = lax.map(index_slot, (query_res, weight_res, res_index, res_len))
    index_new = lax.map(index_slot, (query_new, weight_new, arrived_index, new_lengths))
    index_scores = join_slots(index_res, index_new)
    absorbed = jnp.einsum("sbhn,hnc->sbhc", q_nope.astype(jnp.float32), w_uk.astype(jnp.float32),
                          precision=lax.Precision.HIGHEST).astype(jnp.bfloat16)
    queries = jnp.concatenate([absorbed, q_rope], axis=-1)
    attend_res, attend_new = split_slots(queries)
    chosen_res, chosen_new = split_slots(selected)
    latent_res = lax.map(attend_slot, (attend_res, res_latent, chosen_res))
    latent_new = lax.map(attend_slot, (attend_new, arrived_latent, chosen_new))
    latent = lax.optimization_barrier(join_slots(latent_res, latent_new))
    head_out = jnp.einsum("sbhc,hcd->sbhd", latent.astype(jnp.float32), w_uv.astype(jnp.float32),
                          precision=lax.Precision.HIGHEST).astype(jnp.bfloat16)
    return arrived_latent, arrived_index, index_scores, head_out
```

```python
import jax
import jax.numpy as jnp
from jax import lax
from jax.experimental import pallas as pl
from jax.experimental.pallas import tpu as pltpu
from jax.sharding import PartitionSpec as P

KV, ROPE, NOPE, IDIM, PAGE = 512, 64, 128, 128, 64
LAT = KV + ROPE
STEPS, RES, NEW, BATCH, HEADS_DEV, IHEADS_DEV = 4, 6, 4, 10, 8, 4
CTX_DEV, PG_LOC, N_REQ, SIDE = 1024, 16, 8, 4
QW = 640
HALF = PAGE // 2
QROWS = STEPS * HEADS_DEV
IROWS = STEPS * IHEADS_DEV
BF, F32 = jnp.bfloat16, jnp.float32
MESH = pl.DeviceIdType.MESH
SCALE = (NOPE + ROPE) ** (-0.5)

CHUNKS = (
    [("idx", 0, 0), ("idx", 0, 1), ("rope", 0, 0)]
    + [("lat", j, h) for j in range(KV // 128) for h in range(2)]
)
N_CH = len(CHUNKS)
RING = 3
GROUPS = ((0, 6), (6, 2), (8, 2))


def kernel(
    chosen, sources, limits, lat, idx, rope, qown, iqown, reslat, residx, bias,
    out_lat, out_idx, out_is, out_latent, a_buf,
    b_bufs, zsend, zrecvs, q_all, iq_all, kbuf, ki_res, kfin, kifin, numer, stats,
    ra, rsa, nb_buf, stb, rb, rsb,
    sa_s, sa_r, sb_s, sb_r, sz_s, sz_r, own_a, own_b, load_sem, out_sem, kb_sem,
    ag_s, ag_r, rs_s, rs_r,
):
    req = lax.axis_index("req")
    pos = lax.axis_index("pos")
    y, x = pos // SIDE, pos % SIDE

    def along(axis, delta):
        if axis == 0:
            return (req, y * SIDE + (x + delta) % SIDE)
        return (req, ((y + delta) % SIDE) * SIDE + x)

    def mine(axis):
        return x if axis == 0 else y

    def remote(src, dst, send, recv, target):
        return pltpu.make_async_remote_copy(
            src_ref=src, dst_ref=dst, send_sem=send, recv_sem=recv,
            device_id=target, device_id_type=MESH,
        )

    barrier = pltpu.get_barrier_semaphore()
    for delta in range(1, N_REQ):
        pl.semaphore_signal(barrier, 1, device_id=((req + delta) % N_REQ, pos), device_id_type=MESH)
    for axis in range(2):
        for delta in range(1, SIDE):
            pl.semaphore_signal(barrier, 1, device_id=along(axis, delta), device_id_type=MESH)
    pl.semaphore_wait(barrier, N_REQ - 1 + 2 * (SIDE - 1))

    def first_axis(i):
        return i % 2

    def chunk_source(i, coord):
        kind, plane, half = CHUNKS[i]
        if kind == "rope":
            ref, rows, lanes = rope, pl.ds(0, HALF), pl.ds(0, 128)
        elif kind == "idx":
            ref, rows, lanes = idx, pl.ds(half * HALF, HALF), pl.ds(0, 128)
        else:
            ref, rows, lanes = lat, pl.ds(half * HALF, HALF), pl.ds(plane * 128, 128)
        if first_axis(i) == 0:
            return ref.at[:, :, coord, rows, lanes]
        return ref.at[:, coord, :, rows, lanes]

    def copies_a(i):
        axis = first_axis(i)
        return [
            remote(
                chunk_source(i, (mine(axis) + delta) % SIDE), a_buf.at[i, mine(axis)],
                sa_s.at[i, delta - 1], sa_r.at[i, delta - 1], along(axis, delta),
            )
            for delta in range(1, SIDE)
        ]

    def own_copy_a(i):
        coord = mine(first_axis(i))
        return pltpu.make_async_copy(chunk_source(i, coord), a_buf.at[i, coord], own_a.at[i])

    def copies_b(i):
        axis = 1 - first_axis(i)
        return [
            remote(
                a_buf.at[i, :, :, (mine(axis) + delta) % SIDE], b_bufs[i].at[mine(axis)],
                sb_s.at[i, delta - 1], sb_r.at[i, delta - 1], along(axis, delta),
            )
            for delta in range(1, SIDE)
        ]

    def own_copy_b(i):
        coord = mine(1 - first_axis(i))
        return pltpu.make_async_copy(a_buf.at[i, :, :, coord], b_bufs[i].at[coord], own_b.at[i])

    def copy_z(i, delta):
        return remote(
            zsend.at[i % RING, delta - 1], zrecvs[i].at[req],
            sz_s.at[i, delta - 1], sz_r.at[i, delta - 1], ((req + delta) % N_REQ, pos),
        )

    def start_a(i):
        for copy in copies_a(i):
            copy.start()

    def a_to_b(i):
        own_copy_a(i).wait()
        for copy in copies_a(i):
            copy.wait_recv()
        for copy in copies_b(i):
            copy.start()
        own_copy_b(i).start()

    def b_to_z(i):
        own_copy_b(i).wait()
        for copy in copies_b(i):
            copy.wait_recv()
        if i >= RING:
            for delta in range(1, N_REQ):
                copy_z(i - RING, delta).wait_send()

        def stage(delta, carry):
            k = chosen[(req + delta) % N_REQ]
            zsend[i % RING, delta - 1] = b_bufs[i][:, :, k]
            copy_z(i, delta).start()
            return carry

        lax.fori_loop(1, N_REQ, stage, 0)
        zrecvs[i][req] = b_bufs[i][:, :, chosen[req]]

    def wait_z(i):
        for delta in range(1, N_REQ):
            copy_z(i, delta).wait_recv()

    def out_copies(kind):
        if kind == "idx":
            return pltpu.make_async_copy(kifin, out_idx, out_sem.at[0])
        return pltpu.make_async_copy(kfin, out_lat, out_sem.at[1])

    def finalize(i):
        kind, plane, half = CHUNKS[i]
        by_x = first_axis(i) == 0

        def page(n, carry):
            outer, inner = n // SIDE, n % SIDE
            l = outer * SIDE + inner if by_x else inner * SIDE + outer
            base = (l * (SIDE * SIDE) + pos) * PAGE
            row = lax.broadcasted_iota(jnp.int32, (HALF, 128), 0)
            for k in range(NEW):
                tile = zrecvs[i][sources[k], outer, inner]
                if kind == "rope":
                    for part in range(2):
                        keep = row[:, :ROPE] + (base + part * HALF) < limits[k]
                        value = tile[:, part * ROPE : (part + 1) * ROPE].astype(F32)
                        kfin[k, l, part * HALF : (part + 1) * HALF, KV:LAT] = jnp.where(
                            keep, value, 0.0
                        ).astype(BF)
                else:
                    keep = row + (base + half * HALF) < limits[k]
                    value = jnp.where(keep, tile.astype(F32), 0.0).astype(BF)
                    rows = slice(half * HALF, (half + 1) * HALF)
                    if kind == "idx":
                        kifin[k, l, rows, :] = value
                    else:
                        kfin[k, l, rows, plane * 128 : (plane + 1) * 128] = value
            return carry

        lax.fori_loop(0, SIDE * SIDE, page, 0)

    spans = (pl.ds(0, BATCH // 2), pl.ds(BATCH // 2, BATCH // 2))

    def gather_copies(phase):
        copies = []
        for way in range(2):
            axis = way if phase == 0 else 1 - way
            for which, (own, every) in enumerate(((qown, q_all), (iqown, iq_all))):
                for delta in range(1, SIDE):
                    if phase == 0:
                        src, dst = own.at[spans[way]], every.at[y, x, spans[way]]
                    elif way == 0:
                        src = dst = every.at[y, :, spans[way]]
                    else:
                        src = dst = every.at[:, x, spans[way]]
                    at = (phase, way, which, delta - 1)
                    copies.append(remote(src, dst, ag_s.at[at], ag_r.at[at], along(axis, delta)))
        return copies

    own_q = pltpu.make_async_copy(qown, q_all.at[y, x], load_sem.at[0])
    own_iq = pltpu.make_async_copy(iqown, iq_all.at[y, x], load_sem.at[1])
    load_ki = pltpu.make_async_copy(residx, ki_res, load_sem.at[2])

    def load_k(b):
        return pltpu.make_async_copy(reslat.at[b], kbuf.at[b % 2], kb_sem.at[b])

    def attend(b, g, keys, flipped):
        def part(n, carry):
            q = q_all[pl.ds(2 * n, 2), :, b, :, 0:LAT].reshape(2 * SIDE * QROWS, LAT)
            k = keys()
            key_dim = 0 if flipped else 1
            s = lax.dot_general(q, k, (((1,), (key_dim,)), ((), ())), preferred_element_type=F32)
            s = (s * SCALE).reshape(2 * SIDE, QROWS, CTX_DEV) + bias[b][None]
            s = s.reshape(2 * SIDE * QROWS, CTX_DEV)
            top = jnp.maximum(jnp.max(s, axis=1, keepdims=True), -1e29)
            e = jnp.exp(s - top)
            total = jnp.sum(e, axis=1, keepdims=True)
            v = k[:KV] if flipped else k[:, :KV]
            o = lax.dot_general(
                e.astype(BF), v, (((1,), (1 - key_dim,)), ((), ())), preferred_element_type=F32
            )
            numer[pl.ds(2 * n, 2), :, b] = o.astype(BF).reshape(2, SIDE, QROWS, KV)
            lane = lax.broadcasted_iota(jnp.int32, (2 * SIDE * QROWS, 128), 1)
            shape = (2, SIDE, QROWS, 128)
            here = (lane == b - GROUPS[g][0])
            old_top = stats[g, 0, pl.ds(2 * n, 2)].reshape(2 * SIDE * QROWS, 128)
            old_sum = stats[g, 1, pl.ds(2 * n, 2)].reshape(2 * SIDE * QROWS, 128)
            stats[g, 0, pl.ds(2 * n, 2)] = jnp.where(here, top, old_top).reshape(shape)
            stats[g, 1, pl.ds(2 * n, 2)] = jnp.where(here, total, old_sum).reshape(shape)
            return carry

        lax.fori_loop(0, 2, part, 0)

    def index_scores(b, keys):
        def part(n, carry):
            block = iq_all[:, :, b].reshape(SIDE * SIDE * IROWS, 2 * IDIM)
            k = keys(n)
            logits = lax.dot_general(
                block[:, :IDIM], k, (((1,), (1,)), ((), ())), preferred_element_type=F32
            )
            weight = block[:, IDIM : IDIM + 1].astype(F32)
            value = jnp.maximum(logits, 0.0) * weight
            cols = pl.ds(pl.multiple_of(n * 256, 256), 256)
            out_is[b, :, cols] = jnp.sum(value.reshape(SIDE * SIDE, IROWS, 256), axis=0)
            return carry

        lax.fori_loop(0, CTX_DEV // 256, part, 0)

    def attend_res(b):
        load_k(b).wait()
        attend(b, 0, lambda: kbuf[b % 2], True)
        if b + 2 < RES:
            load_k(b + 2).start()

    def attend_new(k, g):
        attend(RES + k, g, lambda: kfin[k].reshape(CTX_DEV, LAT), False)

    def index_res(b):
        index_scores(b, lambda n: ki_res[b, pl.ds(pl.multiple_of(n * 256, 256), 256)])

    def index_new(k):
        index_scores(RES + k, lambda n: kifin[k, pl.ds(n * 4, 4)].reshape(256, IDIM))

    def lanes(way):
        return pl.ds(way * 256, 256)

    def reduce_copies(g, phase, way):
        b0, count = GROUPS[g]
        span = pl.ds(b0, count)
        axis = way if phase == 0 else 1 - way
        copies = []
        for delta in range(1, SIDE):
            other = (mine(axis) + delta) % SIDE
            if phase == 0:
                if way == 0:
                    src, src_st = numer.at[:, other, span, :, lanes(way)], stats.at[g, :, :, other]
                else:
                    src, src_st = numer.at[other, :, span, :, lanes(way)], stats.at[g, :, other]
                dst, dst_st = ra.at[way, delta - 1, :, span], rsa.at[g, way, delta - 1]
            else:
                src, src_st = nb_buf.at[way, other, span], stb.at[g, way, other]
                dst, dst_st = rb.at[way, delta - 1, span], rsb.at[g, way, delta - 1]
            target = along(axis, delta)
            for which, (s, d) in enumerate(((src, dst), (src_st, dst_st))):
                at = (g, phase, way, which, delta - 1)
                copies.append(remote(s, d, rs_s.at[at], rs_r.at[at], target))
        return copies

    def start_reduce(g, phase, way):
        for copy in reduce_copies(g, phase, way):
            copy.start()

    def merged(tops, sums):
        top = tops[0]
        for value in tops[1:]:
            top = jnp.maximum(top, value)
        factors = [jnp.exp(value - top) for value in tops]
        total = factors[0] * sums[0]
        for factor, value in zip(factors[1:], sums[1:]):
            total = total + factor * value
        return top, factors, total

    def combine_a(g, way):
        b0, count = GROUPS[g]
        for copy in reduce_copies(g, 0, way):
            copy.wait_recv()

        def block(j, carry):
            if way == 0:
                own = (stats[g, 0, j, x], stats[g, 1, j, x])
            else:
                own = (stats[g, 0, y, j], stats[g, 1, y, j])
            tops = [own[0]] + [rsa[g, way, d, 0, j] for d in range(SIDE - 1)]
            sums = [own[1]] + [rsa[g, way, d, 1, j] for d in range(SIDE - 1)]
            top, factors, total = merged(tops, sums)
            stb[g, way, j, 0] = top
            stb[g, way, j, 1] = total
            for n in range(count):
                if way == 0:
                    first = numer[j, x, b0 + n, :, 0:256]
                else:
                    first = numer[y, j, b0 + n, :, 256:512]
                acc = first.astype(F32) * factors[0][:, n : n + 1]
                for d in range(SIDE - 1):
                    acc = acc + ra[way, d, j, b0 + n].astype(F32) * factors[d + 1][:, n : n + 1]
                nb_buf[way, j, b0 + n] = acc.astype(BF)
            return carry

        lax.fori_loop(0, SIDE, block, 0)
        start_reduce(g, 1, way)

    def combine_b(g, way):
        b0, count = GROUPS[g]
        for copy in reduce_copies(g, 1, way):
            copy.wait_recv()
        here = mine(1 - way)
        tops = [stb[g, way, here, 0]] + [rsb[g, way, d, 0] for d in range(SIDE - 1)]
        sums = [stb[g, way, here, 1]] + [rsb[g, way, d, 1] for d in range(SIDE - 1)]
        top, factors, total = merged(tops, sums)
        for n in range(count):
            acc = nb_buf[way, here, b0 + n].astype(F32) * factors[0][:, n : n + 1]
            for d in range(SIDE - 1):
                acc = acc + rb[way, d, b0 + n].astype(F32) * factors[d + 1][:, n : n + 1]
            out_latent[b0 + n, :, way * 256 : (way + 1) * 256] = (
                acc / total[:, n : n + 1]
            ).astype(BF)

    own_q.start()
    own_iq.start()
    for i in range(2):
        own_copy_a(i).start()
        start_a(i)
    for copy in gather_copies(0):
        copy.start()
    for i in range(2, 5):
        own_copy_a(i).start()
        start_a(i)
    load_ki.start()
    load_k(0).start()
    load_k(1).start()
    stats[...] = jnp.zeros_like(stats)
    a_to_b(0)
    a_to_b(1)
    b_to_z(0)
    own_q.wait()
    own_iq.wait()
    for copy in gather_copies(0):
        copy.wait_recv()
    for copy in gather_copies(1):
        copy.start()
    b_to_z(1)
    a_to_b(2)

    for i in range(N_CH):
        wait_z(i)
        if i + 2 < N_CH:
            b_to_z(i + 2)
        if i + 3 < N_CH:
            a_to_b(i + 3)
        if i + 5 < N_CH:
            own_copy_a(i + 5).start()
            start_a(i + 5)
        finalize(i)
        if i == 1:
            out_copies("idx").start()
        if i == 3:
            for copy in gather_copies(1):
                copy.wait_recv()
            attend_res(0)
        elif i == 4:
            attend_res(1)
            attend_res(2)
            attend_res(3)
        elif i == 5:
            attend_res(4)
            attend_res(5)
            for way in range(2):
                start_reduce(0, 0, way)
            load_ki.wait()
            index_res(0)
            index_res(1)
        elif i == 6:
            for b in range(2, RES):
                index_res(b)
        elif i == 7:
            for way in range(2):
                combine_a(0, way)
            index_new(0)
            index_new(1)
        elif i == 8:
            index_new(2)
            index_new(3)
        elif i == 9:
            for way in range(2):
                combine_b(0, way)
    out_copies("lat").start()
    attend_new(0, 1)
    attend_new(1, 1)
    for way in range(2):
        start_reduce(1, 0, way)
    attend_new(2, 2)
    attend_new(3, 2)
    for way in range(2):
        start_reduce(2, 0, way)
    for g in (1, 2):
        for way in range(2):
            combine_a(g, way)
    for g in (1, 2):
        for way in range(2):
            combine_b(g, way)

    for i in range(N_CH):
        for copy in copies_a(i) + copies_b(i):
            copy.wait_send()
    for i in range(N_CH - RING, N_CH):
        for delta in range(1, N_REQ):
            copy_z(i, delta).wait_send()
    for phase in range(2):
        for copy in gather_copies(phase):
            copy.wait_send()
        for g in range(len(GROUPS)):
            for way in range(2):
                for copy in reduce_copies(g, phase, way):
                    copy.wait_send()
    out_copies("idx").wait()
    out_copies("lat").wait()


def run_kernel(*operands):
    smem = pl.BlockSpec(memory_space=pltpu.SMEM)
    vmem = pl.BlockSpec(memory_space=pltpu.VMEM)
    hbm = pl.BlockSpec(memory_space=pl.ANY)
    dma = pltpu.SemaphoreType.DMA
    n_groups = len(GROUPS)
    tile = (SIDE, SIDE, HALF, 128)
    return pl.pallas_call(
        kernel,
        out_shape=(
            jax.ShapeDtypeStruct((NEW, PG_LOC, PAGE, LAT), BF),
            jax.ShapeDtypeStruct((NEW, PG_LOC, PAGE, IDIM), BF),
            jax.ShapeDtypeStruct((BATCH, IROWS, CTX_DEV), F32),
            jax.ShapeDtypeStruct((BATCH, QROWS, KV), BF),
            jax.ShapeDtypeStruct((N_CH, SIDE, NEW, SIDE, HALF, 128), BF),
        ),
        in_specs=[smem] * 3 + [hbm] * 7 + [vmem],
        out_specs=(hbm, hbm, vmem, vmem, hbm),
        scratch_shapes=[
            (pltpu.VMEM((SIDE, SIDE, NEW, HALF, 128), BF),) * N_CH,
            pltpu.VMEM((RING, N_REQ - 1) + tile, BF),
            (pltpu.VMEM((N_REQ,) + tile, BF),) * N_CH,
            pltpu.VMEM((SIDE, SIDE, BATCH, QROWS, QW), BF),
            pltpu.VMEM((SIDE, SIDE, BATCH, IROWS, 2 * IDIM), BF),
            pltpu.VMEM((2, LAT, CTX_DEV), BF),
            pltpu.VMEM((RES, CTX_DEV, IDIM), BF),
            pltpu.VMEM((NEW, PG_LOC, PAGE, LAT), BF),
            pltpu.VMEM((NEW, PG_LOC, PAGE, IDIM), BF),
            pltpu.VMEM((SIDE, SIDE, BATCH, QROWS, KV), BF),
            pltpu.VMEM((n_groups, 2, SIDE, SIDE, QROWS, 128), F32),
            pltpu.VMEM((2, SIDE - 1, SIDE, BATCH, QROWS, 256), BF),
            pltpu.VMEM((n_groups, 2, SIDE - 1, 2, SIDE, QROWS, 128), F32),
            pltpu.VMEM((2, SIDE, BATCH, QROWS, 256), BF),
            pltpu.VMEM((n_groups, 2, SIDE, 2, QROWS, 128), F32),
            pltpu.VMEM((2, SIDE - 1, BATCH, QROWS, 256), BF),
            pltpu.VMEM((n_groups, 2, SIDE - 1, 2, QROWS, 128), F32),
            dma((N_CH, 3)), dma((N_CH, 3)), dma((N_CH, 3)), dma((N_CH, 3)),
            dma((N_CH, N_REQ - 1)), dma((N_CH, N_REQ - 1)),
            dma((N_CH,)), dma((N_CH,)), dma((3,)), dma((2,)), dma((RES,)),
            dma((2, 2, 2, 3)), dma((2, 2, 2, 3)),
            dma((n_groups, 2, 2, 2, 3)), dma((n_groups, 2, 2, 2, 3)),
        ],
        compiler_params=pltpu.CompilerParams(
            collective_id=0, has_side_effects=True, vmem_limit_bytes=63 * 2**20
        ),
        name="decode_step",
    )(*operands)


def body(
    res_latent, res_index, res_len, arrive_latent, arrive_index, arrive_len, destination,
    q_nope, q_rope, w_uk, w_uv, idx_query, idx_weight, selected,
):
    req_index = lax.axis_index("req")
    pos_index = lax.axis_index("pos")
    routing = destination.reshape(N_REQ, NEW)
    group_ids = jnp.arange(N_REQ, dtype=jnp.int32)
    arrival_ids = jnp.arange(NEW, dtype=jnp.int32)
    matches = routing[req_index][None, :] == group_ids[:, None]
    chosen = jnp.sum(jnp.where(matches, arrival_ids[None, :], 0), axis=1)
    sources = jnp.sum(jnp.where(routing == req_index, group_ids[:, None], 0), axis=0)
    new_lengths = arrive_len[sources * NEW + arrival_ids]

    paged = arrive_latent.reshape(NEW, SIDE, SIDE, PAGE, LAT)
    rope = jnp.concatenate([paged[..., :HALF, KV:], paged[..., HALF:, KV:]], axis=-1)

    absorbed = jnp.einsum("sbhn,hnc->sbhc", q_nope, w_uk, preferred_element_type=F32).astype(BF)
    pad = jnp.zeros(q_rope.shape[:-1] + (QW - LAT,), BF)
    queries = jnp.concatenate([absorbed, q_rope, pad], axis=-1)
    queries = queries.transpose(1, 0, 2, 3).reshape(BATCH, QROWS, QW)
    spread = jnp.broadcast_to(idx_weight[..., None], idx_query.shape)
    idx_queries = jnp.concatenate([idx_query, spread], axis=-1)
    idx_queries = idx_queries.transpose(1, 0, 2, 3).reshape(BATCH, IROWS, 2 * IDIM)

    here = (selected % (SIDE * SIDE) == pos_index)[..., None]
    slots = jnp.arange(PG_LOC, dtype=jnp.int32)
    live = jnp.any(here & (selected[..., None] // (SIDE * SIDE) == slots), axis=2)
    bias = jnp.where(jnp.repeat(live, PAGE, axis=-1), 0.0, -1e30).astype(F32)
    bias = jnp.broadcast_to(
        bias.transpose(1, 0, 2)[:, :, None, :], (BATCH, STEPS, HEADS_DEV, CTX_DEV)
    ).reshape(BATCH, QROWS, CTX_DEV)

    new_latent, new_index, raw, latent, _ = run_kernel(
        chosen.astype(jnp.int32), sources.astype(jnp.int32), new_lengths,
        paged, arrive_index.reshape(NEW, SIDE, SIDE, PAGE, IDIM), rope,
        queries, idx_queries, res_latent[:, 0].transpose(0, 2, 1), res_index[:, 0], bias,
    )

    scored = jnp.sum(raw.reshape(BATCH, STEPS, IHEADS_DEV, CTX_DEV), axis=2) * IDIM ** (-0.5)
    lengths = jnp.concatenate([res_len, new_lengths])
    offsets = jnp.arange(CTX_DEV, dtype=jnp.int32)
    logical = (offsets // PAGE * (SIDE * SIDE) + pos_index) * PAGE + offsets % PAGE
    index_scores = jnp.where(logical[None, None, :] < lengths[:, None, None], scored, 0.0)
    index_scores = index_scores.transpose(1, 0, 2)[:, :, None, :]

    latent = latent.reshape(BATCH, STEPS, HEADS_DEV, KV)
    head_out = jnp.einsum("bshc,hcd->sbhd", latent, w_uv, preferred_element_type=F32).astype(BF)
    return (
        new_latent.reshape(NEW, 1, CTX_DEV, LAT),
        new_index.reshape(NEW, 1, CTX_DEV, IDIM),
        index_scores,
        head_out,
    )


def solution(mesh):
    placed = (
        P("req", "pos", None, None),
        P("req", "pos", None, None),
        P("req"),
        P("req", "pos", None),
        P("req", "pos", None),
        P(),
        P(),
        P(None, "req", "pos", None),
        P(None, "req", "pos", None),
        P("pos", None, None),
        P("pos", None, None),
        P(None, "req", "pos", None),
        P(None, "req", "pos"),
        P(None, "req", None),
    )
    return jax.shard_map(
        body,
        mesh=mesh,
        in_specs=placed,
        out_specs=(
            P("req", "pos", None, None),
            P("req", "pos", None, None),
            P(None, "req", "pos", None),
            P(None, "req", "pos", None),
        ),
        check_vma=False,
    )
```

```python
import jax
import jax.numpy as jnp
from jax import lax
from jax.experimental import pallas as pl
from jax.experimental.pallas import tpu as pltpu
from jax.sharding import PartitionSpec as P

KV, ROPE, NOPE, IDIM, PAGE = 512, 64, 128, 128, 64
LAT = KV + ROPE
STEPS, RES, NEW, BATCH, HEADS_DEV = 4, 6, 4, 10, 8
CTX_DEV, PG_LOC, N_REQ, SIDE = 1024, 16, 8, 4
QW = 640
HALF = PAGE // 2
QROWS = STEPS * HEADS_DEV
BF, F32 = jnp.bfloat16, jnp.float32
MESH = pl.DeviceIdType.MESH
SCALE = (NOPE + ROPE) ** (-0.5)

CHUNKS = (
    [("idx", 0, 0), ("idx", 0, 1), ("rope", 0, 0)]
    + [("lat", j, h) for j in range(KV // 128) for h in range(2)]
)
N_CH = len(CHUNKS)
RING = 3
GROUPS = ((0, 6), (6, 2), (8, 2))
STAT_ROWS = (16, 8, 8)


def kernel(
    chosen, sources, limits, lat, idx, rope, qown, wown, reslat, residx, bias,
    out_lat, out_idx, out_is, out_latent, a_buf,
    b_bufs, zsend, zrecvs, q_all, w_all, iq_buf, kbuf, ki_res, kfin, kifin, numer, stats,
    ra, rsa, nb_buf, stb, rb, rsb, fbuf,
    sa_s, sa_r, sb_s, sb_r, sz_s, sz_r, own_a, own_b, load_sem, out_sem, kb_sem,
    ag_s, ag_r, aw_s, aw_r, rs_s, rs_r,
):
    req = lax.axis_index("req")
    pos = lax.axis_index("pos")
    y, x = pos // SIDE, pos % SIDE

    def along(axis, delta):
        if axis == 0:
            return (req, y * SIDE + (x + delta) % SIDE)
        return (req, ((y + delta) % SIDE) * SIDE + x)

    def mine(axis):
        return x if axis == 0 else y

    def remote(src, dst, send, recv, target):
        return pltpu.make_async_remote_copy(
            src_ref=src, dst_ref=dst, send_sem=send, recv_sem=recv,
            device_id=target, device_id_type=MESH,
        )

    barrier = pltpu.get_barrier_semaphore()
    for delta in range(1, N_REQ):
        pl.semaphore_signal(barrier, 1, device_id=((req + delta) % N_REQ, pos), device_id_type=MESH)
    for axis in range(2):
        for delta in range(1, SIDE):
            pl.semaphore_signal(barrier, 1, device_id=along(axis, delta), device_id_type=MESH)
    pl.semaphore_wait(barrier, N_REQ - 1 + 2 * (SIDE - 1))

    def first_axis(i):
        return i % 2

    def chunk_source(i, coord):
        kind, plane, half = CHUNKS[i]
        if kind == "rope":
            ref, rows, lanes = rope, pl.ds(0, HALF), pl.ds(0, 128)
        elif kind == "idx":
            ref, rows, lanes = idx, pl.ds(half * HALF, HALF), pl.ds(0, 128)
        else:
            ref, rows, lanes = lat, pl.ds(half * HALF, HALF), pl.ds(plane * 128, 128)
        if first_axis(i) == 0:
            return ref.at[:, :, coord, rows, lanes]
        return ref.at[:, coord, :, rows, lanes]

    def copies_a(i):
        axis = first_axis(i)
        return [
            remote(
                chunk_source(i, (mine(axis) + delta) % SIDE), a_buf.at[i, mine(axis)],
                sa_s.at[i, delta - 1], sa_r.at[i, delta - 1], along(axis, delta),
            )
            for delta in range(1, SIDE)
        ]

    def own_copy_a(i):
        coord = mine(first_axis(i))
        return pltpu.make_async_copy(chunk_source(i, coord), a_buf.at[i, coord], own_a.at[i])

    def copies_b(i):
        axis = 1 - first_axis(i)
        return [
            remote(
                a_buf.at[i, :, :, (mine(axis) + delta) % SIDE], b_bufs[i].at[mine(axis)],
                sb_s.at[i, delta - 1], sb_r.at[i, delta - 1], along(axis, delta),
            )
            for delta in range(1, SIDE)
        ]

    def own_copy_b(i):
        coord = mine(1 - first_axis(i))
        return pltpu.make_async_copy(a_buf.at[i, :, :, coord], b_bufs[i].at[coord], own_b.at[i])

    def copy_z(i, delta):
        return remote(
            zsend.at[i % RING, delta - 1], zrecvs[i].at[req],
            sz_s.at[i, delta - 1], sz_r.at[i, delta - 1], ((req + delta) % N_REQ, pos),
        )

    def start_a(i):
        for copy in copies_a(i):
            copy.start()

    def a_to_b(i):
        own_copy_a(i).wait()
        for copy in copies_a(i):
            copy.wait_recv()
        for copy in copies_b(i):
            copy.start()
        own_copy_b(i).start()

    def b_to_z(i):
        own_copy_b(i).wait()
        for copy in copies_b(i):
            copy.wait_recv()
        if i >= RING:
            for delta in range(1, N_REQ):
                copy_z(i - RING, delta).wait_send()

        def stage(delta, carry):
            k = chosen[(req + delta) % N_REQ]
            zsend[i % RING, delta - 1] = b_bufs[i][:, :, k]
            copy_z(i, delta).start()
            return carry

        lax.fori_loop(1, N_REQ, stage, 0)
        zrecvs[i][req] = b_bufs[i][:, :, chosen[req]]

    def wait_z(i):
        for delta in range(1, N_REQ):
            copy_z(i, delta).wait_recv()

    def out_copies(kind):
        if kind == "idx":
            return pltpu.make_async_copy(kifin, out_idx, out_sem.at[0])
        return pltpu.make_async_copy(kfin, out_lat, out_sem.at[1])

    def finalize(i):
        kind, plane, half = CHUNKS[i]
        by_x = first_axis(i) == 0

        def page(n, carry):
            outer, inner = n // SIDE, n % SIDE
            l = outer * SIDE + inner if by_x else inner * SIDE + outer
            base = (l * (SIDE * SIDE) + pos) * PAGE
            row = lax.broadcasted_iota(jnp.int32, (HALF, 128), 0)
            for k in range(NEW):
                tile = zrecvs[i][sources[k], outer, inner]
                if kind == "rope":
                    for part in range(2):
                        keep = row[:, :ROPE] + (base + part * HALF) < limits[k]
                        value = tile[:, part * ROPE : (part + 1) * ROPE].astype(F32)
                        kfin[k, l, part * HALF : (part + 1) * HALF, KV:LAT] = jnp.where(
                            keep, value, 0.0
                        ).astype(BF)
                else:
                    keep = row + (base + half * HALF) < limits[k]
                    value = jnp.where(keep, tile.astype(F32), 0.0).astype(BF)
                    rows = slice(half * HALF, (half + 1) * HALF)
                    if kind == "idx":
                        kifin[k, l, rows, :] = value
                    else:
                        kfin[k, l, rows, plane * 128 : (plane + 1) * 128] = value
            return carry

        lax.fori_loop(0, SIDE * SIDE, page, 0)

    spans = (pl.ds(0, BATCH // 2), pl.ds(BATCH // 2, BATCH // 2))

    def gather_views(phase, way):
        if phase == 0:
            return (qown.at[spans[way]], q_all.at[y, x, spans[way]])
        if way == 0:
            block = q_all.at[y, :, spans[way]]
        else:
            block = q_all.at[:, x, spans[way]]
        return (block, block)

    def gather_near(phase):
        copies = []
        for way in range(2):
            axis = way if phase == 0 else 1 - way
            src, dst = gather_views(phase, way)
            for n, delta in enumerate((1, SIDE - 1)):
                at = (phase, way, 0, n)
                copies.append(remote(src, dst, ag_s.at[at], ag_r.at[at], along(axis, delta)))
        return copies

    def gather_far(phase):
        copies = []
        for way in range(2):
            axis = way if phase == 0 else 1 - way
            for n, delta in enumerate((1, SIDE - 1)):
                rows = pl.ds(n * (QROWS // 2), QROWS // 2)
                fx = (x - delta) % SIDE if axis == 0 else x
                fy = (y - delta) % SIDE if axis == 1 else y
                if phase == 0:
                    block = q_all.at[fy, fx, spans[way], rows]
                elif way == 0:
                    block = q_all.at[fy, :, spans[way], rows]
                else:
                    block = q_all.at[:, fx, spans[way], rows]
                at = (phase, way, 1, n)
                copies.append(remote(block, block, ag_s.at[at], ag_r.at[at], along(axis, delta)))
        return copies

    def weight_copies(phase):
        axis = phase
        block = w_all.at[y, x] if phase == 0 else w_all.at[y]
        return [
            remote(
                wown if phase == 0 else block, block, aw_s.at[phase, delta - 1],
                aw_r.at[phase, delta - 1], along(axis, delta),
            )
            for delta in range(1, SIDE)
        ]

    own_q = pltpu.make_async_copy(qown, q_all.at[y, x], load_sem.at[0])
    own_w = pltpu.make_async_copy(wown, w_all.at[y, x], load_sem.at[1])
    load_ki = pltpu.make_async_copy(residx, ki_res, load_sem.at[2])

    def load_k(b):
        return pltpu.make_async_copy(reslat.at[b], kbuf.at[b % 2], kb_sem.at[b])

    def as_row(column):
        size = column.shape[0]
        row = lax.broadcasted_iota(jnp.int32, (size, size), 0)
        lane = lax.broadcasted_iota(jnp.int32, (size, size), 1)
        return jnp.sum(jnp.where(row == lane, column, 0.0), axis=0, keepdims=True)

    def as_column(values, first):
        row = lax.broadcasted_iota(jnp.int32, (QROWS, 128), 0)
        lane = lax.broadcasted_iota(jnp.int32, (QROWS, 128), 1)
        return jnp.sum(jnp.where(lane == row + first, values, 0.0), axis=1, keepdims=True)

    def attend(b, g, keys, flipped):
        b0, half = GROUPS[g][0], STAT_ROWS[g] // 2

        def part(n, carry):
            q = q_all[pl.ds(2 * n, 2), :, b, :, 0:LAT].reshape(2 * SIDE * QROWS, LAT)
            k = keys()
            key_dim = 0 if flipped else 1
            s = lax.dot_general(q, k, (((1,), (key_dim,)), ((), ())), preferred_element_type=F32)
            s = (s * SCALE).reshape(2 * SIDE, QROWS, CTX_DEV) + bias[b][None]
            s = s.reshape(2 * SIDE * QROWS, CTX_DEV)
            top = jnp.maximum(jnp.max(s, axis=1, keepdims=True), -1e29)
            e = jnp.exp(s - top)
            total = jnp.sum(e, axis=1, keepdims=True)
            v = k[:KV] if flipped else k[:, :KV]
            o = lax.dot_general(
                e.astype(BF), v, (((1,), (1 - key_dim,)), ((), ())), preferred_element_type=F32
            )
            numer[pl.ds(2 * n, 2), :, b] = o.astype(BF).reshape(2, SIDE, QROWS, KV)
            cols = pl.ds(pl.multiple_of(n * 256, 256), 256)
            stats[g, b - b0 : b - b0 + 1, cols] = as_row(top)
            stats[g, b - b0 + half : b - b0 + half + 1, cols] = as_row(total)
            return carry

        lax.fori_loop(0, 2, part, 0)

    def index_scores(b, keys):
        shape = (SIDE * SIDE // 2, STEPS, HEADS_DEV, 128)
        both = q_all[:, :, b, :, KV:QW].astype(F32).reshape((SIDE * SIDE // 2, 2) + shape[1:])
        even, odd = both[:, 0].reshape(-1, 8, 128), both[:, 1].reshape(-1, 8, 128)
        row = lax.broadcasted_iota(jnp.int32, even.shape, 1)
        lane = lax.broadcasted_iota(jnp.int32, even.shape, 2)
        upper = jnp.where(lane < ROPE, pltpu.roll(even, ROPE, 2), pltpu.roll(even, 4, 1))
        lower = jnp.where(lane < ROPE, pltpu.roll(pltpu.roll(odd, ROPE, 2), 4, 1), odd)
        iq_buf[...] = jnp.where(row < 4, upper, lower).reshape(-1, 128).astype(BF)
        high = lax.broadcasted_iota(jnp.int32, (QROWS, 128), 0) % 8 < 4
        weights = []
        for pair in range(SIDE * SIDE // 2):
            w_even = w_all[pair // 2, 2 * (pair % 2), b : b + 1]
            w_odd = w_all[pair // 2, 2 * (pair % 2) + 1, b : b + 1]
            weights.append(as_column(jnp.where(high, w_even, w_odd), 0))
        weight = jnp.concatenate(weights, axis=0)

        def part(n, carry):
            k = keys(n)
            logits = lax.dot_general(
                iq_buf[...], k, (((1,), (1,)), ((), ())), preferred_element_type=F32
            )
            value = jnp.maximum(logits, 0.0) * weight
            cols = pl.ds(pl.multiple_of(n * 256, 256), 256)
            out_is[b, :, cols] = jnp.sum(value.reshape(SIDE * SIDE // 2, QROWS, 256), axis=0)
            return carry

        lax.fori_loop(0, CTX_DEV // 256, part, 0)

    def attend_res(b):
        load_k(b).wait()
        attend(b, 0, lambda: kbuf[b % 2], True)
        if b + 2 < RES:
            load_k(b + 2).start()

    def attend_new(k, g):
        attend(RES + k, g, lambda: kfin[k].reshape(CTX_DEV, LAT), False)

    def index_res(b):
        index_scores(b, lambda n: ki_res[b, pl.ds(pl.multiple_of(n * 256, 256), 256)])

    def index_new(k):
        index_scores(RES + k, lambda n: kifin[k, pl.ds(n * 4, 4)].reshape(256, IDIM))

    def lanes(way):
        return pl.ds(way * 256, 256)

    def reduce_copies(g, phase, way):
        b0, count = GROUPS[g]
        span, stat = pl.ds(b0, count), pl.ds(0, STAT_ROWS[g])
        axis = way if phase == 0 else 1 - way
        copies = []
        for delta in range(1, SIDE):
            other = (mine(axis) + delta) % SIDE
            to_y = other if axis == 1 else y
            tile = pl.ds(pl.multiple_of(to_y * 128, 128), 128)
            if phase == 0:
                src = numer.at[:, other, span, :, lanes(way)]
                src_st, dst_st = stats.at[g, stat], rsa.at[g, way, delta - 1, stat]
                if way == 1:
                    src = numer.at[other, :, span, :, lanes(way)]
                    src_st = stats.at[g, stat, tile]
                    dst_st = rsa.at[g, way, delta - 1, stat, pl.ds(0, 128)]
                dst = ra.at[way, delta - 1, :, span]
            else:
                src, src_st = nb_buf.at[way, other, span], stb.at[g, way, stat, tile]
                dst, dst_st = rb.at[way, delta - 1, span], rsb.at[g, way, delta - 1, stat]
            target = along(axis, delta)
            for which, (s, d) in enumerate(((src, dst), (src_st, dst_st))):
                at = (g, phase, way, which, delta - 1)
                copies.append(remote(s, d, rs_s.at[at], rs_r.at[at], target))
        return copies

    def start_reduce(g, phase, way):
        for copy in reduce_copies(g, phase, way):
            copy.start()

    def merged(g, blocks):
        half = STAT_ROWS[g] // 2
        tops = [block[:half] for block in blocks]
        top = tops[0]
        for value in tops[1:]:
            top = jnp.maximum(top, value)
        factors = [jnp.exp(value - top) for value in tops]
        total = factors[0] * blocks[0][half:]
        for factor, block in zip(factors[1:], blocks[1:]):
            total = total + factor * block[half:]
        return top, factors, total

    def combine_a(g, way):
        b0, count = GROUPS[g]
        half = STAT_ROWS[g] // 2
        stat = slice(0, STAT_ROWS[g])
        for copy in reduce_copies(g, 0, way):
            copy.wait_recv()
        if way == 0:
            blocks = [stats[g, stat]] + [rsa[g, way, d, stat] for d in range(SIDE - 1)]
            cols = slice(0, SIDE * 128)
        else:
            blocks = [stats[g, stat, pl.ds(pl.multiple_of(y * 128, 128), 128)]]
            blocks += [rsa[g, way, d, stat, 0:128] for d in range(SIDE - 1)]
            cols = pl.ds(pl.multiple_of(y * 128, 128), 128)
        top, factors, total = merged(g, blocks)
        stb[g, way, 0:half, cols] = top
        stb[g, way, half : 2 * half, cols] = total
        for d in range(SIDE):
            fbuf[d, 0:half, cols] = factors[d]

        def block(j, carry):
            tile = pl.ds(pl.multiple_of((j if way == 0 else y) * 128, 128), 128)
            first = (x if way == 0 else j) * QROWS
            for n in range(count):
                if way == 0:
                    own = numer[j, x, b0 + n, :, 0:256]
                else:
                    own = numer[y, j, b0 + n, :, 256:512]
                acc = own.astype(F32) * as_column(fbuf[0, n : n + 1, tile], first)
                for d in range(SIDE - 1):
                    factor = as_column(fbuf[d + 1, n : n + 1, tile], first)
                    acc = acc + ra[way, d, j, b0 + n].astype(F32) * factor
                nb_buf[way, j, b0 + n] = acc.astype(BF)
            return carry

        lax.fori_loop(0, SIDE, block, 0)
        start_reduce(g, 1, way)

    def combine_b(g, way):
        b0, count = GROUPS[g]
        stat = slice(0, STAT_ROWS[g])
        for copy in reduce_copies(g, 1, way):
            copy.wait_recv()
        here = mine(1 - way)
        blocks = [stb[g, way, stat, pl.ds(pl.multiple_of(y * 128, 128), 128)]]
        blocks += [rsb[g, way, d, stat] for d in range(SIDE - 1)]
        _, factors, total = merged(g, blocks)
        factors = [factor / total for factor in factors]
        for n in range(count):
            acc = nb_buf[way, here, b0 + n].astype(F32) * as_column(factors[0][n : n + 1], x * QROWS)
            for d in range(SIDE - 1):
                factor = as_column(factors[d + 1][n : n + 1], x * QROWS)
                acc = acc + rb[way, d, b0 + n].astype(F32) * factor
            out_latent[b0 + n, :, way * 256 : (way + 1) * 256] = acc.astype(BF)

    own_q.start()
    own_w.start()
    for i in range(2):
        own_copy_a(i).start()
        start_a(i)
    for copy in gather_near(0) + weight_copies(0):
        copy.start()
    for i in range(2, 5):
        own_copy_a(i).start()
        start_a(i)
    load_ki.start()
    load_k(0).start()
    load_k(1).start()
    stats[...] = jnp.zeros_like(stats)
    a_to_b(0)
    a_to_b(1)
    b_to_z(0)
    own_q.wait()
    own_w.wait()
    for copy in gather_near(0) + weight_copies(0):
        copy.wait_recv()
    for copy in gather_far(0) + weight_copies(1):
        copy.start()
    b_to_z(1)
    for copy in gather_far(0):
        copy.wait_recv()
    for copy in gather_near(1):
        copy.start()
    a_to_b(2)

    for i in range(N_CH):
        wait_z(i)
        if i + 2 < N_CH:
            b_to_z(i + 2)
        if i + 3 < N_CH:
            a_to_b(i + 3)
        if i + 5 < N_CH:
            own_copy_a(i + 5).start()
            start_a(i + 5)
        finalize(i)
        if i == 1:
            out_copies("idx").start()
        if i == 1:
            for copy in gather_near(1):
                copy.wait_recv()
            for copy in gather_far(1):
                copy.start()
        if i == 3:
            for copy in gather_far(1) + weight_copies(1):
                copy.wait_recv()
            attend_res(0)
        elif i == 4:
            attend_res(1)
            attend_res(2)
            attend_res(3)
        elif i == 5:
            attend_res(4)
            attend_res(5)
            for way in range(2):
                start_reduce(0, 0, way)
            load_ki.wait()
            index_res(0)
            index_res(1)
        elif i == 6:
            for b in range(2, RES):
                index_res(b)
        elif i == 7:
            for way in range(2):
                combine_a(0, way)
            index_new(0)
            index_new(1)
        elif i == 8:
            index_new(2)
            index_new(3)
        elif i == 9:
            for way in range(2):
                combine_b(0, way)
    out_copies("lat").start()
    attend_new(0, 1)
    attend_new(1, 1)
    for way in range(2):
        start_reduce(1, 0, way)
    attend_new(2, 2)
    attend_new(3, 2)
    for way in range(2):
        start_reduce(2, 0, way)
    for g in (1, 2):
        for way in range(2):
            combine_a(g, way)
    for g in (1, 2):
        for way in range(2):
            combine_b(g, way)

    for i in range(N_CH):
        for copy in copies_a(i) + copies_b(i):
            copy.wait_send()
    for i in range(N_CH - RING, N_CH):
        for delta in range(1, N_REQ):
            copy_z(i, delta).wait_send()
    for phase in range(2):
        for copy in gather_near(phase) + gather_far(phase) + weight_copies(phase):
            copy.wait_send()
        for g in range(len(GROUPS)):
            for way in range(2):
                for copy in reduce_copies(g, phase, way):
                    copy.wait_send()
    out_copies("idx").wait()
    out_copies("lat").wait()


def run_kernel(*operands):
    smem = pl.BlockSpec(memory_space=pltpu.SMEM)
    vmem = pl.BlockSpec(memory_space=pltpu.VMEM)
    hbm = pl.BlockSpec(memory_space=pl.ANY)
    dma = pltpu.SemaphoreType.DMA
    n_groups = len(GROUPS)
    tile = (SIDE, SIDE, HALF, 128)
    return pl.pallas_call(
        kernel,
        out_shape=(
            jax.ShapeDtypeStruct((NEW, PG_LOC, PAGE, LAT), BF),
            jax.ShapeDtypeStruct((NEW, PG_LOC, PAGE, IDIM), BF),
            jax.ShapeDtypeStruct((BATCH, QROWS, CTX_DEV), F32),
            jax.ShapeDtypeStruct((BATCH, QROWS, KV), BF),
            jax.ShapeDtypeStruct((N_CH, SIDE, NEW, SIDE, HALF, 128), BF),
        ),
        in_specs=[smem] * 3 + [hbm] * 7 + [vmem],
        out_specs=(hbm, hbm, vmem, vmem, hbm),
        scratch_shapes=[
            (pltpu.VMEM((SIDE, SIDE, NEW, HALF, 128), BF),) * N_CH,
            pltpu.VMEM((RING, N_REQ - 1) + tile, BF),
            (pltpu.VMEM((N_REQ,) + tile, BF),) * N_CH,
            pltpu.VMEM((SIDE, SIDE, BATCH, QROWS, QW), BF),
            pltpu.VMEM((SIDE, SIDE, 16, 128), F32),
            pltpu.VMEM((SIDE * SIDE // 2 * QROWS, IDIM), BF),
            pltpu.VMEM((2, LAT, CTX_DEV), BF),
            pltpu.VMEM((RES, CTX_DEV, IDIM), BF),
            pltpu.VMEM((NEW, PG_LOC, PAGE, LAT), BF),
            pltpu.VMEM((NEW, PG_LOC, PAGE, IDIM), BF),
            pltpu.VMEM((SIDE, SIDE, BATCH, QROWS, KV), BF),
            pltpu.VMEM((n_groups, 16, SIDE * 128), F32),
            pltpu.VMEM((2, SIDE - 1, SIDE, BATCH, QROWS, 256), BF),
            pltpu.VMEM((n_groups, 2, SIDE - 1, 16, SIDE * 128), F32),
            pltpu.VMEM((2, SIDE, BATCH, QROWS, 256), BF),
            pltpu.VMEM((n_groups, 2, 16, SIDE * 128), F32),
            pltpu.VMEM((2, SIDE - 1, BATCH, QROWS, 256), BF),
            pltpu.VMEM((n_groups, 2, SIDE - 1, 16, 128), F32),
            pltpu.VMEM((SIDE, 8, SIDE * 128), F32),
            dma((N_CH, 3)), dma((N_CH, 3)), dma((N_CH, 3)), dma((N_CH, 3)),
            dma((N_CH, N_REQ - 1)), dma((N_CH, N_REQ - 1)),
            dma((N_CH,)), dma((N_CH,)), dma((3,)), dma((2,)), dma((RES,)),
            dma((2, 2, 2, 2)), dma((2, 2, 2, 2)), dma((2, 3)), dma((2, 3)),
            dma((n_groups, 2, 2, 2, 3)), dma((n_groups, 2, 2, 2, 3)),
        ],
        compiler_params=pltpu.CompilerParams(
            collective_id=0, has_side_effects=True, vmem_limit_bytes=63 * 2**20
        ),
        name="decode_step",
    )(*operands)


def body(
    res_latent, res_index, res_len, arrive_latent, arrive_index, arrive_len, destination,
    q_nope, q_rope, w_uk, w_uv, idx_query, idx_weight, selected,
):
    req_index = lax.axis_index("req")
    pos_index = lax.axis_index("pos")
    routing = destination.reshape(N_REQ, NEW)
    group_ids = jnp.arange(N_REQ, dtype=jnp.int32)
    arrival_ids = jnp.arange(NEW, dtype=jnp.int32)
    matches = routing[req_index][None, :] == group_ids[:, None]
    chosen = jnp.sum(jnp.where(matches, arrival_ids[None, :], 0), axis=1)
    sources = jnp.sum(jnp.where(routing == req_index, group_ids[:, None], 0), axis=0)
    new_lengths = arrive_len[sources * NEW + arrival_ids]

    paged = arrive_latent.reshape(NEW, SIDE, SIDE, PAGE, LAT)
    rope = jnp.concatenate([paged[..., :HALF, KV:], paged[..., HALF:, KV:]], axis=-1)

    absorbed = jnp.einsum("sbhn,hnc->sbhc", q_nope, w_uk, preferred_element_type=F32).astype(BF)
    halves = jnp.concatenate([idx_query[..., : IDIM // 2], idx_query[..., IDIM // 2 :]], axis=2)
    queries = jnp.concatenate([absorbed, q_rope, halves], axis=-1)
    queries = queries.transpose(1, 0, 2, 3).reshape(BATCH, QROWS, QW)
    weights = jnp.concatenate([idx_weight, idx_weight], axis=2).astype(F32)
    weights = weights.transpose(1, 0, 2).reshape(BATCH, QROWS)
    weights = jnp.pad(weights, ((0, 16 - BATCH), (0, 128 - QROWS)))

    here = (selected % (SIDE * SIDE) == pos_index)[..., None]
    slots = jnp.arange(PG_LOC, dtype=jnp.int32)
    live = jnp.any(here & (selected[..., None] // (SIDE * SIDE) == slots), axis=2)
    bias = jnp.where(jnp.repeat(live, PAGE, axis=-1), 0.0, -1e30).astype(F32)
    bias = jnp.broadcast_to(
        bias.transpose(1, 0, 2)[:, :, None, :], (BATCH, STEPS, HEADS_DEV, CTX_DEV)
    ).reshape(BATCH, QROWS, CTX_DEV)

    new_latent, new_index, raw, latent, _ = run_kernel(
        chosen.astype(jnp.int32), sources.astype(jnp.int32), new_lengths,
        paged, arrive_index.reshape(NEW, SIDE, SIDE, PAGE, IDIM), rope,
        queries, weights, res_latent[:, 0].transpose(0, 2, 1), res_index[:, 0], bias,
    )

    scored = jnp.sum(raw.reshape(BATCH, STEPS, HEADS_DEV, CTX_DEV), axis=2) * IDIM ** (-0.5)
    lengths = jnp.concatenate([res_len, new_lengths])
    offsets = jnp.arange(CTX_DEV, dtype=jnp.int32)
    logical = (offsets // PAGE * (SIDE * SIDE) + pos_index) * PAGE + offsets % PAGE
    index_scores = jnp.where(logical[None, None, :] < lengths[:, None, None], scored, 0.0)
    index_scores = index_scores.transpose(1, 0, 2)[:, :, None, :]

    latent = latent.reshape(BATCH, STEPS, HEADS_DEV, KV)
    head_out = jnp.einsum("bshc,hcd->sbhd", latent, w_uv, preferred_element_type=F32).astype(BF)
    return (
        new_latent.reshape(NEW, 1, CTX_DEV, LAT),
        new_index.reshape(NEW, 1, CTX_DEV, IDIM),
        index_scores,
        head_out,
    )


def solution(mesh):
    placed = (
        P("req", "pos", None, None),
        P("req", "pos", None, None),
        P("req"),
        P("req", "pos", None),
        P("req", "pos", None),
        P(),
        P(),
        P(None, "req", "pos", None),
        P(None, "req", "pos", None),
        P("pos", None, None),
        P("pos", None, None),
        P(None, "req", "pos", None),
        P(None, "req", "pos"),
        P(None, "req", None),
    )
    return jax.shard_map(
        body,
        mesh=mesh,
        in_specs=placed,
        out_specs=(
            P("req", "pos", None, None),
            P("req", "pos", None, None),
            P(None, "req", "pos", None),
            P(None, "req", "pos", None),
        ),
        check_vma=False,
    )
```

```python
import jax
import jax.numpy as jnp
from jax import lax
from jax.experimental import pallas as pl
from jax.experimental.pallas import tpu as pltpu
from jax.sharding import PartitionSpec as P

KV, ROPE, NOPE, IDIM, PAGE = 512, 64, 128, 128, 64
LAT = KV + ROPE
STEPS, RES, NEW, BATCH, HEADS_DEV = 4, 6, 4, 10, 8
CTX_DEV, PG_LOC, N_REQ, SIDE = 1024, 16, 8, 4
QW = 640
HALF = PAGE // 2
QROWS = STEPS * HEADS_DEV
BF, F32 = jnp.bfloat16, jnp.float32
MESH = pl.DeviceIdType.MESH
SCALE = (NOPE + ROPE) ** (-0.5)

N_IDX, N_LAT, DEPTH = 2, LAT // 64, 64
N_CH = N_IDX + N_LAT
N_XF = (N_LAT + 1) // 2
RING = 3
GROUPS = ((0, 6), (6, 1), (7, 1), (8, 1), (9, 1))
STAT_ROWS = (16, 8, 8, 8, 8)


def kernel(
    chosen, sources, limits, lat, idx, qown, wown, reslat, residx, bias,
    out_lat, out_idx, out_is, out_latent, a_idx, a_lat,
    ay_bufs, b_idx, b_lat, loads, pack_x, pack_y, unpacked, zs_idx, zs_lat, zrecvs, q_all, w_all, iq_buf, kbuf, ki_res, kfin, kifin, numer, stats,
    ra, rsa, nb_buf, stb, rb, rsb, fbuf,
    sa_s, sa_r, sb_s, sb_r, sz_s, sz_r, own_a, own_b, lat_sem, load_sem, out_sem, kb_sem,
    ag_s, ag_r, aw_s, aw_r, rs_s, rs_r,
):
    req = lax.axis_index("req")
    pos = lax.axis_index("pos")
    y, x = pos // SIDE, pos % SIDE

    def along(axis, delta):
        if axis == 0:
            return (req, y * SIDE + (x + delta) % SIDE)
        return (req, ((y + delta) % SIDE) * SIDE + x)

    def mine(axis):
        return x if axis == 0 else y

    def remote(src, dst, send, recv, target):
        return pltpu.make_async_remote_copy(
            src_ref=src, dst_ref=dst, send_sem=send, recv_sem=recv,
            device_id=target, device_id_type=MESH,
        )

    barrier = pltpu.get_barrier_semaphore()
    for delta in range(1, N_REQ):
        pl.semaphore_signal(barrier, 1, device_id=((req + delta) % N_REQ, pos), device_id_type=MESH)
    for axis in range(2):
        for delta in range(1, SIDE):
            pl.semaphore_signal(barrier, 1, device_id=along(axis, delta), device_id_type=MESH)
    pl.semaphore_wait(barrier, N_REQ - 1 + 2 * (SIDE - 1))

    def first_axis(i):
        return i % 2

    def depth(i):
        return pl.ds((i - N_IDX) * DEPTH, DEPTH)

    def load_lat(i):
        n = (i - N_IDX) // 2
        return pltpu.make_async_copy(lat.at[:, depth(i)], loads.at[n % 2], lat_sem.at[n])

    def a_slot(i):
        if i < N_IDX:
            return a_idx.at[i]
        return a_lat.at[(i - N_IDX) // 2] if first_axis(i) == 0 else ay_bufs[(i - N_IDX) // 2]

    def a_source(i, coord):
        if i < N_IDX:
            rows = pl.ds(i * HALF, HALF)
            return idx.at[:, :, coord, rows] if first_axis(i) == 0 else idx.at[:, coord, :, rows]
        if first_axis(i) == 0:
            return pack_x.at[(i - N_IDX) // 2 % 2, coord]
        return lat.at[:, depth(i), pl.ds(pl.multiple_of(coord * 256, 256), 256)]

    def b_slot(i):
        return b_idx[i] if i < N_IDX else b_lat[i - N_IDX]

    def b_source(i, coord):
        if i >= N_IDX and first_axis(i) == 1:
            return pack_y.at[(i - N_IDX) // 2 % 2, coord]
        return a_slot(i).at[:, :, coord]

    def copies_a(i):
        axis = first_axis(i)
        return [
            remote(
                a_source(i, (mine(axis) + delta) % SIDE), a_slot(i).at[mine(axis)],
                sa_s.at[i, delta - 1], sa_r.at[i, delta - 1], along(axis, delta),
            )
            for delta in range(1, SIDE)
        ]

    def own_copy_a(i):
        coord = mine(first_axis(i))
        return pltpu.make_async_copy(a_source(i, coord), a_slot(i).at[coord], own_a.at[i])

    def copies_b(i):
        axis = 1 - first_axis(i)
        return [
            remote(
                b_source(i, (mine(axis) + delta) % SIDE), b_slot(i).at[mine(axis)],
                sb_s.at[i, delta - 1], sb_r.at[i, delta - 1], along(axis, delta),
            )
            for delta in range(1, SIDE)
        ]

    def own_copy_b(i):
        coord = mine(1 - first_axis(i))
        return pltpu.make_async_copy(b_source(i, coord), b_slot(i).at[coord], own_b.at[i])

    def z_send(i):
        return zs_idx.at[i] if i < N_IDX else zs_lat.at[(i - N_IDX) % RING]

    def copy_z(i, delta):
        return remote(
            z_send(i).at[delta - 1], zrecvs[i].at[req],
            sz_s.at[i, delta - 1], sz_r.at[i, delta - 1], ((req + delta) % N_REQ, pos),
        )

    sent = set()

    def drain(kind, i):
        if (kind, i) in sent:
            return
        sent.add((kind, i))
        copies = {"a": copies_a, "b": copies_b}.get(kind)
        if copies is None:
            copies = lambda n: [copy_z(n, delta) for delta in range(1, N_REQ)]
        for copy in copies(i):
            copy.wait_send()

    low = lax.broadcasted_iota(jnp.int32, (DEPTH, 128), 1) < PAGE

    def swapped(first, second):
        first, second = first.astype(F32), second.astype(F32)
        lows = jnp.where(low, first, pltpu.roll(second, PAGE, 1))
        highs = jnp.where(low, pltpu.roll(first, PAGE, 1), second)
        return lows.astype(BF), highs.astype(BF)

    def lane_tile(n):
        return pl.ds(pl.multiple_of(n * 128, 128), 128)

    def start_a(i):
        if i >= N_IDX and first_axis(i) == 0:
            n = (i - N_IDX) // 2
            load_lat(i).wait()
            if n >= 2:
                drain("a", i - 4)

            def pack(row, carry):
                for pair in range(2):
                    for kp in range(2):
                        tile = lane_tile(row * 2 + pair)
                        lows, highs = swapped(
                            loads[n % 2, 2 * kp, :, tile], loads[n % 2, 2 * kp + 1, :, tile]
                        )
                        pack_x[n % 2, 2 * pair, kp, row] = lows
                        pack_x[n % 2, 2 * pair + 1, kp, row] = highs
                return carry

            lax.fori_loop(0, SIDE, pack, 0)
            if i + 4 < N_CH:
                load_lat(i + 4).start()
        own_copy_a(i).start()
        for copy in copies_a(i):
            copy.start()

    def a_to_b(i):
        own_copy_a(i).wait()
        for copy in copies_a(i):
            copy.wait_recv()
        if i >= N_IDX and first_axis(i) == 1:
            n = (i - N_IDX) // 2
            if n >= 2:
                drain("b", i - 4)

            def pack(row, carry):
                for pair in range(2):
                    tile = slice(pair * 128, (pair + 1) * 128)
                    for kp in range(2):
                        lows, highs = swapped(
                            ay_bufs[n][row, 2 * kp, :, tile], ay_bufs[n][row, 2 * kp + 1, :, tile]
                        )
                        pack_y[n % 2, 2 * pair, row, kp] = lows
                        pack_y[n % 2, 2 * pair + 1, row, kp] = highs
                return carry

            lax.fori_loop(0, SIDE, pack, 0)
        for copy in copies_b(i):
            copy.start()
        own_copy_b(i).start()

    def b_to_z(i):
        own_copy_b(i).wait()
        for copy in copies_b(i):
            copy.wait_recv()
        if i >= N_IDX + RING:
            drain("z", i - RING)
        buf = b_slot(i)
        if i >= N_IDX:
            def unpack(row, carry):
                for pair in range(2):
                    for kp in range(2):
                        if first_axis(i) == 0:
                            even, odd = buf[row, 2 * pair, kp], buf[row, 2 * pair + 1, kp]
                        else:
                            even, odd = buf[2 * pair, row, kp], buf[2 * pair + 1, row, kp]
                        lows, highs = swapped(even, odd)
                        unpacked[2 * kp, :, lane_tile(row * 2 + pair)] = lows
                        unpacked[2 * kp + 1, :, lane_tile(row * 2 + pair)] = highs
                return carry

            lax.fori_loop(0, SIDE, unpack, 0)

        def block(k):
            return buf[:, :, k] if i < N_IDX else unpacked[k]

        def stage(delta, carry):
            z_send(i)[delta - 1] = block(chosen[(req + delta) % N_REQ])
            copy_z(i, delta).start()
            return carry

        lax.fori_loop(1, N_REQ, stage, 0)
        zrecvs[i][req] = block(chosen[req])

    def wait_z(i):
        for delta in range(1, N_REQ):
            copy_z(i, delta).wait_recv()

    def out_copies(kind):
        if kind == "idx":
            return pltpu.make_async_copy(kifin, out_idx, out_sem.at[0])
        return pltpu.make_async_copy(kfin, out_lat, out_sem.at[1])

    def finalize_idx(i):
        def page(n, carry):
            outer, inner = n // SIDE, n % SIDE
            l = outer * SIDE + inner if first_axis(i) == 0 else inner * SIDE + outer
            base = (l * (SIDE * SIDE) + pos) * PAGE + i * HALF
            row = lax.broadcasted_iota(jnp.int32, (HALF, 128), 0)
            for k in range(NEW):
                tile = zrecvs[i][sources[k], outer, inner].astype(F32)
                value = jnp.where(row + base < limits[k], tile, 0.0).astype(BF)
                kifin[k, l, i * HALF : (i + 1) * HALF, :] = value
            return carry

        lax.fori_loop(0, SIDE * SIDE, page, 0)

    def finalize(i):
        if i < N_IDX:
            return finalize_idx(i)

        def tiles(n, carry):
            lane = lax.broadcasted_iota(jnp.int32, (DEPTH, 128), 1)
            logical = (2 * n + lane // PAGE) * (SIDE * SIDE * PAGE) + pos * PAGE + lane % PAGE
            for k in range(NEW):
                tile = zrecvs[i][sources[k], :, lane_tile(n)].astype(F32)
                value = jnp.where(logical < limits[k], tile, 0.0).astype(BF)
                kfin[k, depth(i), lane_tile(n)] = value
            return carry

        lax.fori_loop(0, CTX_DEV // 128, tiles, 0)

    spans = (pl.ds(0, BATCH // 2), pl.ds(BATCH // 2, BATCH // 2))

    def gather_views(phase, way):
        if phase == 0:
            return (qown.at[spans[way]], q_all.at[y, x, spans[way]])
        if way == 0:
            block = q_all.at[y, :, spans[way]]
        else:
            block = q_all.at[:, x, spans[way]]
        return (block, block)

    def gather_near(phase):
        copies = []
        for way in range(2):
            axis = way if phase == 0 else 1 - way
            src, dst = gather_views(phase, way)
            for n, delta in enumerate((1, SIDE - 1)):
                at = (phase, way, 0, n)
                copies.append(remote(src, dst, ag_s.at[at], ag_r.at[at], along(axis, delta)))
        return copies

    def gather_far(phase):
        copies = []
        for way in range(2):
            axis = way if phase == 0 else 1 - way
            for n, delta in enumerate((1, SIDE - 1)):
                rows = pl.ds(n * (QROWS // 2), QROWS // 2)
                fx = (x - delta) % SIDE if axis == 0 else x
                fy = (y - delta) % SIDE if axis == 1 else y
                if phase == 0:
                    block = q_all.at[fy, fx, spans[way], rows]
                elif way == 0:
                    block = q_all.at[fy, :, spans[way], rows]
                else:
                    block = q_all.at[:, fx, spans[way], rows]
                at = (phase, way, 1, n)
                copies.append(remote(block, block, ag_s.at[at], ag_r.at[at], along(axis, delta)))
        return copies

    def weight_copies(phase):
        axis = phase
        block = w_all.at[y, x] if phase == 0 else w_all.at[y]
        return [
            remote(
                wown if phase == 0 else block, block, aw_s.at[phase, delta - 1],
                aw_r.at[phase, delta - 1], along(axis, delta),
            )
            for delta in range(1, SIDE)
        ]

    own_q = pltpu.make_async_copy(qown, q_all.at[y, x], load_sem.at[0])
    own_w = pltpu.make_async_copy(wown, w_all.at[y, x], load_sem.at[1])
    load_ki = pltpu.make_async_copy(residx, ki_res, load_sem.at[2])

    def load_k(b):
        return pltpu.make_async_copy(reslat.at[b], kbuf.at[b % 2], kb_sem.at[b])

    def as_row(column):
        size = column.shape[0]
        row = lax.broadcasted_iota(jnp.int32, (size, size), 0)
        lane = lax.broadcasted_iota(jnp.int32, (size, size), 1)
        return jnp.sum(jnp.where(row == lane, column, 0.0), axis=0, keepdims=True)

    def as_column(values, first):
        row = lax.broadcasted_iota(jnp.int32, (QROWS, 128), 0)
        lane = lax.broadcasted_iota(jnp.int32, (QROWS, 128), 1)
        return jnp.sum(jnp.where(lane == row + first, values, 0.0), axis=1, keepdims=True)

    def attend(b, g, keys):
        b0, half = GROUPS[g][0], STAT_ROWS[g] // 2

        def part(n, carry):
            q = q_all[pl.ds(2 * n, 2), :, b, :, 0:LAT].reshape(2 * SIDE * QROWS, LAT)
            k = keys()
            s = jnp.dot(q, k, preferred_element_type=F32)
            s = (s * SCALE).reshape(2 * SIDE, QROWS, CTX_DEV) + bias[b][None]
            s = s.reshape(2 * SIDE * QROWS, CTX_DEV)
            top = jnp.maximum(jnp.max(s, axis=1, keepdims=True), -1e29)
            e = jnp.exp(s - top)
            total = jnp.sum(e, axis=1, keepdims=True)
            o = lax.dot_general(
                e.astype(BF), k[:KV], (((1,), (1,)), ((), ())), preferred_element_type=F32
            )
            numer[pl.ds(2 * n, 2), :, b] = o.astype(BF).reshape(2, SIDE, QROWS, KV)
            cols = pl.ds(pl.multiple_of(n * 256, 256), 256)
            stats[g, b - b0 : b - b0 + 1, cols] = as_row(top)
            stats[g, b - b0 + half : b - b0 + half + 1, cols] = as_row(total)
            return carry

        lax.fori_loop(0, 2, part, 0)

    def index_scores(b, keys):
        shape = (SIDE * SIDE // 2, STEPS, HEADS_DEV, 128)
        both = q_all[:, :, b, :, KV:QW].astype(F32).reshape((SIDE * SIDE // 2, 2) + shape[1:])
        even, odd = both[:, 0].reshape(-1, 8, 128), both[:, 1].reshape(-1, 8, 128)
        row = lax.broadcasted_iota(jnp.int32, even.shape, 1)
        lane = lax.broadcasted_iota(jnp.int32, even.shape, 2)
        upper = jnp.where(lane < ROPE, pltpu.roll(even, ROPE, 2), pltpu.roll(even, 4, 1))
        lower = jnp.where(lane < ROPE, pltpu.roll(pltpu.roll(odd, ROPE, 2), 4, 1), odd)
        iq_buf[...] = jnp.where(row < 4, upper, lower).reshape(-1, 128).astype(BF)
        high = lax.broadcasted_iota(jnp.int32, (QROWS, 128), 0) % 8 < 4
        weights = []
        for pair in range(SIDE * SIDE // 2):
            w_even = w_all[pair // 2, 2 * (pair % 2), b : b + 1]
            w_odd = w_all[pair // 2, 2 * (pair % 2) + 1, b : b + 1]
            weights.append(as_column(jnp.where(high, w_even, w_odd), 0))
        weight = jnp.concatenate(weights, axis=0)

        def part(n, carry):
            k = keys(n)
            logits = lax.dot_general(
                iq_buf[...], k, (((1,), (1,)), ((), ())), preferred_element_type=F32
            )
            value = jnp.maximum(logits, 0.0) * weight
            cols = pl.ds(pl.multiple_of(n * 256, 256), 256)
            out_is[b, :, cols] = jnp.sum(value.reshape(SIDE * SIDE // 2, QROWS, 256), axis=0)
            return carry

        lax.fori_loop(0, CTX_DEV // 256, part, 0)

    def attend_res(b):
        load_k(b).wait()
        attend(b, 0, lambda: kbuf[b % 2])
        if b + 2 < RES:
            load_k(b + 2).start()

    def attend_new(k, g):
        attend(RES + k, g, lambda: kfin[k])

    def index_res(b):
        index_scores(b, lambda n: ki_res[b, pl.ds(pl.multiple_of(n * 256, 256), 256)])

    def index_new(k):
        index_scores(RES + k, lambda n: kifin[k, pl.ds(n * 4, 4)].reshape(256, IDIM))

    def lanes(way):
        return pl.ds(way * 256, 256)

    def reduce_copies(g, phase, way):
        b0, count = GROUPS[g]
        span, stat = pl.ds(b0, count), pl.ds(0, STAT_ROWS[g])
        axis = way if phase == 0 else 1 - way
        copies = []
        for delta in range(1, SIDE):
            other = (mine(axis) + delta) % SIDE
            to_y = other if axis == 1 else y
            tile = pl.ds(pl.multiple_of(to_y * 128, 128), 128)
            if phase == 0:
                src = numer.at[:, other, span, :, lanes(way)]
                src_st, dst_st = stats.at[g, stat], rsa.at[g, way, delta - 1, stat]
                if way == 1:
                    src = numer.at[other, :, span, :, lanes(way)]
                    src_st = stats.at[g, stat, tile]
                    dst_st = rsa.at[g, way, delta - 1, stat, pl.ds(0, 128)]
                dst = ra.at[way, delta - 1, :, span]
            else:
                src, src_st = nb_buf.at[way, other, span], stb.at[g, way, stat, tile]
                dst, dst_st = rb.at[way, delta - 1, span], rsb.at[g, way, delta - 1, stat]
            target = along(axis, delta)
            for which, (s, d) in enumerate(((src, dst), (src_st, dst_st))):
                at = (g, phase, way, which, delta - 1)
                copies.append(remote(s, d, rs_s.at[at], rs_r.at[at], target))
        return copies

    def start_reduce(g, phase, way):
        for copy in reduce_copies(g, phase, way):
            copy.start()

    def merged(g, blocks):
        half = STAT_ROWS[g] // 2
        tops = [block[:half] for block in blocks]
        top = tops[0]
        for value in tops[1:]:
            top = jnp.maximum(top, value)
        factors = [jnp.exp(value - top) for value in tops]
        total = factors[0] * blocks[0][half:]
        for factor, block in zip(factors[1:], blocks[1:]):
            total = total + factor * block[half:]
        return top, factors, total

    def combine_a(g, way):
        b0, count = GROUPS[g]
        half = STAT_ROWS[g] // 2
        stat = slice(0, STAT_ROWS[g])
        for copy in reduce_copies(g, 0, way):
            copy.wait_recv()
        if way == 0:
            blocks = [stats[g, stat]] + [rsa[g, way, d, stat] for d in range(SIDE - 1)]
            cols = slice(0, SIDE * 128)
        else:
            blocks = [stats[g, stat, pl.ds(pl.multiple_of(y * 128, 128), 128)]]
            blocks += [rsa[g, way, d, stat, 0:128] for d in range(SIDE - 1)]
            cols = pl.ds(pl.multiple_of(y * 128, 128), 128)
        top, factors, total = merged(g, blocks)
        stb[g, way, 0:half, cols] = top
        stb[g, way, half : 2 * half, cols] = total
        for d in range(SIDE):
            fbuf[d, 0:half, cols] = factors[d]

        def block(j, carry):
            tile = pl.ds(pl.multiple_of((j if way == 0 else y) * 128, 128), 128)
            first = (x if way == 0 else j) * QROWS
            for n in range(count):
                if way == 0:
                    own = numer[j, x, b0 + n, :, 0:256]
                else:
                    own = numer[y, j, b0 + n, :, 256:512]
                acc = own.astype(F32) * as_column(fbuf[0, n : n + 1, tile], first)
                for d in range(SIDE - 1):
                    factor = as_column(fbuf[d + 1, n : n + 1, tile], first)
                    acc = acc + ra[way, d, j, b0 + n].astype(F32) * factor
                nb_buf[way, j, b0 + n] = acc.astype(BF)
            return carry

        lax.fori_loop(0, SIDE, block, 0)
        start_reduce(g, 1, way)

    def combine_b(g, way):
        b0, count = GROUPS[g]
        stat = slice(0, STAT_ROWS[g])
        for copy in reduce_copies(g, 1, way):
            copy.wait_recv()
        here = mine(1 - way)
        blocks = [stb[g, way, stat, pl.ds(pl.multiple_of(y * 128, 128), 128)]]
        blocks += [rsb[g, way, d, stat] for d in range(SIDE - 1)]
        _, factors, total = merged(g, blocks)
        factors = [factor / total for factor in factors]
        for n in range(count):
            acc = nb_buf[way, here, b0 + n].astype(F32) * as_column(factors[0][n : n + 1], x * QROWS)
            for d in range(SIDE - 1):
                factor = as_column(factors[d + 1][n : n + 1], x * QROWS)
                acc = acc + rb[way, d, b0 + n].astype(F32) * factor
            out_latent[b0 + n, :, way * 256 : (way + 1) * 256] = acc.astype(BF)

    def start(copies):
        for copy in copies:
            copy.start()

    def arrived(copies):
        for copy in copies:
            copy.wait_recv()

    load_lat(N_IDX).start()
    load_lat(N_IDX + 2).start()
    start_a(0)
    start_a(1)
    own_q.start()
    own_w.start()
    load_ki.start()
    load_k(0).start()
    load_k(1).start()
    start_a(2)
    start_a(3)
    stats[...] = jnp.zeros_like(stats)
    a_to_b(0)
    a_to_b(1)
    start(gather_near(0) + weight_copies(0))
    start_a(4)
    b_to_z(0)
    a_to_b(2)
    start_a(5)
    b_to_z(1)
    a_to_b(3)
    own_q.wait()
    own_w.wait()
    arrived(gather_near(0) + weight_copies(0))
    start(gather_far(0) + weight_copies(1))
    start_a(6)
    b_to_z(2)
    a_to_b(4)

    for i in range(N_CH):
        wait_z(i)
        if i + 3 < N_CH:
            b_to_z(i + 3)
        if i + 5 < N_CH:
            a_to_b(i + 5)
        if i + 7 < N_CH:
            start_a(i + 7)
        finalize(i)
        if i == 0:
            arrived(gather_far(0))
            start(gather_near(1))
        elif i == 1:
            out_copies("idx").start()
        elif i == 2:
            arrived(gather_near(1))
            start(gather_far(1))
        elif i == 4:
            arrived(gather_far(1) + weight_copies(1))
            attend_res(0)
            attend_res(1)
        elif i == 5:
            attend_res(2)
            attend_res(3)
            load_ki.wait()
            index_res(0)
        elif i == 6:
            attend_res(4)
            attend_res(5)
            for way in range(2):
                start_reduce(0, 0, way)
            index_res(1)
        elif i == 7:
            for b in range(2, RES):
                index_res(b)
        elif i == 8:
            for way in range(2):
                combine_a(0, way)
            index_new(0)
            index_new(1)
        elif i == 9:
            index_new(2)
            index_new(3)
        if i == N_CH - 1:
            out_copies("lat").start()
            attend_new(0, 1)
            for way in range(2):
                start_reduce(1, 0, way)
            attend_new(1, 2)
            for way in range(2):
                start_reduce(2, 0, way)
            for way in range(2):
                combine_b(0, way)
    for k in (2, 3):
        attend_new(k, k + 1)
        for way in range(2):
            start_reduce(k + 1, 0, way)
    for g in (1, 2, 3, 4):
        for way in range(2):
            combine_a(g, way)
    for g in (1, 2, 3, 4):
        for way in range(2):
            combine_b(g, way)

    for i in range(N_CH):
        for kind in ("a", "b", "z"):
            drain(kind, i)
    for phase in range(2):
        for copy in gather_near(phase) + gather_far(phase) + weight_copies(phase):
            copy.wait_send()
        for g in range(len(GROUPS)):
            for way in range(2):
                for copy in reduce_copies(g, phase, way):
                    copy.wait_send()
    out_copies("idx").wait()
    out_copies("lat").wait()


def run_kernel(*operands):
    smem = pl.BlockSpec(memory_space=pltpu.SMEM)
    vmem = pl.BlockSpec(memory_space=pltpu.VMEM)
    hbm = pl.BlockSpec(memory_space=pl.ANY)
    dma = pltpu.SemaphoreType.DMA
    n_groups = len(GROUPS)
    tile = (SIDE, SIDE, HALF, 128)
    return pl.pallas_call(
        kernel,
        out_shape=(
            jax.ShapeDtypeStruct((NEW, LAT, CTX_DEV), BF),
            jax.ShapeDtypeStruct((NEW, PG_LOC, PAGE, IDIM), BF),
            jax.ShapeDtypeStruct((BATCH, QROWS, CTX_DEV), F32),
            jax.ShapeDtypeStruct((BATCH, QROWS, KV), BF),
            jax.ShapeDtypeStruct((N_IDX, SIDE, NEW, SIDE, HALF, 128), BF),
            jax.ShapeDtypeStruct((N_XF, SIDE, 2, SIDE, DEPTH, 128), BF),
        ),
        in_specs=[smem] * 3 + [hbm] * 6 + [vmem],
        out_specs=(hbm, hbm, vmem, vmem, hbm, hbm),
        scratch_shapes=[
            (pltpu.VMEM((SIDE, NEW, DEPTH, 256), BF),) * (N_LAT - N_XF),
            (pltpu.VMEM((SIDE, SIDE, NEW, HALF, 128), BF),) * N_IDX,
            (pltpu.VMEM((SIDE, SIDE, 2, DEPTH, 128), BF),) * N_LAT,
            pltpu.VMEM((2, NEW, DEPTH, CTX_DEV), BF),
            pltpu.VMEM((2, SIDE, 2, SIDE, DEPTH, 128), BF),
            pltpu.VMEM((2, SIDE, SIDE, 2, DEPTH, 128), BF),
            pltpu.VMEM((NEW, DEPTH, CTX_DEV), BF),
            pltpu.VMEM((N_IDX, N_REQ - 1) + tile, BF),
            pltpu.VMEM((RING, N_REQ - 1, DEPTH, CTX_DEV), BF),
            (pltpu.VMEM((N_REQ,) + tile, BF),) * N_IDX
            + (pltpu.VMEM((N_REQ, DEPTH, CTX_DEV), BF),) * N_LAT,
            pltpu.VMEM((SIDE, SIDE, BATCH, QROWS, QW), BF),
            pltpu.VMEM((SIDE, SIDE, 16, 128), F32),
            pltpu.VMEM((SIDE * SIDE // 2 * QROWS, IDIM), BF),
            pltpu.VMEM((2, LAT, CTX_DEV), BF),
            pltpu.VMEM((RES, CTX_DEV, IDIM), BF),
            pltpu.VMEM((NEW, LAT, CTX_DEV), BF),
            pltpu.VMEM((NEW, PG_LOC, PAGE, IDIM), BF),
            pltpu.VMEM((SIDE, SIDE, BATCH, QROWS, KV), BF),
            pltpu.VMEM((n_groups, 16, SIDE * 128), F32),
            pltpu.VMEM((2, SIDE - 1, SIDE, BATCH, QROWS, 256), BF),
            pltpu.VMEM((n_groups, 2, SIDE - 1, 16, SIDE * 128), F32),
            pltpu.VMEM((2, SIDE, BATCH, QROWS, 256), BF),
            pltpu.VMEM((n_groups, 2, 16, SIDE * 128), F32),
            pltpu.VMEM((2, SIDE - 1, BATCH, QROWS, 256), BF),
            pltpu.VMEM((n_groups, 2, SIDE - 1, 16, 128), F32),
            pltpu.VMEM((SIDE, 8, SIDE * 128), F32),
            dma((N_CH, 3)), dma((N_CH, 3)), dma((N_CH, 3)), dma((N_CH, 3)),
            dma((N_CH, N_REQ - 1)), dma((N_CH, N_REQ - 1)),
            dma((N_CH,)), dma((N_CH,)), dma((N_XF,)), dma((3,)), dma((2,)), dma((RES,)),
            dma((2, 2, 2, 2)), dma((2, 2, 2, 2)), dma((2, 3)), dma((2, 3)),
            dma((n_groups, 2, 2, 2, 3)), dma((n_groups, 2, 2, 2, 3)),
        ],
        compiler_params=pltpu.CompilerParams(
            collective_id=0, has_side_effects=True, vmem_limit_bytes=63 * 2**20
        ),
        name="decode_step",
    )(*operands)


def body(
    res_latent, res_index, res_len, arrive_latent, arrive_index, arrive_len, destination,
    q_nope, q_rope, w_uk, w_uv, idx_query, idx_weight, selected,
):
    req_index = lax.axis_index("req")
    pos_index = lax.axis_index("pos")
    routing = destination.reshape(N_REQ, NEW)
    group_ids = jnp.arange(N_REQ, dtype=jnp.int32)
    arrival_ids = jnp.arange(NEW, dtype=jnp.int32)
    matches = routing[req_index][None, :] == group_ids[:, None]
    chosen = jnp.sum(jnp.where(matches, arrival_ids[None, :], 0), axis=1)
    sources = jnp.sum(jnp.where(routing == req_index, group_ids[:, None], 0), axis=0)
    new_lengths = arrive_len[sources * NEW + arrival_ids]

    absorbed = jnp.einsum("sbhn,hnc->sbhc", q_nope, w_uk, preferred_element_type=F32).astype(BF)
    halves = jnp.concatenate([idx_query[..., : IDIM // 2], idx_query[..., IDIM // 2 :]], axis=2)
    queries = jnp.concatenate([absorbed, q_rope, halves], axis=-1)
    queries = queries.transpose(1, 0, 2, 3).reshape(BATCH, QROWS, QW)
    weights = jnp.concatenate([idx_weight, idx_weight], axis=2).astype(F32)
    weights = weights.transpose(1, 0, 2).reshape(BATCH, QROWS)
    weights = jnp.pad(weights, ((0, 16 - BATCH), (0, 128 - QROWS)))

    here = (selected % (SIDE * SIDE) == pos_index)[..., None]
    slots = jnp.arange(PG_LOC, dtype=jnp.int32)
    live = jnp.any(here & (selected[..., None] // (SIDE * SIDE) == slots), axis=2)
    bias = jnp.where(jnp.repeat(live, PAGE, axis=-1), 0.0, -1e30).astype(F32)
    bias = jnp.broadcast_to(
        bias.transpose(1, 0, 2)[:, :, None, :], (BATCH, STEPS, HEADS_DEV, CTX_DEV)
    ).reshape(BATCH, QROWS, CTX_DEV)

    new_latent, new_index, raw, latent, _, _ = run_kernel(
        chosen.astype(jnp.int32), sources.astype(jnp.int32), new_lengths,
        arrive_latent.transpose(0, 2, 1), arrive_index.reshape(NEW, SIDE, SIDE, PAGE, IDIM),
        queries, weights, res_latent[:, 0].transpose(0, 2, 1), res_index[:, 0], bias,
    )

    scored = jnp.sum(raw.reshape(BATCH, STEPS, HEADS_DEV, CTX_DEV), axis=2) * IDIM ** (-0.5)
    lengths = jnp.concatenate([res_len, new_lengths])
    offsets = jnp.arange(CTX_DEV, dtype=jnp.int32)
    logical = (offsets // PAGE * (SIDE * SIDE) + pos_index) * PAGE + offsets % PAGE
    index_scores = jnp.where(logical[None, None, :] < lengths[:, None, None], scored, 0.0)
    index_scores = index_scores.transpose(1, 0, 2)[:, :, None, :]

    latent = latent.reshape(BATCH, STEPS, HEADS_DEV, KV)
    head_out = jnp.einsum("bshc,hcd->sbhd", latent, w_uv, preferred_element_type=F32).astype(BF)
    return (
        new_latent.transpose(0, 2, 1).reshape(NEW, 1, CTX_DEV, LAT),
        new_index.reshape(NEW, 1, CTX_DEV, IDIM),
        index_scores,
        head_out,
    )


def solution(mesh):
    placed = (
        P("req", "pos", None, None),
        P("req", "pos", None, None),
        P("req"),
        P("req", "pos", None),
        P("req", "pos", None),
        P(),
        P(),
        P(None, "req", "pos", None),
        P(None, "req", "pos", None),
        P("pos", None, None),
        P("pos", None, None),
        P(None, "req", "pos", None),
        P(None, "req", "pos"),
        P(None, "req", None),
    )
    return jax.shard_map(
        body,
        mesh=mesh,
        in_specs=placed,
        out_specs=(
            P("req", "pos", None, None),
            P("req", "pos", None, None),
            P(None, "req", "pos", None),
            P(None, "req", "pos", None),
        ),
        check_vma=False,
    )
```

```python
import jax
import jax.numpy as jnp
from jax import lax
from jax.experimental import pallas as pl
from jax.experimental.pallas import tpu as pltpu
from jax.sharding import PartitionSpec as P

KV, ROPE, NOPE, IDIM, PAGE = 512, 64, 128, 128, 64
LAT = KV + ROPE
STEPS, RES, NEW, BATCH, HEADS_DEV = 4, 6, 4, 10, 8
CTX_DEV, PG_LOC, N_REQ, SIDE = 1024, 16, 8, 4
QW = 640
HALF = PAGE // 2
QROWS = STEPS * HEADS_DEV
BF, F32 = jnp.bfloat16, jnp.float32
MESH = pl.DeviceIdType.MESH
SCALE = (NOPE + ROPE) ** (-0.5)

N_IDX, N_LAT, DEPTH = 2, LAT // 64, 64
N_CH = N_IDX + N_LAT
N_XF = (N_LAT + 1) // 2
RING = 3
GROUPS = ((0, 6), (6, 1), (7, 1), (8, 1), (9, 1))
STAT_ROWS = (16, 8, 8, 8, 8)


def kernel(
    destination, arrive_len, res_len, lat, idx, wown, reslat, residx, w_uk, q_nope, q_rope, idx_query, selected,
    out_lat, out_idx, out_is, out_latent, a_idx, a_lat,
    qown, w_buf, live, idx_in, w_idx, ay_bufs, b_idx, b_lat, loads, pack_x, pack_y, unpacked, zs_idx, zs_lat, zrecvs, q_all, w_all, iq_buf, kbuf, ki_res, kfin, kifin, numer, stats,
    ra, rsa, nb_buf, stb, rb, rsb, fbuf,
    sa_s, sa_r, sb_s, sb_r, sz_s, sz_r, own_a, own_b, lat_sem, load_sem, out_sem, kb_sem,
    ag_s, ag_r, aw_s, aw_r, rs_s, rs_r,
):
    req = lax.axis_index("req")
    pos = lax.axis_index("pos")
    y, x = pos // SIDE, pos % SIDE

    def along(axis, delta):
        if axis == 0:
            return (req, y * SIDE + (x + delta) % SIDE)
        return (req, ((y + delta) % SIDE) * SIDE + x)

    def mine(axis):
        return x if axis == 0 else y

    def remote(src, dst, send, recv, target):
        return pltpu.make_async_remote_copy(
            src_ref=src, dst_ref=dst, send_sem=send, recv_sem=recv,
            device_id=target, device_id_type=MESH,
        )

    def chosen(group):
        k = jnp.int32(0)
        for n in range(1, NEW):
            k = jnp.maximum(k, jnp.where(destination[req * NEW + n] == group, n, 0))
        return k

    def source(k):
        s = jnp.int32(0)
        for n in range(1, N_REQ):
            s = jnp.maximum(s, jnp.where(destination[n * NEW + k] == req, n, 0))
        return s

    sources = [source(k) for k in range(NEW)]
    limits = [arrive_len[sources[k] * NEW + k] for k in range(NEW)]

    load_idx = pltpu.make_async_copy(idx, idx_in, load_sem.at[3])
    load_idx.start()
    barrier = pltpu.get_barrier_semaphore()
    for delta in range(1, N_REQ):
        pl.semaphore_signal(barrier, 1, device_id=((req + delta) % N_REQ, pos), device_id_type=MESH)
    for axis in range(2):
        for delta in range(1, SIDE):
            pl.semaphore_signal(barrier, 1, device_id=along(axis, delta), device_id_type=MESH)
    pl.semaphore_wait(barrier, N_REQ - 1 + 2 * (SIDE - 1))

    def first_axis(i):
        return i % 2

    def depth(i):
        return pl.ds((i - N_IDX) * DEPTH, DEPTH)

    def load_lat(i):
        n = (i - N_IDX) // 2
        return pltpu.make_async_copy(lat.at[:, depth(i)], loads.at[n % 2], lat_sem.at[n])

    def a_slot(i):
        if i < N_IDX:
            return a_idx.at[i]
        return a_lat.at[(i - N_IDX) // 2] if first_axis(i) == 0 else ay_bufs[(i - N_IDX) // 2]

    def a_source(i, coord):
        if i < N_IDX:
            return w_idx.at[i, :, :, coord] if first_axis(i) == 0 else w_idx.at[i, :, coord]
        if first_axis(i) == 0:
            return pack_x.at[(i - N_IDX) // 2 % 2, coord]
        return lat.at[:, depth(i), pl.ds(pl.multiple_of(coord * 256, 256), 256)]

    def b_slot(i):
        return b_idx[i] if i < N_IDX else b_lat[i - N_IDX]

    def b_source(i, coord):
        if i >= N_IDX and first_axis(i) == 1:
            return pack_y.at[(i - N_IDX) // 2 % 2, coord]
        return a_slot(i).at[:, :, coord]

    def copies_a(i):
        axis = first_axis(i)
        return [
            remote(
                a_source(i, (mine(axis) + delta) % SIDE), a_slot(i).at[mine(axis)],
                sa_s.at[i, delta - 1], sa_r.at[i, delta - 1], along(axis, delta),
            )
            for delta in range(1, SIDE)
        ]

    def own_copy_a(i):
        coord = mine(first_axis(i))
        return pltpu.make_async_copy(a_source(i, coord), a_slot(i).at[coord], own_a.at[i])

    def copies_b(i):
        axis = 1 - first_axis(i)
        return [
            remote(
                b_source(i, (mine(axis) + delta) % SIDE), b_slot(i).at[mine(axis)],
                sb_s.at[i, delta - 1], sb_r.at[i, delta - 1], along(axis, delta),
            )
            for delta in range(1, SIDE)
        ]

    def own_copy_b(i):
        coord = mine(1 - first_axis(i))
        return pltpu.make_async_copy(b_source(i, coord), b_slot(i).at[coord], own_b.at[i])

    def z_send(i):
        return zs_idx.at[i] if i < N_IDX else zs_lat.at[(i - N_IDX) % RING]

    def copy_z(i, delta):
        return remote(
            z_send(i).at[delta - 1], zrecvs[i].at[req],
            sz_s.at[i, delta - 1], sz_r.at[i, delta - 1], ((req + delta) % N_REQ, pos),
        )

    sent = set()

    def drain(kind, i):
        if (kind, i) in sent:
            return
        sent.add((kind, i))
        copies = {"a": copies_a, "b": copies_b}.get(kind)
        if copies is None:
            copies = lambda n: [copy_z(n, delta) for delta in range(1, N_REQ)]
        for copy in copies(i):
            copy.wait_send()

    low = lax.broadcasted_iota(jnp.int32, (DEPTH, 128), 1) < PAGE

    def swapped(first, second):
        first, second = first.astype(F32), second.astype(F32)
        lows = jnp.where(low, first, pltpu.roll(second, PAGE, 1))
        highs = jnp.where(low, pltpu.roll(first, PAGE, 1), second)
        return lows.astype(BF), highs.astype(BF)

    def lane_tile(n):
        return pl.ds(pl.multiple_of(n * 128, 128), 128)

    def start_a(i):
        if i >= N_IDX and first_axis(i) == 0:
            n = (i - N_IDX) // 2
            load_lat(i).wait()
            if n >= 2:
                drain("a", i - 4)

            def pack(row, carry):
                for pair in range(2):
                    for kp in range(2):
                        tile = lane_tile(row * 2 + pair)
                        lows, highs = swapped(
                            loads[n % 2, 2 * kp, :, tile], loads[n % 2, 2 * kp + 1, :, tile]
                        )
                        pack_x[n % 2, 2 * pair, kp, row] = lows
                        pack_x[n % 2, 2 * pair + 1, kp, row] = highs
                return carry

            lax.fori_loop(0, SIDE, pack, 0)
            if i + 4 < N_CH:
                load_lat(i + 4).start()
        own_copy_a(i).start()
        for copy in copies_a(i):
            copy.start()

    def a_to_b(i):
        own_copy_a(i).wait()
        for copy in copies_a(i):
            copy.wait_recv()
        if i >= N_IDX and first_axis(i) == 1:
            n = (i - N_IDX) // 2
            if n >= 2:
                drain("b", i - 4)

            def pack(row, carry):
                for pair in range(2):
                    tile = slice(pair * 128, (pair + 1) * 128)
                    for kp in range(2):
                        lows, highs = swapped(
                            ay_bufs[n][row, 2 * kp, :, tile], ay_bufs[n][row, 2 * kp + 1, :, tile]
                        )
                        pack_y[n % 2, 2 * pair, row, kp] = lows
                        pack_y[n % 2, 2 * pair + 1, row, kp] = highs
                return carry

            lax.fori_loop(0, SIDE, pack, 0)
        for copy in copies_b(i):
            copy.start()
        own_copy_b(i).start()

    def stage_z(i, block):
        def stage(delta, carry):
            z_send(i)[delta - 1] = block(chosen((req + delta) % N_REQ))
            copy_z(i, delta).start()
            return carry

        lax.fori_loop(1, N_REQ, stage, 0)
        zrecvs[i][req] = block(chosen(req))

    def index_to_z(i):
        stage_z(i, lambda k: idx_in[k, :, :, i * HALF : (i + 1) * HALF])

    def index_to_a(i):
        for k in range(NEW):
            w_idx[i, k] = zrecvs[i][sources[k]]
        start_a(i)

    def b_to_z(i):
        own_copy_b(i).wait()
        for copy in copies_b(i):
            copy.wait_recv()
        if i >= N_IDX + RING:
            drain("z", i - RING)
        buf = b_slot(i)

        def unpack(row, carry):
            for pair in range(2):
                for kp in range(2):
                    if first_axis(i) == 0:
                        even, odd = buf[row, 2 * pair, kp], buf[row, 2 * pair + 1, kp]
                    else:
                        even, odd = buf[2 * pair, row, kp], buf[2 * pair + 1, row, kp]
                    lows, highs = swapped(even, odd)
                    unpacked[2 * kp, :, lane_tile(row * 2 + pair)] = lows
                    unpacked[2 * kp + 1, :, lane_tile(row * 2 + pair)] = highs
            return carry

        lax.fori_loop(0, SIDE, unpack, 0)

        def block(k):
            return unpacked[k]

        stage_z(i, block)

    def wait_z(i):
        for delta in range(1, N_REQ):
            copy_z(i, delta).wait_recv()

    def out_copies(kind):
        if kind == "idx":
            return pltpu.make_async_copy(kifin, out_idx, out_sem.at[0])
        return pltpu.make_async_copy(kfin, out_lat, out_sem.at[1])

    def finalize_idx(i):
        own_copy_b(i).wait()
        for copy in copies_b(i):
            copy.wait_recv()

        def page(n, carry):
            outer, inner = n // SIDE, n % SIDE
            l = outer * SIDE + inner if first_axis(i) == 0 else inner * SIDE + outer
            base = (l * (SIDE * SIDE) + pos) * PAGE + i * HALF
            row = lax.broadcasted_iota(jnp.int32, (HALF, 128), 0)
            for k in range(NEW):
                tile = b_idx[i][outer, inner, k].astype(F32)
                value = jnp.where(row + base < limits[k], tile, 0.0).astype(BF)
                kifin[k, l, i * HALF : (i + 1) * HALF, :] = value
            return carry

        lax.fori_loop(0, SIDE * SIDE, page, 0)

    def finalize(i):
        def tiles(n, carry):
            lane = lax.broadcasted_iota(jnp.int32, (DEPTH, 128), 1)
            logical = (2 * n + lane // PAGE) * (SIDE * SIDE * PAGE) + pos * PAGE + lane % PAGE
            for k in range(NEW):
                tile = zrecvs[i][sources[k], :, lane_tile(n)].astype(F32)
                value = jnp.where(logical < limits[k], tile, 0.0).astype(BF)
                kfin[k, depth(i), lane_tile(n)] = value
            return carry

        lax.fori_loop(0, CTX_DEV // 128, tiles, 0)

    spans = (pl.ds(0, BATCH // 2), pl.ds(BATCH // 2, BATCH // 2))

    def gather_views(phase, way):
        if phase == 0:
            return (qown.at[spans[way]], q_all.at[y, x, spans[way]])
        if way == 0:
            block = q_all.at[y, :, spans[way]]
        else:
            block = q_all.at[:, x, spans[way]]
        return (block, block)

    def gather_near(phase):
        copies = []
        for way in range(2):
            axis = way if phase == 0 else 1 - way
            src, dst = gather_views(phase, way)
            for n, delta in enumerate((1, SIDE - 1)):
                at = (phase, way, 0, n)
                copies.append(remote(src, dst, ag_s.at[at], ag_r.at[at], along(axis, delta)))
        return copies

    def gather_far(phase):
        copies = []
        for way in range(2):
            axis = way if phase == 0 else 1 - way
            for n, delta in enumerate((1, SIDE - 1)):
                rows = pl.ds(n * (QROWS // 2), QROWS // 2)
                fx = (x - delta) % SIDE if axis == 0 else x
                fy = (y - delta) % SIDE if axis == 1 else y
                if phase == 0:
                    block = q_all.at[fy, fx, spans[way], rows]
                elif way == 0:
                    block = q_all.at[fy, :, spans[way], rows]
                else:
                    block = q_all.at[:, fx, spans[way], rows]
                at = (phase, way, 1, n)
                copies.append(remote(block, block, ag_s.at[at], ag_r.at[at], along(axis, delta)))
        return copies

    def weight_copies(phase):
        axis = phase
        block = w_all.at[y, x] if phase == 0 else w_all.at[y]
        return [
            remote(
                wown if phase == 0 else block, block, aw_s.at[phase, delta - 1],
                aw_r.at[phase, delta - 1], along(axis, delta),
            )
            for delta in range(1, SIDE)
        ]

    own_q = pltpu.make_async_copy(qown, q_all.at[y, x], load_sem.at[0])
    own_w = pltpu.make_async_copy(wown, w_all.at[y, x], load_sem.at[1])
    load_w = pltpu.make_async_copy(w_uk, w_buf, load_sem.at[4])
    load_ki = pltpu.make_async_copy(residx, ki_res, load_sem.at[2])

    def load_k(b):
        return pltpu.make_async_copy(reslat.at[b], kbuf.at[b % 2], kb_sem.at[b])

    def absorb():
        rows = BATCH * HEADS_DEV
        head = lax.broadcasted_iota(jnp.int32, (rows, KV), 0) % HEADS_DEV
        for pair in range(STEPS // 2):
            blocks = []
            for t in (2 * pair, 2 * pair + 1):
                q = q_nope[t].reshape(rows, NOPE)
                total = jnp.zeros((rows, KV), F32)
                for h in range(HEADS_DEV):
                    part = jnp.dot(q, w_buf[h], preferred_element_type=F32)
                    total = jnp.where(head == h, part, total)
                keys = idx_query[t].astype(F32)
                halves = jnp.concatenate([keys[..., :ROPE], keys[..., ROPE:]], axis=1)
                tail = jnp.concatenate([q_rope[t].astype(F32), halves], axis=2)
                blocks.append(
                    jnp.concatenate([total.reshape(BATCH, HEADS_DEV, KV), tail], axis=2)
                )
            block = jnp.concatenate(blocks, axis=1).astype(BF)
            qown[:, pair * 16 : (pair + 1) * 16, :] = block

    def find_live(b):
        page = lax.broadcasted_iota(jnp.int32, (STEPS, CTX_DEV), 1) // PAGE * (SIDE * SIDE) + pos
        wanted = selected[b]
        found = wanted[:, 0:1] == page
        for n in range(1, wanted.shape[1]):
            found = found | (wanted[:, n : n + 1] == page)
        bias = jnp.where(found, 0.0, -1e30)
        for t in range(STEPS):
            live[t * HEADS_DEV : (t + 1) * HEADS_DEV, :] = jnp.broadcast_to(
                bias[t : t + 1], (HEADS_DEV, CTX_DEV)
            )

    def as_row(column):
        size = column.shape[0]
        row = lax.broadcasted_iota(jnp.int32, (size, size), 0)
        lane = lax.broadcasted_iota(jnp.int32, (size, size), 1)
        return jnp.sum(jnp.where(row == lane, column, 0.0), axis=0, keepdims=True)

    def as_column(values, first):
        row = lax.broadcasted_iota(jnp.int32, (QROWS, 128), 0)
        lane = lax.broadcasted_iota(jnp.int32, (QROWS, 128), 1)
        return jnp.sum(jnp.where(lane == row + first, values, 0.0), axis=1, keepdims=True)

    def attend(b, g, keys):
        b0, half = GROUPS[g][0], STAT_ROWS[g] // 2
        find_live(b)

        def part(n, carry):
            q = q_all[pl.ds(2 * n, 2), :, b, :, 0:LAT].reshape(2 * SIDE * QROWS, LAT)
            k = keys()
            s = jnp.dot(q, k, preferred_element_type=F32)
            s = (s * SCALE).reshape(2 * SIDE, QROWS, CTX_DEV) + live[...][None]
            s = s.reshape(2 * SIDE * QROWS, CTX_DEV)
            top = jnp.maximum(jnp.max(s, axis=1, keepdims=True), -1e29)
            e = jnp.exp(s - top)
            total = jnp.sum(e, axis=1, keepdims=True)
            o = lax.dot_general(
                e.astype(BF), k[:KV], (((1,), (1,)), ((), ())), preferred_element_type=F32
            )
            numer[pl.ds(2 * n, 2), :, b] = o.astype(BF).reshape(2, SIDE, QROWS, KV)
            cols = pl.ds(pl.multiple_of(n * 256, 256), 256)
            stats[g, b - b0 : b - b0 + 1, cols] = as_row(top)
            stats[g, b - b0 + half : b - b0 + half + 1, cols] = as_row(total)
            return carry

        lax.fori_loop(0, 2, part, 0)

    def index_scores(b, length, keys):
        shape = (SIDE * SIDE // 2, STEPS, HEADS_DEV, 128)
        both = q_all[:, :, b, :, KV:QW].astype(F32).reshape((SIDE * SIDE // 2, 2) + shape[1:])
        even, odd = both[:, 0].reshape(-1, 8, 128), both[:, 1].reshape(-1, 8, 128)
        row = lax.broadcasted_iota(jnp.int32, even.shape, 1)
        lane = lax.broadcasted_iota(jnp.int32, even.shape, 2)
        upper = jnp.where(lane < ROPE, pltpu.roll(even, ROPE, 2), pltpu.roll(even, 4, 1))
        lower = jnp.where(lane < ROPE, pltpu.roll(pltpu.roll(odd, ROPE, 2), 4, 1), odd)
        iq_buf[...] = jnp.where(row < 4, upper, lower).reshape(-1, 128).astype(BF)
        high = lax.broadcasted_iota(jnp.int32, (QROWS, 128), 0) % 8 < 4
        weights = []
        for pair in range(SIDE * SIDE // 2):
            w_even = w_all[pair // 2, 2 * (pair % 2), b : b + 1]
            w_odd = w_all[pair // 2, 2 * (pair % 2) + 1, b : b + 1]
            weights.append(as_column(jnp.where(high, w_even, w_odd), 0))
        weight = jnp.concatenate(weights, axis=0)

        def part(n, carry):
            k = keys(n)
            logits = lax.dot_general(
                iq_buf[...], k, (((1,), (1,)), ((), ())), preferred_element_type=F32
            )
            value = jnp.maximum(logits, 0.0) * weight
            cols = pl.ds(pl.multiple_of(n * 256, 256), 256)
            value = jnp.sum(value.reshape(SIDE * SIDE // 2, QROWS, 256), axis=0)
            value = jnp.sum(value.reshape(STEPS, HEADS_DEV, 256), axis=1) * IDIM ** (-0.5)
            lane = lax.broadcasted_iota(jnp.int32, (STEPS, 256), 1) + n * 256
            logical = lane // PAGE * (SIDE * SIDE * PAGE) + pos * PAGE + lane % PAGE
            value = jnp.where(logical < length, value, 0.0)
            for t in range(STEPS):
                out_is[t, b, :, cols] = value[t : t + 1]
            return carry

        lax.fori_loop(0, CTX_DEV // 256, part, 0)

    def attend_res(b):
        load_k(b).wait()
        attend(b, 0, lambda: kbuf[b % 2])
        if b + 2 < RES:
            load_k(b + 2).start()

    def attend_new(k, g):
        attend(RES + k, g, lambda: kfin[k])

    def index_res(b):
        index_scores(b, res_len[b], lambda n: ki_res[b, pl.ds(pl.multiple_of(n * 256, 256), 256)])

    def index_new(k):
        index_scores(RES + k, limits[k], lambda n: kifin[k, pl.ds(n * 4, 4)].reshape(256, IDIM))

    def lanes(way):
        return pl.ds(way * 256, 256)

    def reduce_copies(g, phase, way):
        b0, count = GROUPS[g]
        span, stat = pl.ds(b0, count), pl.ds(0, STAT_ROWS[g])
        axis = way if phase == 0 else 1 - way
        copies = []
        for delta in range(1, SIDE):
            other = (mine(axis) + delta) % SIDE
            to_y = other if axis == 1 else y
            tile = pl.ds(pl.multiple_of(to_y * 128, 128), 128)
            if phase == 0:
                src = numer.at[:, other, span, :, lanes(way)]
                src_st, dst_st = stats.at[g, stat], rsa.at[g, way, delta - 1, stat]
                if way == 1:
                    src = numer.at[other, :, span, :, lanes(way)]
                    src_st = stats.at[g, stat, tile]
                    dst_st = rsa.at[g, way, delta - 1, stat, pl.ds(0, 128)]
                dst = ra.at[way, delta - 1, :, span]
            else:
                src, src_st = nb_buf.at[way, other, span], stb.at[g, way, stat, tile]
                dst, dst_st = rb.at[way, delta - 1, span], rsb.at[g, way, delta - 1, stat]
            target = along(axis, delta)
            for which, (s, d) in enumerate(((src, dst), (src_st, dst_st))):
                at = (g, phase, way, which, delta - 1)
                copies.append(remote(s, d, rs_s.at[at], rs_r.at[at], target))
        return copies

    def start_reduce(g, phase, way):
        for copy in reduce_copies(g, phase, way):
            copy.start()

    def merged(g, blocks):
        half = STAT_ROWS[g] // 2
        tops = [block[:half] for block in blocks]
        top = tops[0]
        for value in tops[1:]:
            top = jnp.maximum(top, value)
        factors = [jnp.exp(value - top) for value in tops]
        total = factors[0] * blocks[0][half:]
        for factor, block in zip(factors[1:], blocks[1:]):
            total = total + factor * block[half:]
        return top, factors, total

    def combine_a(g, way):
        b0, count = GROUPS[g]
        half = STAT_ROWS[g] // 2
        stat = slice(0, STAT_ROWS[g])
        for copy in reduce_copies(g, 0, way):
            copy.wait_recv()
        if way == 0:
            blocks = [stats[g, stat]] + [rsa[g, way, d, stat] for d in range(SIDE - 1)]
            cols = slice(0, SIDE * 128)
        else:
            blocks = [stats[g, stat, pl.ds(pl.multiple_of(y * 128, 128), 128)]]
            blocks += [rsa[g, way, d, stat, 0:128] for d in range(SIDE - 1)]
            cols = pl.ds(pl.multiple_of(y * 128, 128), 128)
        top, factors, total = merged(g, blocks)
        stb[g, way, 0:half, cols] = top
        stb[g, way, half : 2 * half, cols] = total
        for d in range(SIDE):
            fbuf[d, 0:half, cols] = factors[d]

        def block(j, carry):
            tile = pl.ds(pl.multiple_of((j if way == 0 else y) * 128, 128), 128)
            first = (x if way == 0 else j) * QROWS
            for n in range(count):
                if way == 0:
                    own = numer[j, x, b0 + n, :, 0:256]
                else:
                    own = numer[y, j, b0 + n, :, 256:512]
                acc = own.astype(F32) * as_column(fbuf[0, n : n + 1, tile], first)
                for d in range(SIDE - 1):
                    factor = as_column(fbuf[d + 1, n : n + 1, tile], first)
                    acc = acc + ra[way, d, j, b0 + n].astype(F32) * factor
                nb_buf[way, j, b0 + n] = acc.astype(BF)
            return carry

        lax.fori_loop(0, SIDE, block, 0)
        start_reduce(g, 1, way)

    def combine_b(g, way):
        b0, count = GROUPS[g]
        stat = slice(0, STAT_ROWS[g])
        for copy in reduce_copies(g, 1, way):
            copy.wait_recv()
        here = mine(1 - way)
        blocks = [stb[g, way, stat, pl.ds(pl.multiple_of(y * 128, 128), 128)]]
        blocks += [rsb[g, way, d, stat] for d in range(SIDE - 1)]
        _, factors, total = merged(g, blocks)
        factors = [factor / total for factor in factors]
        for n in range(count):
            acc = nb_buf[way, here, b0 + n].astype(F32) * as_column(factors[0][n : n + 1], x * QROWS)
            for d in range(SIDE - 1):
                factor = as_column(factors[d + 1][n : n + 1], x * QROWS)
                acc = acc + rb[way, d, b0 + n].astype(F32) * factor
            out_latent[b0 + n, :, way * 256 : (way + 1) * 256] = acc.astype(BF)

    def start(copies):
        for copy in copies:
            copy.start()

    def arrived(copies):
        for copy in copies:
            copy.wait_recv()

    load_lat(N_IDX).start()
    load_lat(N_IDX + 2).start()
    load_w.start()
    own_w.start()
    load_idx.wait()
    index_to_z(0)
    index_to_z(1)
    start_a(2)
    start_a(3)
    load_ki.start()
    load_k(0).start()
    load_k(1).start()
    stats[...] = jnp.zeros_like(stats)
    start_a(4)
    a_to_b(2)
    a_to_b(3)
    load_w.wait()
    absorb()
    own_q.start()
    start(gather_near(0) + weight_copies(0))
    start_a(5)
    b_to_z(2)
    a_to_b(4)
    own_q.wait()
    own_w.wait()
    arrived(gather_near(0) + weight_copies(0))
    start(gather_far(0) + weight_copies(1))
    start_a(6)

    for i in range(N_CH):
        wait_z(i)
        if i + 3 < N_CH:
            b_to_z(i + 3)
        if i + 5 < N_CH:
            a_to_b(i + 5)
        if i + 7 < N_CH:
            start_a(i + 7)
        if i < N_IDX:
            index_to_a(i)
        else:
            finalize(i)
        if i == 0:
            arrived(gather_far(0))
            start(gather_near(1))
        elif i == 2:
            arrived(gather_near(1))
            start(gather_far(1))
            a_to_b(0)
        elif i == 3:
            a_to_b(1)
        elif i == 4:
            arrived(gather_far(1) + weight_copies(1))
            attend_res(0)
            attend_res(1)
        elif i == 5:
            attend_res(2)
            attend_res(3)
            load_ki.wait()
            index_res(0)
            finalize_idx(0)
            finalize_idx(1)
            out_copies("idx").start()
        elif i == 6:
            attend_res(4)
            attend_res(5)
            for way in range(2):
                start_reduce(0, 0, way)
            index_res(1)
        elif i == 7:
            for b in range(2, RES):
                index_res(b)
        elif i == 8:
            for way in range(2):
                combine_a(0, way)
            index_new(0)
            index_new(1)
        elif i == 9:
            index_new(2)
            index_new(3)
        if i == N_CH - 1:
            out_copies("lat").start()
            attend_new(0, 1)
            for way in range(2):
                start_reduce(1, 0, way)
            attend_new(1, 2)
            for way in range(2):
                start_reduce(2, 0, way)
            for way in range(2):
                combine_b(0, way)
    for k in (2, 3):
        attend_new(k, k + 1)
        for way in range(2):
            start_reduce(k + 1, 0, way)
    for g in (1, 2, 3, 4):
        for way in range(2):
            combine_a(g, way)
    for g in (1, 2, 3, 4):
        for way in range(2):
            combine_b(g, way)

    for i in range(N_CH):
        for kind in ("a", "b", "z"):
            drain(kind, i)
    for phase in range(2):
        for copy in gather_near(phase) + gather_far(phase) + weight_copies(phase):
            copy.wait_send()
        for g in range(len(GROUPS)):
            for way in range(2):
                for copy in reduce_copies(g, phase, way):
                    copy.wait_send()
    out_copies("idx").wait()
    out_copies("lat").wait()


def run_kernel(*operands):
    smem = pl.BlockSpec(memory_space=pltpu.SMEM)
    vmem = pl.BlockSpec(memory_space=pltpu.VMEM)
    hbm = pl.BlockSpec(memory_space=pl.ANY)
    dma = pltpu.SemaphoreType.DMA
    n_groups = len(GROUPS)
    tile = (SIDE, SIDE, HALF, 128)
    return pl.pallas_call(
        kernel,
        out_shape=(
            jax.ShapeDtypeStruct((NEW, LAT, CTX_DEV), BF),
            jax.ShapeDtypeStruct((NEW, PG_LOC, PAGE, IDIM), BF),
            jax.ShapeDtypeStruct((STEPS, BATCH, 1, CTX_DEV), F32),
            jax.ShapeDtypeStruct((BATCH, QROWS, KV), BF),
            jax.ShapeDtypeStruct((N_IDX, SIDE, NEW, SIDE, HALF, 128), BF),
            jax.ShapeDtypeStruct((N_XF, SIDE, 2, SIDE, DEPTH, 128), BF),
        ),
        in_specs=[smem] * 3 + [hbm] * 6 + [vmem] * 4,
        out_specs=(hbm, hbm, vmem, vmem, hbm, hbm),
        scratch_shapes=[
            pltpu.VMEM((BATCH, QROWS, QW), BF),
            pltpu.VMEM((HEADS_DEV, NOPE, KV), BF),
            pltpu.VMEM((QROWS, CTX_DEV), F32),
            pltpu.VMEM((NEW, SIDE, SIDE, PAGE, IDIM), BF),
            pltpu.VMEM((N_IDX, NEW) + tile, BF),
            (pltpu.VMEM((SIDE, NEW, DEPTH, 256), BF),) * (N_LAT - N_XF),
            (pltpu.VMEM((SIDE, SIDE, NEW, HALF, 128), BF),) * N_IDX,
            (pltpu.VMEM((SIDE, SIDE, 2, DEPTH, 128), BF),) * N_LAT,
            pltpu.VMEM((2, NEW, DEPTH, CTX_DEV), BF),
            pltpu.VMEM((2, SIDE, 2, SIDE, DEPTH, 128), BF),
            pltpu.VMEM((2, SIDE, SIDE, 2, DEPTH, 128), BF),
            pltpu.VMEM((NEW, DEPTH, CTX_DEV), BF),
            pltpu.VMEM((N_IDX, N_REQ - 1) + tile, BF),
            pltpu.VMEM((RING, N_REQ - 1, DEPTH, CTX_DEV), BF),
            (pltpu.VMEM((N_REQ,) + tile, BF),) * N_IDX
            + (pltpu.VMEM((N_REQ, DEPTH, CTX_DEV), BF),) * N_LAT,
            pltpu.VMEM((SIDE, SIDE, BATCH, QROWS, QW), BF),
            pltpu.VMEM((SIDE, SIDE, 16, 128), F32),
            pltpu.VMEM((SIDE * SIDE // 2 * QROWS, IDIM), BF),
            pltpu.VMEM((2, LAT, CTX_DEV), BF),
            pltpu.VMEM((RES, CTX_DEV, IDIM), BF),
            pltpu.VMEM((NEW, LAT, CTX_DEV), BF),
            pltpu.VMEM((NEW, PG_LOC, PAGE, IDIM), BF),
            pltpu.VMEM((SIDE, SIDE, BATCH, QROWS, KV), BF),
            pltpu.VMEM((n_groups, 16, SIDE * 128), F32),
            pltpu.VMEM((2, SIDE - 1, SIDE, BATCH, QROWS, 256), BF),
            pltpu.VMEM((n_groups, 2, SIDE - 1, 16, SIDE * 128), F32),
            pltpu.VMEM((2, SIDE, BATCH, QROWS, 256), BF),
            pltpu.VMEM((n_groups, 2, 16, SIDE * 128), F32),
            pltpu.VMEM((2, SIDE - 1, BATCH, QROWS, 256), BF),
            pltpu.VMEM((n_groups, 2, SIDE - 1, 16, 128), F32),
            pltpu.VMEM((SIDE, 8, SIDE * 128), F32),
            dma((N_CH, 3)), dma((N_CH, 3)), dma((N_CH, 3)), dma((N_CH, 3)),
            dma((N_CH, N_REQ - 1)), dma((N_CH, N_REQ - 1)),
            dma((N_CH,)), dma((N_CH,)), dma((N_XF,)), dma((5,)), dma((2,)), dma((RES,)),
            dma((2, 2, 2, 2)), dma((2, 2, 2, 2)), dma((2, 3)), dma((2, 3)),
            dma((n_groups, 2, 2, 2, 3)), dma((n_groups, 2, 2, 2, 3)),
        ],
        compiler_params=pltpu.CompilerParams(
            collective_id=0, has_side_effects=True, vmem_limit_bytes=63 * 2**20
        ),
        name="decode_step",
    )(*operands)


def body(
    res_latent, res_index, res_len, arrive_latent, arrive_index, arrive_len, destination,
    q_nope, q_rope, w_uk, w_uv, idx_query, idx_weight, selected,
):
    weights = jnp.concatenate([idx_weight, idx_weight], axis=2).astype(F32)
    weights = weights.transpose(1, 0, 2).reshape(BATCH, QROWS)
    weights = jnp.pad(weights, ((0, 16 - BATCH), (0, 128 - QROWS)))

    new_latent, new_index, index_scores, latent, _, _ = run_kernel(
        destination, arrive_len, res_len,
        arrive_latent.transpose(0, 2, 1), arrive_index.reshape(NEW, SIDE, SIDE, PAGE, IDIM),
        weights, res_latent[:, 0].transpose(0, 2, 1), res_index[:, 0], w_uk,
        q_nope, q_rope, idx_query, selected.transpose(1, 0, 2),
    )

    latent = latent.reshape(BATCH, STEPS, HEADS_DEV, KV)
    head_out = jnp.einsum("bshc,hcd->sbhd", latent, w_uv, preferred_element_type=F32).astype(BF)
    return (
        new_latent.transpose(0, 2, 1).reshape(NEW, 1, CTX_DEV, LAT),
        new_index.reshape(NEW, 1, CTX_DEV, IDIM),
        index_scores,
        head_out,
    )


def solution(mesh):
    placed = (
        P("req", "pos", None, None),
        P("req", "pos", None, None),
        P("req"),
        P("req", "pos", None),
        P("req", "pos", None),
        P(),
        P(),
        P(None, "req", "pos", None),
        P(None, "req", "pos", None),
        P("pos", None, None),
        P("pos", None, None),
        P(None, "req", "pos", None),
        P(None, "req", "pos"),
        P(None, "req", None),
    )
    return jax.shard_map(
        body,
        mesh=mesh,
        in_specs=placed,
        out_specs=(
            P("req", "pos", None, None),
            P("req", "pos", None, None),
            P(None, "req", "pos", None),
            P(None, "req", "pos", None),
        ),
        check_vma=False,
    )
```

```python
import jax
import jax.numpy as jnp
from jax import lax
from jax.experimental import pallas as pl
from jax.experimental.pallas import tpu as pltpu
from jax.sharding import PartitionSpec as P

KV, ROPE, NOPE, IDIM, PAGE = 512, 64, 128, 128, 64
LAT = KV + ROPE
STEPS, RES, NEW, BATCH, HEADS_DEV = 4, 6, 4, 10, 8
CTX_DEV, PG_LOC, N_REQ, SIDE = 1024, 16, 8, 4
QW = 640
HALF = PAGE // 2
QROWS = STEPS * HEADS_DEV
BF, F32 = jnp.bfloat16, jnp.float32
MESH = pl.DeviceIdType.MESH
SCALE = (NOPE + ROPE) ** (-0.5)

N_IDX, N_LAT, DEPTH = 2, LAT // 64, 64
N_CH = N_IDX + N_LAT
N_XF = (N_LAT + 1) // 2
RING = 4
GROUPS = ((0, 3), (6, 1), (7, 1), (8, 1), (9, 1), (3, 3))
STAT_ROWS = (8, 8, 8, 8, 8, 8)


def kernel(
    destination, arrive_len, res_len, lat, idx, wown, reslat, residx, w_uk, q_nope, q_rope, idx_query, selected,
    out_lat, out_idx, out_is, out_latent, a_idx, a_lat,
    qown, w_buf, live, idx_in, w_idx, ay_bufs, b_idx, b_lat, loads, pack_x, pack_y, unpacked, zs_idx, zs_lat, zrecvs, q_all, w_all, iq_buf, kbuf, ki_res, kfin, kifin, numer, stats,
    ra, rsa, nb_buf, stb, rb, rsb, fbuf,
    sa_s, sa_r, sb_s, sb_r, sz_s, sz_r, own_a, own_b, lat_sem, load_sem, out_sem, kb_sem,
    ag_s, ag_r, aw_s, aw_r, rs_s, rs_r,
):
    req = lax.axis_index("req")
    pos = lax.axis_index("pos")
    y, x = pos // SIDE, pos % SIDE

    def along(axis, delta):
        if axis == 0:
            return (req, y * SIDE + (x + delta) % SIDE)
        return (req, ((y + delta) % SIDE) * SIDE + x)

    def mine(axis):
        return x if axis == 0 else y

    def remote(src, dst, send, recv, target):
        return pltpu.make_async_remote_copy(
            src_ref=src, dst_ref=dst, send_sem=send, recv_sem=recv,
            device_id=target, device_id_type=MESH,
        )

    def chosen(group):
        k = jnp.int32(0)
        for n in range(1, NEW):
            k = jnp.maximum(k, jnp.where(destination[req * NEW + n] == group, n, 0))
        return k

    def source(k):
        s = jnp.int32(0)
        for n in range(1, N_REQ):
            s = jnp.maximum(s, jnp.where(destination[n * NEW + k] == req, n, 0))
        return s

    sources = [source(k) for k in range(NEW)]
    limits = [arrive_len[sources[k] * NEW + k] for k in range(NEW)]

    load_idx = pltpu.make_async_copy(idx, idx_in, load_sem.at[3])
    load_idx.start()
    barrier = pltpu.get_barrier_semaphore()
    for delta in range(1, N_REQ):
        pl.semaphore_signal(barrier, 1, device_id=((req + delta) % N_REQ, pos), device_id_type=MESH)
    for axis in range(2):
        for delta in range(1, SIDE):
            pl.semaphore_signal(barrier, 1, device_id=along(axis, delta), device_id_type=MESH)
    pl.semaphore_wait(barrier, N_REQ - 1 + 2 * (SIDE - 1))

    def first_axis(i):
        return i % 2

    def depth(i):
        return pl.ds((i - N_IDX) * DEPTH, DEPTH)

    def load_lat(i):
        n = (i - N_IDX) // 2
        return pltpu.make_async_copy(lat.at[:, depth(i)], loads.at[n % 2], lat_sem.at[n])

    def a_slot(i):
        if i < N_IDX:
            return a_idx.at[i]
        return a_lat.at[(i - N_IDX) // 2] if first_axis(i) == 0 else ay_bufs[(i - N_IDX) // 2]

    def a_source(i, coord):
        if i < N_IDX:
            return w_idx.at[i, :, :, coord] if first_axis(i) == 0 else w_idx.at[i, :, coord]
        if first_axis(i) == 0:
            return pack_x.at[(i - N_IDX) // 2 % 2, coord]
        return lat.at[:, depth(i), pl.ds(pl.multiple_of(coord * 256, 256), 256)]

    def b_slot(i):
        return b_idx[i] if i < N_IDX else b_lat[i - N_IDX]

    def b_source(i, coord):
        if i >= N_IDX and first_axis(i) == 1:
            return pack_y.at[(i - N_IDX) // 2 % 2, coord]
        return a_slot(i).at[:, :, coord]

    def copies_a(i):
        axis = first_axis(i)
        return [
            remote(
                a_source(i, (mine(axis) + delta) % SIDE), a_slot(i).at[mine(axis)],
                sa_s.at[i, delta - 1], sa_r.at[i, delta - 1], along(axis, delta),
            )
            for delta in range(1, SIDE)
        ]

    def own_copy_a(i):
        coord = mine(first_axis(i))
        return pltpu.make_async_copy(a_source(i, coord), a_slot(i).at[coord], own_a.at[i])

    def copies_b(i):
        axis = 1 - first_axis(i)
        return [
            remote(
                b_source(i, (mine(axis) + delta) % SIDE), b_slot(i).at[mine(axis)],
                sb_s.at[i, delta - 1], sb_r.at[i, delta - 1], along(axis, delta),
            )
            for delta in range(1, SIDE)
        ]

    def own_copy_b(i):
        coord = mine(1 - first_axis(i))
        return pltpu.make_async_copy(b_source(i, coord), b_slot(i).at[coord], own_b.at[i])

    def z_send(i):
        return zs_idx.at[i] if i < N_IDX else zs_lat.at[(i - N_IDX) % RING]

    def copy_z(i, delta):
        return remote(
            z_send(i).at[delta - 1], zrecvs[i].at[req],
            sz_s.at[i, delta - 1], sz_r.at[i, delta - 1], ((req + delta) % N_REQ, pos),
        )

    sent = set()

    def drain(kind, i):
        if (kind, i) in sent:
            return
        sent.add((kind, i))
        copies = {"a": copies_a, "b": copies_b}.get(kind)
        if copies is None:
            copies = lambda n: [copy_z(n, delta) for delta in range(1, N_REQ)]
        for copy in copies(i):
            copy.wait_send()

    low = lax.broadcasted_iota(jnp.int32, (DEPTH, 128), 1) < PAGE

    def swapped(first, second):
        first, second = first.astype(F32), second.astype(F32)
        lows = jnp.where(low, first, pltpu.roll(second, PAGE, 1))
        highs = jnp.where(low, pltpu.roll(first, PAGE, 1), second)
        return lows.astype(BF), highs.astype(BF)

    def lane_tile(n):
        return pl.ds(pl.multiple_of(n * 128, 128), 128)

    def start_a(i):
        if i >= N_IDX and first_axis(i) == 0:
            n = (i - N_IDX) // 2
            load_lat(i).wait()
            if n >= 2:
                drain("a", i - 4)

            def pack(row, carry):
                for pair in range(2):
                    for kp in range(2):
                        tile = lane_tile(row * 2 + pair)
                        lows, highs = swapped(
                            loads[n % 2, 2 * kp, :, tile], loads[n % 2, 2 * kp + 1, :, tile]
                        )
                        pack_x[n % 2, 2 * pair, kp, row] = lows
                        pack_x[n % 2, 2 * pair + 1, kp, row] = highs
                return carry

            lax.fori_loop(0, SIDE, pack, 0)
            if i + 4 < N_CH:
                load_lat(i + 4).start()
        own_copy_a(i).start()
        for copy in copies_a(i):
            copy.start()

    def a_to_b(i):
        own_copy_a(i).wait()
        for copy in copies_a(i):
            copy.wait_recv()
        if i >= N_IDX and first_axis(i) == 1:
            n = (i - N_IDX) // 2
            if n >= 2:
                drain("b", i - 4)

            def pack(row, carry):
                for pair in range(2):
                    tile = slice(pair * 128, (pair + 1) * 128)
                    for kp in range(2):
                        lows, highs = swapped(
                            ay_bufs[n][row, 2 * kp, :, tile], ay_bufs[n][row, 2 * kp + 1, :, tile]
                        )
                        pack_y[n % 2, 2 * pair, row, kp] = lows
                        pack_y[n % 2, 2 * pair + 1, row, kp] = highs
                return carry

            lax.fori_loop(0, SIDE, pack, 0)
        for copy in copies_b(i):
            copy.start()
        own_copy_b(i).start()

    def stage_z(i, block):
        def stage(delta, carry):
            z_send(i)[delta - 1] = block(chosen((req + delta) % N_REQ))
            copy_z(i, delta).start()
            return carry

        lax.fori_loop(1, N_REQ, stage, 0)
        zrecvs[i][req] = block(chosen(req))

    def index_to_z(i):
        stage_z(i, lambda k: idx_in[k, :, :, i * HALF : (i + 1) * HALF])

    def index_to_a(i):
        for k in range(NEW):
            w_idx[i, k] = zrecvs[i][sources[k]]
        start_a(i)

    def b_to_z(i):
        own_copy_b(i).wait()
        for copy in copies_b(i):
            copy.wait_recv()
        if i >= N_IDX + RING:
            drain("z", i - RING)
        buf = b_slot(i)

        def unpack(row, carry):
            for pair in range(2):
                for kp in range(2):
                    if first_axis(i) == 0:
                        even, odd = buf[row, 2 * pair, kp], buf[row, 2 * pair + 1, kp]
                    else:
                        even, odd = buf[2 * pair, row, kp], buf[2 * pair + 1, row, kp]
                    lows, highs = swapped(even, odd)
                    unpacked[2 * kp, :, lane_tile(row * 2 + pair)] = lows
                    unpacked[2 * kp + 1, :, lane_tile(row * 2 + pair)] = highs
            return carry

        lax.fori_loop(0, SIDE, unpack, 0)

        def block(k):
            return unpacked[k]

        stage_z(i, block)

    def wait_z(i):
        for delta in range(1, N_REQ):
            copy_z(i, delta).wait_recv()

    def out_copies(kind):
        if kind == "idx":
            return pltpu.make_async_copy(kifin, out_idx, out_sem.at[0])
        return pltpu.make_async_copy(kfin, out_lat, out_sem.at[1])

    def finalize_idx(i):
        own_copy_b(i).wait()
        for copy in copies_b(i):
            copy.wait_recv()

        def page(n, carry):
            outer, inner = n // SIDE, n % SIDE
            l = outer * SIDE + inner if first_axis(i) == 0 else inner * SIDE + outer
            base = (l * (SIDE * SIDE) + pos) * PAGE + i * HALF
            row = lax.broadcasted_iota(jnp.int32, (HALF, 128), 0)
            for k in range(NEW):
                tile = b_idx[i][outer, inner, k].astype(F32)
                value = jnp.where(row + base < limits[k], tile, 0.0).astype(BF)
                kifin[k, l, i * HALF : (i + 1) * HALF, :] = value
            return carry

        lax.fori_loop(0, SIDE * SIDE, page, 0)

    def finalize(i):
        def tiles(n, carry):
            lane = lax.broadcasted_iota(jnp.int32, (DEPTH, 128), 1)
            logical = (2 * n + lane // PAGE) * (SIDE * SIDE * PAGE) + pos * PAGE + lane % PAGE
            for k in range(NEW):
                tile = zrecvs[i][sources[k], :, lane_tile(n)].astype(F32)
                value = jnp.where(logical < limits[k], tile, 0.0).astype(BF)
                kfin[k, depth(i), lane_tile(n)] = value
            return carry

        lax.fori_loop(0, CTX_DEV // 128, tiles, 0)

    spans = (pl.ds(0, BATCH // 2), pl.ds(BATCH // 2, BATCH // 2))

    def gather_views(phase, way):
        if phase == 0:
            return (qown.at[spans[way]], q_all.at[y, x, spans[way]])
        if way == 0:
            block = q_all.at[y, :, spans[way]]
        else:
            block = q_all.at[:, x, spans[way]]
        return (block, block)

    def gather_near(phase):
        copies = []
        for way in range(2):
            axis = way if phase == 0 else 1 - way
            src, dst = gather_views(phase, way)
            for n, delta in enumerate((1, SIDE - 1)):
                at = (phase, way, 0, n)
                copies.append(remote(src, dst, ag_s.at[at], ag_r.at[at], along(axis, delta)))
        return copies

    def gather_far(phase):
        copies = []
        for way in range(2):
            axis = way if phase == 0 else 1 - way
            for n, delta in enumerate((1, SIDE - 1)):
                rows = pl.ds(n * (QROWS // 2), QROWS // 2)
                fx = (x - delta) % SIDE if axis == 0 else x
                fy = (y - delta) % SIDE if axis == 1 else y
                if phase == 0:
                    block = q_all.at[fy, fx, spans[way], rows]
                elif way == 0:
                    block = q_all.at[fy, :, spans[way], rows]
                else:
                    block = q_all.at[:, fx, spans[way], rows]
                at = (phase, way, 1, n)
                copies.append(remote(block, block, ag_s.at[at], ag_r.at[at], along(axis, delta)))
        return copies

    def weight_copies(phase):
        axis = phase
        block = w_all.at[y, x] if phase == 0 else w_all.at[y]
        return [
            remote(
                wown if phase == 0 else block, block, aw_s.at[phase, delta - 1],
                aw_r.at[phase, delta - 1], along(axis, delta),
            )
            for delta in range(1, SIDE)
        ]

    own_q = pltpu.make_async_copy(qown, q_all.at[y, x], load_sem.at[0])
    own_w = pltpu.make_async_copy(wown, w_all.at[y, x], load_sem.at[1])
    load_w = pltpu.make_async_copy(w_uk, w_buf, load_sem.at[4])
    load_ki = pltpu.make_async_copy(residx, ki_res, load_sem.at[2])

    def load_k(b):
        return pltpu.make_async_copy(reslat.at[b], kbuf.at[b % 2], kb_sem.at[b])

    def absorb():
        rows = BATCH * HEADS_DEV
        head = lax.broadcasted_iota(jnp.int32, (rows, KV), 0) % HEADS_DEV
        for pair in range(STEPS // 2):
            blocks = []
            for t in (2 * pair, 2 * pair + 1):
                q = q_nope[t].reshape(rows, NOPE)
                total = jnp.zeros((rows, KV), F32)
                for h in range(HEADS_DEV):
                    part = jnp.dot(q, w_buf[h], preferred_element_type=F32)
                    total = jnp.where(head == h, part, total)
                keys = idx_query[t].astype(F32)
                halves = jnp.concatenate([keys[..., :ROPE], keys[..., ROPE:]], axis=1)
                tail = jnp.concatenate([q_rope[t].astype(F32), halves], axis=2)
                blocks.append(
                    jnp.concatenate([total.reshape(BATCH, HEADS_DEV, KV), tail], axis=2)
                )
            block = jnp.concatenate(blocks, axis=1).astype(BF)
            qown[:, pair * 16 : (pair + 1) * 16, :] = block

    def find_live(b):
        page = lax.broadcasted_iota(jnp.int32, (STEPS, CTX_DEV), 1) // PAGE * (SIDE * SIDE) + pos
        wanted = selected[b]
        found = wanted[:, 0:1] == page
        for n in range(1, wanted.shape[1]):
            found = found | (wanted[:, n : n + 1] == page)
        bias = jnp.where(found, 0.0, -1e30)
        for t in range(STEPS):
            live[t * HEADS_DEV : (t + 1) * HEADS_DEV, :] = jnp.broadcast_to(
                bias[t : t + 1], (HEADS_DEV, CTX_DEV)
            )

    def as_row(column):
        size = column.shape[0]
        row = lax.broadcasted_iota(jnp.int32, (size, size), 0)
        lane = lax.broadcasted_iota(jnp.int32, (size, size), 1)
        return jnp.sum(jnp.where(row == lane, column, 0.0), axis=0, keepdims=True)

    def as_column(values, first):
        row = lax.broadcasted_iota(jnp.int32, (QROWS, 128), 0)
        lane = lax.broadcasted_iota(jnp.int32, (QROWS, 128), 1)
        return jnp.sum(jnp.where(lane == row + first, values, 0.0), axis=1, keepdims=True)

    def attend(b, g, keys):
        b0, half = GROUPS[g][0], STAT_ROWS[g] // 2
        find_live(b)

        def part(n, carry):
            q = q_all[pl.ds(2 * n, 2), :, b, :, 0:LAT].reshape(2 * SIDE * QROWS, LAT)
            k = keys()
            s = jnp.dot(q, k, preferred_element_type=F32)
            s = (s * SCALE).reshape(2 * SIDE, QROWS, CTX_DEV) + live[...][None]
            s = s.reshape(2 * SIDE * QROWS, CTX_DEV)
            top = jnp.maximum(jnp.max(s, axis=1, keepdims=True), -1e29)
            e = jnp.exp(s - top)
            total = jnp.sum(e, axis=1, keepdims=True)
            o = lax.dot_general(
                e.astype(BF), k[:KV], (((1,), (1,)), ((), ())), preferred_element_type=F32
            )
            numer[pl.ds(2 * n, 2), :, b] = o.astype(BF).reshape(2, SIDE, QROWS, KV)
            cols = pl.ds(pl.multiple_of(n * 256, 256), 256)
            stats[g, b - b0 : b - b0 + 1, cols] = as_row(top)
            stats[g, b - b0 + half : b - b0 + half + 1, cols] = as_row(total)
            return carry

        lax.fori_loop(0, 2, part, 0)

    def index_scores(b, length, keys):
        shape = (SIDE * SIDE // 2, STEPS, HEADS_DEV, 128)
        both = q_all[:, :, b, :, KV:QW].astype(F32).reshape((SIDE * SIDE // 2, 2) + shape[1:])
        even, odd = both[:, 0].reshape(-1, 8, 128), both[:, 1].reshape(-1, 8, 128)
        row = lax.broadcasted_iota(jnp.int32, even.shape, 1)
        lane = lax.broadcasted_iota(jnp.int32, even.shape, 2)
        upper = jnp.where(lane < ROPE, pltpu.roll(even, ROPE, 2), pltpu.roll(even, 4, 1))
        lower = jnp.where(lane < ROPE, pltpu.roll(pltpu.roll(odd, ROPE, 2), 4, 1), odd)
        iq_buf[...] = jnp.where(row < 4, upper, lower).reshape(-1, 128).astype(BF)
        high = lax.broadcasted_iota(jnp.int32, (QROWS, 128), 0) % 8 < 4
        weights = []
        for pair in range(SIDE * SIDE // 2):
            w_even = w_all[pair // 2, 2 * (pair % 2), b : b + 1]
            w_odd = w_all[pair // 2, 2 * (pair % 2) + 1, b : b + 1]
            weights.append(as_column(jnp.where(high, w_even, w_odd), 0))
        weight = jnp.concatenate(weights, axis=0)

        def part(n, carry):
            k = keys(n)
            logits = lax.dot_general(
                iq_buf[...], k, (((1,), (1,)), ((), ())), preferred_element_type=F32
            )
            value = jnp.maximum(logits, 0.0) * weight
            cols = pl.ds(pl.multiple_of(n * 256, 256), 256)
            value = jnp.sum(value.reshape(SIDE * SIDE // 2, QROWS, 256), axis=0)
            value = jnp.sum(value.reshape(STEPS, HEADS_DEV, 256), axis=1) * IDIM ** (-0.5)
            lane = lax.broadcasted_iota(jnp.int32, (STEPS, 256), 1) + n * 256
            logical = lane // PAGE * (SIDE * SIDE * PAGE) + pos * PAGE + lane % PAGE
            value = jnp.where(logical < length, value, 0.0)
            for t in range(STEPS):
                out_is[t, b, :, cols] = value[t : t + 1]
            return carry

        lax.fori_loop(0, CTX_DEV // 256, part, 0)

    def attend_res(b):
        load_k(b).wait()
        attend(b, 0 if b < 3 else 5, lambda: kbuf[b % 2])
        if b + 2 < RES:
            load_k(b + 2).start()

    def attend_new(k, g):
        attend(RES + k, g, lambda: kfin[k])

    def index_res(b):
        index_scores(b, res_len[b], lambda n: ki_res[b, pl.ds(pl.multiple_of(n * 256, 256), 256)])

    def index_new(k):
        index_scores(RES + k, limits[k], lambda n: kifin[k, pl.ds(n * 4, 4)].reshape(256, IDIM))

    def lanes(way):
        return pl.ds(way * 256, 256)

    def reduce_copies(g, phase, way):
        b0, count = GROUPS[g]
        span, stat = pl.ds(b0, count), pl.ds(0, STAT_ROWS[g])
        axis = way if phase == 0 else 1 - way
        copies = []
        for delta in range(1, SIDE):
            other = (mine(axis) + delta) % SIDE
            to_y = other if axis == 1 else y
            tile = pl.ds(pl.multiple_of(to_y * 128, 128), 128)
            if phase == 0:
                src = numer.at[:, other, span, :, lanes(way)]
                src_st, dst_st = stats.at[g, stat], rsa.at[g, way, delta - 1, stat]
                if way == 1:
                    src = numer.at[other, :, span, :, lanes(way)]
                    src_st = stats.at[g, stat, tile]
                    dst_st = rsa.at[g, way, delta - 1, stat, pl.ds(0, 128)]
                dst = ra.at[way, delta - 1, :, span]
            else:
                src, src_st = nb_buf.at[way, other, span], stb.at[g, way, stat, tile]
                dst, dst_st = rb.at[way, delta - 1, span], rsb.at[g, way, delta - 1, stat]
            target = along(axis, delta)
            for which, (s, d) in enumerate(((src, dst), (src_st, dst_st))):
                at = (g, phase, way, which, delta - 1)
                copies.append(remote(s, d, rs_s.at[at], rs_r.at[at], target))
        return copies

    def start_reduce(g, phase, way):
        for copy in reduce_copies(g, phase, way):
            copy.start()

    def merged(g, blocks):
        half = STAT_ROWS[g] // 2
        tops = [block[:half] for block in blocks]
        top = tops[0]
        for value in tops[1:]:
            top = jnp.maximum(top, value)
        factors = [jnp.exp(value - top) for value in tops]
        total = factors[0] * blocks[0][half:]
        for factor, block in zip(factors[1:], blocks[1:]):
            total = total + factor * block[half:]
        return top, factors, total

    def combine_a(g, way):
        b0, count = GROUPS[g]
        half = STAT_ROWS[g] // 2
        stat = slice(0, STAT_ROWS[g])
        for copy in reduce_copies(g, 0, way):
            copy.wait_recv()
        if way == 0:
            blocks = [stats[g, stat]] + [rsa[g, way, d, stat] for d in range(SIDE - 1)]
            cols = slice(0, SIDE * 128)
        else:
            blocks = [stats[g, stat, pl.ds(pl.multiple_of(y * 128, 128), 128)]]
            blocks += [rsa[g, way, d, stat, 0:128] for d in range(SIDE - 1)]
            cols = pl.ds(pl.multiple_of(y * 128, 128), 128)
        top, factors, total = merged(g, blocks)
        stb[g, way, 0:half, cols] = top
        stb[g, way, half : 2 * half, cols] = total
        for d in range(SIDE):
            fbuf[d, 0:half, cols] = factors[d]

        def block(j, carry):
            tile = pl.ds(pl.multiple_of((j if way == 0 else y) * 128, 128), 128)
            first = (x if way == 0 else j) * QROWS
            for n in range(count):
                if way == 0:
                    own = numer[j, x, b0 + n, :, 0:256]
                else:
                    own = numer[y, j, b0 + n, :, 256:512]
                acc = own.astype(F32) * as_column(fbuf[0, n : n + 1, tile], first)
                for d in range(SIDE - 1):
                    factor = as_column(fbuf[d + 1, n : n + 1, tile], first)
                    acc = acc + ra[way, d, j, b0 + n].astype(F32) * factor
                nb_buf[way, j, b0 + n] = acc.astype(BF)
            return carry

        lax.fori_loop(0, SIDE, block, 0)
        start_reduce(g, 1, way)

    def combine_b(g, way):
        b0, count = GROUPS[g]
        stat = slice(0, STAT_ROWS[g])
        for copy in reduce_copies(g, 1, way):
            copy.wait_recv()
        here = mine(1 - way)
        blocks = [stb[g, way, stat, pl.ds(pl.multiple_of(y * 128, 128), 128)]]
        blocks += [rsb[g, way, d, stat] for d in range(SIDE - 1)]
        _, factors, total = merged(g, blocks)
        factors = [factor / total for factor in factors]
        for n in range(count):
            acc = nb_buf[way, here, b0 + n].astype(F32) * as_column(factors[0][n : n + 1], x * QROWS)
            for d in range(SIDE - 1):
                factor = as_column(factors[d + 1][n : n + 1], x * QROWS)
                acc = acc + rb[way, d, b0 + n].astype(F32) * factor
            out_latent[b0 + n, :, way * 256 : (way + 1) * 256] = acc.astype(BF)

    def start(copies):
        for copy in copies:
            copy.start()

    def arrived(copies):
        for copy in copies:
            copy.wait_recv()

    load_lat(N_IDX).start()
    load_lat(N_IDX + 2).start()
    load_w.start()
    own_w.start()
    load_idx.wait()
    index_to_z(0)
    index_to_z(1)
    start_a(2)
    start_a(3)
    load_ki.start()
    load_k(0).start()
    load_k(1).start()
    stats[...] = jnp.zeros_like(stats)
    start_a(4)
    a_to_b(2)
    a_to_b(3)
    load_w.wait()
    absorb()
    own_q.start()
    start(gather_near(0) + weight_copies(0))
    start_a(5)
    b_to_z(2)
    a_to_b(4)
    own_q.wait()
    own_w.wait()
    arrived(gather_near(0) + weight_copies(0))
    start(gather_far(0) + weight_copies(1))
    start_a(6)
    a_to_b(5)
    start_a(7)
    b_to_z(3)
    b_to_z(4)

    for i in range(N_CH):
        wait_z(i)
        if 0 < i < N_CH - 4:
            b_to_z(i + 4)
        if i + 6 < N_CH:
            a_to_b(i + 6)
        if i + 8 < N_CH:
            start_a(i + 8)
        if i < N_IDX:
            index_to_a(i)
        else:
            finalize(i)
        if i == 0:
            arrived(gather_far(0))
            start(gather_near(1))
        elif i == 2:
            arrived(gather_near(1))
            start(gather_far(1))
            a_to_b(0)
        elif i == 3:
            a_to_b(1)
        elif i == 4:
            arrived(gather_far(1) + weight_copies(1))
            attend_res(0)
            attend_res(1)
        elif i == 5:
            attend_res(2)
            for way in range(2):
                start_reduce(0, 0, way)
            attend_res(3)
        elif i == 6:
            attend_res(4)
            attend_res(5)
            for way in range(2):
                start_reduce(5, 0, way)
            load_ki.wait()
            index_res(0)
        elif i == 7:
            for way in range(2):
                combine_a(0, way)
            index_res(1)
            index_res(2)
            finalize_idx(0)
            finalize_idx(1)
            out_copies("idx").start()
        elif i == 8:
            for way in range(2):
                combine_a(5, way)
            index_res(3)
            index_res(4)
        elif i == 9:
            index_res(5)
            index_new(0)
            for way in range(2):
                combine_b(0, way)
            index_new(1)
            for way in range(2):
                combine_b(5, way)
    out_copies("lat").start()
    for k in range(NEW):
        attend_new(k, k + 1)
        for way in range(2):
            start_reduce(k + 1, 0, way)
    index_new(2)
    for way in range(2):
        combine_a(1, way)
    index_new(3)
    for g in (2, 3, 4):
        for way in range(2):
            combine_a(g, way)
    for g in (1, 2, 3, 4):
        for way in range(2):
            combine_b(g, way)

    for i in range(N_CH):
        for kind in ("a", "b", "z"):
            drain(kind, i)
    for phase in range(2):
        for copy in gather_near(phase) + gather_far(phase) + weight_copies(phase):
            copy.wait_send()
        for g in range(len(GROUPS)):
            for way in range(2):
                for copy in reduce_copies(g, phase, way):
                    copy.wait_send()
    out_copies("idx").wait()
    out_copies("lat").wait()


def run_kernel(*operands):
    smem = pl.BlockSpec(memory_space=pltpu.SMEM)
    vmem = pl.BlockSpec(memory_space=pltpu.VMEM)
    hbm = pl.BlockSpec(memory_space=pl.ANY)
    dma = pltpu.SemaphoreType.DMA
    n_groups = len(GROUPS)
    tile = (SIDE, SIDE, HALF, 128)
    return pl.pallas_call(
        kernel,
        out_shape=(
            jax.ShapeDtypeStruct((NEW, LAT, CTX_DEV), BF),
            jax.ShapeDtypeStruct((NEW, PG_LOC, PAGE, IDIM), BF),
            jax.ShapeDtypeStruct((STEPS, BATCH, 1, CTX_DEV), F32),
            jax.ShapeDtypeStruct((BATCH, QROWS, KV), BF),
            jax.ShapeDtypeStruct((N_IDX, SIDE, NEW, SIDE, HALF, 128), BF),
            jax.ShapeDtypeStruct((N_XF, SIDE, 2, SIDE, DEPTH, 128), BF),
        ),
        in_specs=[smem] * 3 + [hbm] * 6 + [vmem] * 4,
        out_specs=(hbm, hbm, vmem, vmem, hbm, hbm),
        scratch_shapes=[
            pltpu.VMEM((BATCH, QROWS, QW), BF),
            pltpu.VMEM((HEADS_DEV, NOPE, KV), BF),
            pltpu.VMEM((QROWS, CTX_DEV), F32),
            pltpu.VMEM((NEW, SIDE, SIDE, PAGE, IDIM), BF),
            pltpu.VMEM((N_IDX, NEW) + tile, BF),
            (pltpu.VMEM((SIDE, NEW, DEPTH, 256), BF),) * (N_LAT - N_XF),
            (pltpu.VMEM((SIDE, SIDE, NEW, HALF, 128), BF),) * N_IDX,
            (pltpu.VMEM((SIDE, SIDE, 2, DEPTH, 128), BF),) * N_LAT,
            pltpu.VMEM((2, NEW, DEPTH, CTX_DEV), BF),
            pltpu.VMEM((2, SIDE, 2, SIDE, DEPTH, 128), BF),
            pltpu.VMEM((2, SIDE, SIDE, 2, DEPTH, 128), BF),
            pltpu.VMEM((NEW, DEPTH, CTX_DEV), BF),
            pltpu.VMEM((N_IDX, N_REQ - 1) + tile, BF),
            pltpu.VMEM((RING, N_REQ - 1, DEPTH, CTX_DEV), BF),
            (pltpu.VMEM((N_REQ,) + tile, BF),) * N_IDX
            + (pltpu.VMEM((N_REQ, DEPTH, CTX_DEV), BF),) * N_LAT,
            pltpu.VMEM((SIDE, SIDE, BATCH, QROWS, QW), BF),
            pltpu.VMEM((SIDE, SIDE, 16, 128), F32),
            pltpu.VMEM((SIDE * SIDE // 2 * QROWS, IDIM), BF),
            pltpu.VMEM((2, LAT, CTX_DEV), BF),
            pltpu.VMEM((RES, CTX_DEV, IDIM), BF),
            pltpu.VMEM((NEW, LAT, CTX_DEV), BF),
            pltpu.VMEM((NEW, PG_LOC, PAGE, IDIM), BF),
            pltpu.VMEM((SIDE, SIDE, BATCH, QROWS, KV), BF),
            pltpu.VMEM((n_groups, 16, SIDE * 128), F32),
            pltpu.VMEM((2, SIDE - 1, SIDE, BATCH, QROWS, 256), BF),
            pltpu.VMEM((n_groups, 2, SIDE - 1, 16, SIDE * 128), F32),
            pltpu.VMEM((2, SIDE, BATCH, QROWS, 256), BF),
            pltpu.VMEM((n_groups, 2, 16, SIDE * 128), F32),
            pltpu.VMEM((2, SIDE - 1, BATCH, QROWS, 256), BF),
            pltpu.VMEM((n_groups, 2, SIDE - 1, 16, 128), F32),
            pltpu.VMEM((SIDE, 8, SIDE * 128), F32),
            dma((N_CH, 3)), dma((N_CH, 3)), dma((N_CH, 3)), dma((N_CH, 3)),
            dma((N_CH, N_REQ - 1)), dma((N_CH, N_REQ - 1)),
            dma((N_CH,)), dma((N_CH,)), dma((N_XF,)), dma((5,)), dma((2,)), dma((RES,)),
            dma((2, 2, 2, 2)), dma((2, 2, 2, 2)), dma((2, 3)), dma((2, 3)),
            dma((n_groups, 2, 2, 2, 3)), dma((n_groups, 2, 2, 2, 3)),
        ],
        compiler_params=pltpu.CompilerParams(
            collective_id=0, has_side_effects=True, vmem_limit_bytes=63 * 2**20
        ),
        name="decode_step",
    )(*operands)


def body(
    res_latent, res_index, res_len, arrive_latent, arrive_index, arrive_len, destination,
    q_nope, q_rope, w_uk, w_uv, idx_query, idx_weight, selected,
):
    weights = jnp.concatenate([idx_weight, idx_weight], axis=2).astype(F32)
    weights = weights.transpose(1, 0, 2).reshape(BATCH, QROWS)
    weights = jnp.pad(weights, ((0, 16 - BATCH), (0, 128 - QROWS)))

    new_latent, new_index, index_scores, latent, _, _ = run_kernel(
        destination, arrive_len, res_len,
        arrive_latent.transpose(0, 2, 1), arrive_index.reshape(NEW, SIDE, SIDE, PAGE, IDIM),
        weights, res_latent[:, 0].transpose(0, 2, 1), res_index[:, 0], w_uk,
        q_nope, q_rope, idx_query, selected.transpose(1, 0, 2),
    )

    latent = latent.reshape(BATCH, STEPS, HEADS_DEV, KV)
    head_out = jnp.einsum("bshc,hcd->sbhd", latent, w_uv, preferred_element_type=F32).astype(BF)
    return (
        new_latent.transpose(0, 2, 1).reshape(NEW, 1, CTX_DEV, LAT),
        new_index.reshape(NEW, 1, CTX_DEV, IDIM),
        index_scores,
        head_out,
    )


def solution(mesh):
    placed = (
        P("req", "pos", None, None),
        P("req", "pos", None, None),
        P("req"),
        P("req", "pos", None),
        P("req", "pos", None),
        P(),
        P(),
        P(None, "req", "pos", None),
        P(None, "req", "pos", None),
        P("pos", None, None),
        P("pos", None, None),
        P(None, "req", "pos", None),
        P(None, "req", "pos"),
        P(None, "req", None),
    )
    return jax.shard_map(
        body,
        mesh=mesh,
        in_specs=placed,
        out_specs=(
            P("req", "pos", None, None),
            P("req", "pos", None, None),
            P(None, "req", "pos", None),
            P(None, "req", "pos", None),
        ),
        check_vma=False,
    )
```

```python
import jax
import jax.numpy as jnp
from jax import lax
from jax.experimental import pallas as pl
from jax.experimental.pallas import tpu as pltpu
from jax.sharding import PartitionSpec as P

KV, ROPE, NOPE, IDIM, PAGE = 512, 64, 128, 128, 64
LAT = KV + ROPE
STEPS, RES, NEW, BATCH, HEADS_DEV = 4, 6, 4, 10, 8
CTX_DEV, PG_LOC, N_REQ, SIDE = 1024, 16, 8, 4
QW = 640
HALF = PAGE // 2
QROWS = STEPS * HEADS_DEV
BF, F32 = jnp.bfloat16, jnp.float32
MESH = pl.DeviceIdType.MESH
SCALE = (NOPE + ROPE) ** (-0.5)

N_IDX, N_LAT, DEPTH = 2, LAT // 64, 64
N_CH = N_IDX + N_LAT
N_XF = (N_LAT + 1) // 2
RING = 4
GROUPS = ((0, 3), (6, 1), (7, 1), (8, 1), (9, 1), (3, 3))
STAT_ROWS = (8, 8, 8, 8, 8, 8)


def kernel(
    destination, arrive_len, res_len, lat, idx, wown, reslat, residx, w_uk, q_nope, q_rope, idx_query, selected,
    out_lat, out_idx, out_is, out_latent, a_idx, a_lat,
    qown, w_buf, live, idx_in, w_idx, ay_bufs, b_idx, b_lat, loads, pack_x, pack_y, unpacked, zs_idx, zs_lat, zrecvs, q_all, w_all, iq_buf, kbuf, ki_res, kfin, kifin, numer, stats,
    ra, rsa, nb_buf, stb, rb, rsb, fbuf,
    sa_s, sa_r, sb_s, sb_r, sz_s, sz_r, own_a, own_b, lat_sem, load_sem, out_sem, kb_sem,
    ag_s, ag_r, aw_s, aw_r, rs_s, rs_r,
):
    req = lax.axis_index("req")
    pos = lax.axis_index("pos")
    y, x = pos // SIDE, pos % SIDE

    def along(axis, delta):
        if axis == 0:
            return (req, y * SIDE + (x + delta) % SIDE)
        return (req, ((y + delta) % SIDE) * SIDE + x)

    def mine(axis):
        return x if axis == 0 else y

    def remote(src, dst, send, recv, target):
        return pltpu.make_async_remote_copy(
            src_ref=src, dst_ref=dst, send_sem=send, recv_sem=recv,
            device_id=target, device_id_type=MESH,
        )

    def chosen(group):
        k = jnp.int32(0)
        for n in range(1, NEW):
            k = jnp.maximum(k, jnp.where(destination[req * NEW + n] == group, n, 0))
        return k

    def source(k):
        s = jnp.int32(0)
        for n in range(1, N_REQ):
            s = jnp.maximum(s, jnp.where(destination[n * NEW + k] == req, n, 0))
        return s

    sources = [source(k) for k in range(NEW)]
    limits = [arrive_len[sources[k] * NEW + k] for k in range(NEW)]

    load_idx = pltpu.make_async_copy(idx, idx_in, load_sem.at[3])
    load_idx.start()
    barrier = pltpu.get_barrier_semaphore()
    for delta in range(1, N_REQ):
        pl.semaphore_signal(barrier, 1, device_id=((req + delta) % N_REQ, pos), device_id_type=MESH)
    for axis in range(2):
        for delta in range(1, SIDE):
            pl.semaphore_signal(barrier, 1, device_id=along(axis, delta), device_id_type=MESH)
    pl.semaphore_wait(barrier, N_REQ - 1 + 2 * (SIDE - 1))

    def first_axis(i):
        return i % 2

    def depth(i):
        return pl.ds((i - N_IDX) * DEPTH, DEPTH)

    def load_lat(i):
        n = (i - N_IDX) // 2
        return pltpu.make_async_copy(lat.at[:, depth(i)], loads.at[n % 2], lat_sem.at[n])

    def a_slot(i):
        if i < N_IDX:
            return a_idx.at[i]
        return a_lat.at[(i - N_IDX) // 2] if first_axis(i) == 0 else ay_bufs[(i - N_IDX) // 2]

    def a_source(i, coord):
        if i < N_IDX:
            return w_idx.at[i, :, :, coord] if first_axis(i) == 0 else w_idx.at[i, :, coord]
        if first_axis(i) == 0:
            return pack_x.at[(i - N_IDX) // 2 % 2, coord]
        return lat.at[:, depth(i), pl.ds(pl.multiple_of(coord * 256, 256), 256)]

    def b_slot(i):
        return b_idx[i] if i < N_IDX else b_lat[i - N_IDX]

    def b_source(i, coord):
        if i >= N_IDX and first_axis(i) == 1:
            return pack_y.at[(i - N_IDX) // 2 % 2, coord]
        return a_slot(i).at[:, :, coord]

    def copies_a(i):
        axis = first_axis(i)
        return [
            remote(
                a_source(i, (mine(axis) + delta) % SIDE), a_slot(i).at[mine(axis)],
                sa_s.at[i, delta - 1], sa_r.at[i, delta - 1], along(axis, delta),
            )
            for delta in range(1, SIDE)
        ]

    def own_copy_a(i):
        coord = mine(first_axis(i))
        return pltpu.make_async_copy(a_source(i, coord), a_slot(i).at[coord], own_a.at[i])

    def copies_b(i):
        axis = 1 - first_axis(i)
        return [
            remote(
                b_source(i, (mine(axis) + delta) % SIDE), b_slot(i).at[mine(axis)],
                sb_s.at[i, delta - 1], sb_r.at[i, delta - 1], along(axis, delta),
            )
            for delta in range(1, SIDE)
        ]

    def own_copy_b(i):
        coord = mine(1 - first_axis(i))
        return pltpu.make_async_copy(b_source(i, coord), b_slot(i).at[coord], own_b.at[i])

    def z_send(i):
        return zs_idx.at[i] if i < N_IDX else zs_lat.at[(i - N_IDX) % RING]

    def copy_z(i, delta):
        return remote(
            z_send(i).at[delta - 1], zrecvs[i].at[req],
            sz_s.at[i, delta - 1], sz_r.at[i, delta - 1], ((req + delta) % N_REQ, pos),
        )

    sent = set()

    def drain(kind, i):
        if (kind, i) in sent:
            return
        sent.add((kind, i))
        copies = {"a": copies_a, "b": copies_b}.get(kind)
        if copies is None:
            copies = lambda n: [copy_z(n, delta) for delta in range(1, N_REQ)]
        for copy in copies(i):
            copy.wait_send()

    low = lax.broadcasted_iota(jnp.int32, (DEPTH, 128), 1) < PAGE

    def swapped(first, second):
        first, second = first.astype(F32), second.astype(F32)
        lows = jnp.where(low, first, pltpu.roll(second, PAGE, 1))
        highs = jnp.where(low, pltpu.roll(first, PAGE, 1), second)
        return lows.astype(BF), highs.astype(BF)

    def lane_tile(n):
        return pl.ds(pl.multiple_of(n * 128, 128), 128)

    def start_a(i):
        if i >= N_IDX and first_axis(i) == 0:
            n = (i - N_IDX) // 2
            load_lat(i).wait()
            if n >= 2:
                drain("a", i - 4)

            def pack(row, carry):
                for pair in range(2):
                    for kp in range(2):
                        tile = lane_tile(row * 2 + pair)
                        lows, highs = swapped(
                            loads[n % 2, 2 * kp, :, tile], loads[n % 2, 2 * kp + 1, :, tile]
                        )
                        pack_x[n % 2, 2 * pair, kp, row] = lows
                        pack_x[n % 2, 2 * pair + 1, kp, row] = highs
                return carry

            lax.fori_loop(0, SIDE, pack, 0)
            if i + 4 < N_CH:
                load_lat(i + 4).start()
        own_copy_a(i).start()
        for copy in copies_a(i):
            copy.start()

    def a_to_b(i):
        own_copy_a(i).wait()
        for copy in copies_a(i):
            copy.wait_recv()
        if i >= N_IDX and first_axis(i) == 1:
            n = (i - N_IDX) // 2
            if n >= 2:
                drain("b", i - 4)

            def pack(row, carry):
                for pair in range(2):
                    tile = slice(pair * 128, (pair + 1) * 128)
                    for kp in range(2):
                        lows, highs = swapped(
                            ay_bufs[n][row, 2 * kp, :, tile], ay_bufs[n][row, 2 * kp + 1, :, tile]
                        )
                        pack_y[n % 2, 2 * pair, row, kp] = lows
                        pack_y[n % 2, 2 * pair + 1, row, kp] = highs
                return carry

            lax.fori_loop(0, SIDE, pack, 0)
        for copy in copies_b(i):
            copy.start()
        own_copy_b(i).start()

    def stage_z(i, block):
        def stage(delta, carry):
            z_send(i)[delta - 1] = block(chosen((req + delta) % N_REQ))
            copy_z(i, delta).start()
            return carry

        lax.fori_loop(1, N_REQ, stage, 0)
        zrecvs[i][req] = block(chosen(req))

    def index_to_z(i):
        stage_z(i, lambda k: idx_in[k, :, :, i * HALF : (i + 1) * HALF])

    def index_to_a(i):
        for k in range(NEW):
            w_idx[i, k] = zrecvs[i][sources[k]]
        start_a(i)

    def b_to_z(i):
        own_copy_b(i).wait()
        for copy in copies_b(i):
            copy.wait_recv()
        if i >= N_IDX + RING:
            drain("z", i - RING)
        buf = b_slot(i)

        def unpack(row, carry):
            for pair in range(2):
                for kp in range(2):
                    if first_axis(i) == 0:
                        even, odd = buf[row, 2 * pair, kp], buf[row, 2 * pair + 1, kp]
                    else:
                        even, odd = buf[2 * pair, row, kp], buf[2 * pair + 1, row, kp]
                    lows, highs = swapped(even, odd)
                    unpacked[2 * kp, :, lane_tile(row * 2 + pair)] = lows
                    unpacked[2 * kp + 1, :, lane_tile(row * 2 + pair)] = highs
            return carry

        lax.fori_loop(0, SIDE, unpack, 0)

        def block(k):
            return unpacked[k]

        stage_z(i, block)

    def wait_z(i):
        for delta in range(1, N_REQ):
            copy_z(i, delta).wait_recv()

    def out_copies(kind):
        if kind == "idx":
            return pltpu.make_async_copy(kifin, out_idx, out_sem.at[0])
        return pltpu.make_async_copy(kfin, out_lat, out_sem.at[1])

    def finalize_idx(i):
        own_copy_b(i).wait()
        for copy in copies_b(i):
            copy.wait_recv()

        def page(n, carry):
            outer, inner = n // SIDE, n % SIDE
            l = outer * SIDE + inner if first_axis(i) == 0 else inner * SIDE + outer
            base = (l * (SIDE * SIDE) + pos) * PAGE + i * HALF
            row = lax.broadcasted_iota(jnp.int32, (HALF, 128), 0)
            for k in range(NEW):
                tile = b_idx[i][outer, inner, k].astype(F32)
                value = jnp.where(row + base < limits[k], tile, 0.0).astype(BF)
                kifin[k, l, i * HALF : (i + 1) * HALF, :] = value
            return carry

        lax.fori_loop(0, SIDE * SIDE, page, 0)

    def finalize(i):
        def tiles(n, carry):
            lane = lax.broadcasted_iota(jnp.int32, (DEPTH, 128), 1)
            logical = (2 * n + lane // PAGE) * (SIDE * SIDE * PAGE) + pos * PAGE + lane % PAGE
            for k in range(NEW):
                tile = zrecvs[i][sources[k], :, lane_tile(n)].astype(F32)
                value = jnp.where(logical < limits[k], tile, 0.0).astype(BF)
                kfin[k, depth(i), lane_tile(n)] = value
            return carry

        lax.fori_loop(0, CTX_DEV // 128, tiles, 0)

    spans = (pl.ds(0, BATCH // 2), pl.ds(BATCH // 2, BATCH // 2))

    def gather_views(phase, way):
        if phase == 0:
            return (qown.at[spans[way]], q_all.at[y, x, spans[way]])
        if way == 0:
            block = q_all.at[y, :, spans[way]]
        else:
            block = q_all.at[:, x, spans[way]]
        return (block, block)

    def gather_near(phase):
        copies = []
        for way in range(2):
            axis = way if phase == 0 else 1 - way
            src, dst = gather_views(phase, way)
            for n, delta in enumerate((1, SIDE - 1)):
                at = (phase, way, 0, n)
                copies.append(remote(src, dst, ag_s.at[at], ag_r.at[at], along(axis, delta)))
        return copies

    def gather_far(phase):
        copies = []
        for way in range(2):
            axis = way if phase == 0 else 1 - way
            for n, delta in enumerate((1, SIDE - 1)):
                rows = pl.ds(n * (QROWS // 2), QROWS // 2)
                fx = (x - delta) % SIDE if axis == 0 else x
                fy = (y - delta) % SIDE if axis == 1 else y
                if phase == 0:
                    block = q_all.at[fy, fx, spans[way], rows]
                elif way == 0:
                    block = q_all.at[fy, :, spans[way], rows]
                else:
                    block = q_all.at[:, fx, spans[way], rows]
                at = (phase, way, 1, n)
                copies.append(remote(block, block, ag_s.at[at], ag_r.at[at], along(axis, delta)))
        return copies

    def weight_copies(phase):
        axis = phase
        block = w_all.at[y, x] if phase == 0 else w_all.at[y]
        return [
            remote(
                wown if phase == 0 else block, block, aw_s.at[phase, delta - 1],
                aw_r.at[phase, delta - 1], along(axis, delta),
            )
            for delta in range(1, SIDE)
        ]

    own_q = pltpu.make_async_copy(qown, q_all.at[y, x], load_sem.at[0])
    own_w = pltpu.make_async_copy(wown, w_all.at[y, x], load_sem.at[1])
    load_w = pltpu.make_async_copy(w_uk, w_buf, load_sem.at[4])
    load_ki = pltpu.make_async_copy(residx, ki_res, load_sem.at[2])

    def load_k(b):
        return pltpu.make_async_copy(reslat.at[b], kbuf.at[b % 2], kb_sem.at[b])

    def absorb():
        rows = BATCH * HEADS_DEV
        head = lax.broadcasted_iota(jnp.int32, (rows, KV), 0) % HEADS_DEV
        for pair in range(STEPS // 2):
            blocks = []
            for t in (2 * pair, 2 * pair + 1):
                q = q_nope[t].reshape(rows, NOPE)
                total = jnp.zeros((rows, KV), F32)
                for h in range(HEADS_DEV):
                    part = jnp.dot(q, w_buf[h], preferred_element_type=F32)
                    total = jnp.where(head == h, part, total)
                keys = idx_query[t].astype(F32)
                halves = jnp.concatenate([keys[..., :ROPE], keys[..., ROPE:]], axis=1)
                tail = jnp.concatenate([q_rope[t].astype(F32), halves], axis=2)
                blocks.append(
                    jnp.concatenate([total.reshape(BATCH, HEADS_DEV, KV), tail], axis=2)
                )
            block = jnp.concatenate(blocks, axis=1).astype(BF)
            qown[:, pair * 16 : (pair + 1) * 16, :] = block

    def find_live(b):
        page = lax.broadcasted_iota(jnp.int32, (STEPS, CTX_DEV), 1) // PAGE * (SIDE * SIDE) + pos
        wanted = selected[b]
        found = wanted[:, 0:1] == page
        for n in range(1, wanted.shape[1]):
            found = found | (wanted[:, n : n + 1] == page)
        bias = jnp.where(found, 0.0, -1e30)
        for t in range(STEPS):
            live[t * HEADS_DEV : (t + 1) * HEADS_DEV, :] = jnp.broadcast_to(
                bias[t : t + 1], (HEADS_DEV, CTX_DEV)
            )

    def as_row(column):
        size = column.shape[0]
        row = lax.broadcasted_iota(jnp.int32, (size, size), 0)
        lane = lax.broadcasted_iota(jnp.int32, (size, size), 1)
        return jnp.sum(jnp.where(row == lane, column, 0.0), axis=0, keepdims=True)

    def as_column(values, first):
        row = lax.broadcasted_iota(jnp.int32, (QROWS, 128), 0)
        lane = lax.broadcasted_iota(jnp.int32, (QROWS, 128), 1)
        return jnp.sum(jnp.where(lane == row + first, values, 0.0), axis=1, keepdims=True)

    def attend(b, g, keys):
        b0, half = GROUPS[g][0], STAT_ROWS[g] // 2
        find_live(b)

        def part(n, carry):
            q = q_all[pl.ds(2 * n, 2), :, b, :, 0:LAT].reshape(2 * SIDE * QROWS, LAT)
            k = keys()
            s = jnp.dot(q, k, preferred_element_type=F32)
            s = (s * SCALE).reshape(2 * SIDE, QROWS, CTX_DEV) + live[...][None]
            s = s.reshape(2 * SIDE * QROWS, CTX_DEV)
            top = jnp.maximum(jnp.max(s, axis=1, keepdims=True), -1e29)
            e = jnp.exp(s - top)
            total = jnp.sum(e, axis=1, keepdims=True)
            o = lax.dot_general(
                e.astype(BF), k[:KV], (((1,), (1,)), ((), ())), preferred_element_type=F32
            )
            numer[pl.ds(2 * n, 2), :, b] = o.astype(BF).reshape(2, SIDE, QROWS, KV)
            cols = pl.ds(pl.multiple_of(n * 256, 256), 256)
            stats[g, b - b0 : b - b0 + 1, cols] = as_row(top)
            stats[g, b - b0 + half : b - b0 + half + 1, cols] = as_row(total)
            return carry

        lax.fori_loop(0, 2, part, 0)

    def index_scores(b, length, keys):
        shape = (SIDE * SIDE // 2, STEPS, HEADS_DEV, 128)
        both = q_all[:, :, b, :, KV:QW].astype(F32).reshape((SIDE * SIDE // 2, 2) + shape[1:])
        even, odd = both[:, 0].reshape(-1, 8, 128), both[:, 1].reshape(-1, 8, 128)
        row = lax.broadcasted_iota(jnp.int32, even.shape, 1)
        lane = lax.broadcasted_iota(jnp.int32, even.shape, 2)
        upper = jnp.where(lane < ROPE, pltpu.roll(even, ROPE, 2), pltpu.roll(even, 4, 1))
        lower = jnp.where(lane < ROPE, pltpu.roll(pltpu.roll(odd, ROPE, 2), 4, 1), odd)
        iq_buf[...] = jnp.where(row < 4, upper, lower).reshape(-1, 128).astype(BF)
        high = lax.broadcasted_iota(jnp.int32, (QROWS, 128), 0) % 8 < 4
        weights = []
        for pair in range(SIDE * SIDE // 2):
            w_even = w_all[pair // 2, 2 * (pair % 2), b : b + 1]
            w_odd = w_all[pair // 2, 2 * (pair % 2) + 1, b : b + 1]
            weights.append(as_column(jnp.where(high, w_even, w_odd), 0))
        weight = jnp.concatenate(weights, axis=0)

        def part(n, carry):
            k = keys(n)
            logits = lax.dot_general(
                iq_buf[...], k, (((1,), (1,)), ((), ())), preferred_element_type=F32
            )
            value = jnp.maximum(logits, 0.0) * weight
            cols = pl.ds(pl.multiple_of(n * 256, 256), 256)
            value = jnp.sum(value.reshape(SIDE * SIDE // 2, QROWS, 256), axis=0)
            value = jnp.sum(value.reshape(STEPS, HEADS_DEV, 256), axis=1) * IDIM ** (-0.5)
            lane = lax.broadcasted_iota(jnp.int32, (STEPS, 256), 1) + n * 256
            logical = lane // PAGE * (SIDE * SIDE * PAGE) + pos * PAGE + lane % PAGE
            value = jnp.where(logical < length, value, 0.0)
            for t in range(STEPS):
                out_is[t, b, :, cols] = value[t : t + 1]
            return carry

        lax.fori_loop(0, CTX_DEV // 256, part, 0)

    def attend_res(b):
        load_k(b).wait()
        attend(b, 0 if b < 3 else 5, lambda: kbuf[b % 2])
        if b + 2 < RES:
            load_k(b + 2).start()

    def attend_new(k, g):
        attend(RES + k, g, lambda: kfin[k])

    def index_res(b):
        index_scores(b, res_len[b], lambda n: ki_res[b, pl.ds(pl.multiple_of(n * 256, 256), 256)])

    def index_new(k):
        index_scores(RES + k, limits[k], lambda n: kifin[k, pl.ds(n * 4, 4)].reshape(256, IDIM))

    def lanes(way):
        return pl.ds(way * 256, 256)

    def reduce_copies(g, phase, way):
        b0, count = GROUPS[g]
        span, stat = pl.ds(b0, count), pl.ds(0, STAT_ROWS[g])
        axis = way if phase == 0 else 1 - way
        copies = []
        for delta in range(1, SIDE):
            other = (mine(axis) + delta) % SIDE
            to_y = other if axis == 1 else y
            tile = pl.ds(pl.multiple_of(to_y * 128, 128), 128)
            if phase == 0:
                src = numer.at[:, other, span, :, lanes(way)]
                src_st, dst_st = stats.at[g, stat], rsa.at[g, way, delta - 1, stat]
                if way == 1:
                    src = numer.at[other, :, span, :, lanes(way)]
                    src_st = stats.at[g, stat, tile]
                    dst_st = rsa.at[g, way, delta - 1, stat, pl.ds(0, 128)]
                dst = ra.at[way, delta - 1, :, span]
            else:
                src, src_st = nb_buf.at[way, other, span], stb.at[g, way, stat, tile]
                dst, dst_st = rb.at[way, delta - 1, span], rsb.at[g, way, delta - 1, stat]
            target = along(axis, delta)
            for which, (s, d) in enumerate(((src, dst), (src_st, dst_st))):
                at = (g, phase, way, which, delta - 1)
                copies.append(remote(s, d, rs_s.at[at], rs_r.at[at], target))
        return copies

    def start_reduce(g, phase, way):
        for copy in reduce_copies(g, phase, way):
            copy.start()

    def merged(g, blocks):
        half = STAT_ROWS[g] // 2
        tops = [block[:half] for block in blocks]
        top = tops[0]
        for value in tops[1:]:
            top = jnp.maximum(top, value)
        factors = [jnp.exp(value - top) for value in tops]
        total = factors[0] * blocks[0][half:]
        for factor, block in zip(factors[1:], blocks[1:]):
            total = total + factor * block[half:]
        return top, factors, total

    def combine_a(g, way):
        b0, count = GROUPS[g]
        half = STAT_ROWS[g] // 2
        stat = slice(0, STAT_ROWS[g])
        for copy in reduce_copies(g, 0, way):
            copy.wait_recv()
        if way == 0:
            blocks = [stats[g, stat]] + [rsa[g, way, d, stat] for d in range(SIDE - 1)]
            cols = slice(0, SIDE * 128)
        else:
            blocks = [stats[g, stat, pl.ds(pl.multiple_of(y * 128, 128), 128)]]
            blocks += [rsa[g, way, d, stat, 0:128] for d in range(SIDE - 1)]
            cols = pl.ds(pl.multiple_of(y * 128, 128), 128)
        top, factors, total = merged(g, blocks)
        stb[g, way, 0:half, cols] = top
        stb[g, way, half : 2 * half, cols] = total
        for d in range(SIDE):
            fbuf[d, 0:half, cols] = factors[d]

        def block(j, carry):
            tile = pl.ds(pl.multiple_of((j if way == 0 else y) * 128, 128), 128)
            first = (x if way == 0 else j) * QROWS
            for n in range(count):
                if way == 0:
                    own = numer[j, x, b0 + n, :, 0:256]
                else:
                    own = numer[y, j, b0 + n, :, 256:512]
                acc = own.astype(F32) * as_column(fbuf[0, n : n + 1, tile], first)
                for d in range(SIDE - 1):
                    factor = as_column(fbuf[d + 1, n : n + 1, tile], first)
                    acc = acc + ra[way, d, j, b0 + n].astype(F32) * factor
                nb_buf[way, j, b0 + n] = acc.astype(BF)
            return carry

        lax.fori_loop(0, SIDE, block, 0)
        start_reduce(g, 1, way)

    def combine_b(g, way):
        b0, count = GROUPS[g]
        stat = slice(0, STAT_ROWS[g])
        for copy in reduce_copies(g, 1, way):
            copy.wait_recv()
        here = mine(1 - way)
        blocks = [stb[g, way, stat, pl.ds(pl.multiple_of(y * 128, 128), 128)]]
        blocks += [rsb[g, way, d, stat] for d in range(SIDE - 1)]
        _, factors, total = merged(g, blocks)
        factors = [factor / total for factor in factors]
        for n in range(count):
            acc = nb_buf[way, here, b0 + n].astype(F32) * as_column(factors[0][n : n + 1], x * QROWS)
            for d in range(SIDE - 1):
                factor = as_column(factors[d + 1][n : n + 1], x * QROWS)
                acc = acc + rb[way, d, b0 + n].astype(F32) * factor
            out_latent[b0 + n, :, way * 256 : (way + 1) * 256] = acc.astype(BF)

    def start(copies):
        for copy in copies:
            copy.start()

    def arrived(copies):
        for copy in copies:
            copy.wait_recv()

    load_lat(N_IDX).start()
    load_lat(N_IDX + 2).start()
    load_w.start()
    own_w.start()
    load_idx.wait()
    index_to_z(0)
    index_to_z(1)
    start_a(2)
    start_a(3)
    load_ki.start()
    load_k(0).start()
    load_k(1).start()
    stats[...] = jnp.zeros_like(stats)
    start_a(4)
    a_to_b(2)
    a_to_b(3)
    load_w.wait()
    absorb()
    own_q.start()
    start(gather_near(0) + weight_copies(0))
    start_a(5)
    b_to_z(2)
    a_to_b(4)
    own_q.wait()
    own_w.wait()
    arrived(gather_near(0) + weight_copies(0))
    start(gather_far(0) + weight_copies(1))
    start_a(6)
    a_to_b(5)
    start_a(7)
    b_to_z(3)
    b_to_z(4)

    for i in range(N_CH):
        wait_z(i)
        if i + 6 < N_CH:
            a_to_b(i + 6)
        if i + 8 < N_CH:
            start_a(i + 8)
        if 0 < i < N_CH - 4:
            b_to_z(i + 4)
        if i < N_IDX:
            index_to_a(i)
        else:
            finalize(i)
        if i == 0:
            arrived(gather_far(0))
            start(gather_near(1))
        elif i == 2:
            arrived(gather_near(1))
            start(gather_far(1))
            a_to_b(0)
        elif i == 3:
            a_to_b(1)
        elif i == 4:
            arrived(gather_far(1) + weight_copies(1))
            attend_res(0)
            attend_res(1)
        elif i == 5:
            attend_res(2)
            for way in range(2):
                start_reduce(0, 0, way)
            attend_res(3)
        elif i == 6:
            attend_res(4)
            attend_res(5)
            for way in range(2):
                start_reduce(5, 0, way)
            load_ki.wait()
            index_res(0)
        elif i == 7:
            for way in range(2):
                combine_a(0, way)
            index_res(1)
            index_res(2)
            finalize_idx(0)
            finalize_idx(1)
            out_copies("idx").start()
        elif i == 8:
            for way in range(2):
                combine_a(5, way)
            index_res(3)
            index_res(4)
        elif i == 9:
            index_res(5)
            index_new(0)
            for way in range(2):
                combine_b(0, way)
            index_new(1)
            for way in range(2):
                combine_b(5, way)
    out_copies("lat").start()
    for k in range(NEW):
        attend_new(k, k + 1)
        for way in range(2):
            start_reduce(k + 1, 0, way)
    index_new(2)
    for way in range(2):
        combine_a(1, way)
    index_new(3)
    for g in (2, 3, 4):
        for way in range(2):
            combine_a(g, way)
    for g in (1, 2, 3, 4):
        for way in range(2):
            combine_b(g, way)

    for i in range(N_CH):
        for kind in ("a", "b", "z"):
            drain(kind, i)
    for phase in range(2):
        for copy in gather_near(phase) + gather_far(phase) + weight_copies(phase):
            copy.wait_send()
        for g in range(len(GROUPS)):
            for way in range(2):
                for copy in reduce_copies(g, phase, way):
                    copy.wait_send()
    out_copies("idx").wait()
    out_copies("lat").wait()


def run_kernel(*operands):
    smem = pl.BlockSpec(memory_space=pltpu.SMEM)
    vmem = pl.BlockSpec(memory_space=pltpu.VMEM)
    hbm = pl.BlockSpec(memory_space=pl.ANY)
    dma = pltpu.SemaphoreType.DMA
    n_groups = len(GROUPS)
    tile = (SIDE, SIDE, HALF, 128)
    return pl.pallas_call(
        kernel,
        out_shape=(
            jax.ShapeDtypeStruct((NEW, LAT, CTX_DEV), BF),
            jax.ShapeDtypeStruct((NEW, PG_LOC, PAGE, IDIM), BF),
            jax.ShapeDtypeStruct((STEPS, BATCH, 1, CTX_DEV), F32),
            jax.ShapeDtypeStruct((BATCH, QROWS, KV), BF),
            jax.ShapeDtypeStruct((N_IDX, SIDE, NEW, SIDE, HALF, 128), BF),
            jax.ShapeDtypeStruct((N_XF, SIDE, 2, SIDE, DEPTH, 128), BF),
        ),
        in_specs=[smem] * 3 + [hbm] * 6 + [vmem] * 4,
        out_specs=(hbm, hbm, vmem, vmem, hbm, hbm),
        scratch_shapes=[
            pltpu.VMEM((BATCH, QROWS, QW), BF),
            pltpu.VMEM((HEADS_DEV, NOPE, KV), BF),
            pltpu.VMEM((QROWS, CTX_DEV), F32),
            pltpu.VMEM((NEW, SIDE, SIDE, PAGE, IDIM), BF),
            pltpu.VMEM((N_IDX, NEW) + tile, BF),
            (pltpu.VMEM((SIDE, NEW, DEPTH, 256), BF),) * (N_LAT - N_XF),
            (pltpu.VMEM((SIDE, SIDE, NEW, HALF, 128), BF),) * N_IDX,
            (pltpu.VMEM((SIDE, SIDE, 2, DEPTH, 128), BF),) * N_LAT,
            pltpu.VMEM((2, NEW, DEPTH, CTX_DEV), BF),
            pltpu.VMEM((2, SIDE, 2, SIDE, DEPTH, 128), BF),
            pltpu.VMEM((2, SIDE, SIDE, 2, DEPTH, 128), BF),
            pltpu.VMEM((NEW, DEPTH, CTX_DEV), BF),
            pltpu.VMEM((N_IDX, N_REQ - 1) + tile, BF),
            pltpu.VMEM((RING, N_REQ - 1, DEPTH, CTX_DEV), BF),
            (pltpu.VMEM((N_REQ,) + tile, BF),) * N_IDX
            + (pltpu.VMEM((N_REQ, DEPTH, CTX_DEV), BF),) * N_LAT,
            pltpu.VMEM((SIDE, SIDE, BATCH, QROWS, QW), BF),
            pltpu.VMEM((SIDE, SIDE, 16, 128), F32),
            pltpu.VMEM((SIDE * SIDE // 2 * QROWS, IDIM), BF),
            pltpu.VMEM((2, LAT, CTX_DEV), BF),
            pltpu.VMEM((RES, CTX_DEV, IDIM), BF),
            pltpu.VMEM((NEW, LAT, CTX_DEV), BF),
            pltpu.VMEM((NEW, PG_LOC, PAGE, IDIM), BF),
            pltpu.VMEM((SIDE, SIDE, BATCH, QROWS, KV), BF),
            pltpu.VMEM((n_groups, 16, SIDE * 128), F32),
            pltpu.VMEM((2, SIDE - 1, SIDE, BATCH, QROWS, 256), BF),
            pltpu.VMEM((n_groups, 2, SIDE - 1, 16, SIDE * 128), F32),
            pltpu.VMEM((2, SIDE, BATCH, QROWS, 256), BF),
            pltpu.VMEM((n_groups, 2, 16, SIDE * 128), F32),
            pltpu.VMEM((2, SIDE - 1, BATCH, QROWS, 256), BF),
            pltpu.VMEM((n_groups, 2, SIDE - 1, 16, 128), F32),
            pltpu.VMEM((SIDE, 8, SIDE * 128), F32),
            dma((N_CH, 3)), dma((N_CH, 3)), dma((N_CH, 3)), dma((N_CH, 3)),
            dma((N_CH, N_REQ - 1)), dma((N_CH, N_REQ - 1)),
            dma((N_CH,)), dma((N_CH,)), dma((N_XF,)), dma((5,)), dma((2,)), dma((RES,)),
            dma((2, 2, 2, 2)), dma((2, 2, 2, 2)), dma((2, 3)), dma((2, 3)),
            dma((n_groups, 2, 2, 2, 3)), dma((n_groups, 2, 2, 2, 3)),
        ],
        compiler_params=pltpu.CompilerParams(
            collective_id=0, has_side_effects=True, vmem_limit_bytes=63 * 2**20
        ),
        name="decode_step",
    )(*operands)


def body(
    res_latent, res_index, res_len, arrive_latent, arrive_index, arrive_len, destination,
    q_nope, q_rope, w_uk, w_uv, idx_query, idx_weight, selected,
):
    weights = jnp.concatenate([idx_weight, idx_weight], axis=2).astype(F32)
    weights = weights.transpose(1, 0, 2).reshape(BATCH, QROWS)
    weights = jnp.pad(weights, ((0, 16 - BATCH), (0, 128 - QROWS)))

    new_latent, new_index, index_scores, latent, _, _ = run_kernel(
        destination, arrive_len, res_len,
        arrive_latent.transpose(0, 2, 1), arrive_index.reshape(NEW, SIDE, SIDE, PAGE, IDIM),
        weights, res_latent[:, 0].transpose(0, 2, 1), res_index[:, 0], w_uk,
        q_nope, q_rope, idx_query, selected.transpose(1, 0, 2),
    )

    latent = latent.reshape(BATCH, STEPS, HEADS_DEV, KV)
    head_out = jnp.einsum("bshc,hcd->sbhd", latent, w_uv, preferred_element_type=F32).astype(BF)
    return (
        new_latent.transpose(0, 2, 1).reshape(NEW, 1, CTX_DEV, LAT),
        new_index.reshape(NEW, 1, CTX_DEV, IDIM),
        index_scores,
        head_out,
    )


def solution(mesh):
    placed = (
        P("req", "pos", None, None),
        P("req", "pos", None, None),
        P("req"),
        P("req", "pos", None),
        P("req", "pos", None),
        P(),
        P(),
        P(None, "req", "pos", None),
        P(None, "req", "pos", None),
        P("pos", None, None),
        P("pos", None, None),
        P(None, "req", "pos", None),
        P(None, "req", "pos"),
        P(None, "req", None),
    )
    return jax.shard_map(
        body,
        mesh=mesh,
        in_specs=placed,
        out_specs=(
            P("req", "pos", None, None),
            P("req", "pos", None, None),
            P(None, "req", "pos", None),
            P(None, "req", "pos", None),
        ),
        check_vma=False,
    )
```
